32 devices in a mesh: dp: 4 (over y, x), seq: 4 (over z), mp: 2 (over core).
Axes of the slice: x: 2, y: 2, z: 4, core: 2. Of those that a mesh axis runs over, the one named last changes fastest.
Arguments:
- src: bfloat16 [8, 1024, 1024], P('dp', 'seq'), may hold values from -6 to 6
- tgt: bfloat16 [8, 1024, 1024], P('dp', 'seq'), may hold values from -6 to 6
- cotangent: bfloat16 [8, 1024, 1024], P('dp', 'seq'), may hold values from -6 to 6
- lengths: int32 [8, 8], P('dp'), may hold values from 1 to 800, as said below
- groups: int32 [8, 8], P('dp'), may hold values from 0 to 3, as said below
- enc_gains: bfloat16 [2, 1024], P(None, ('dp', 'seq')), may hold values from 0.5 to 1.5
- enc_biases: bfloat16 [2, 1024], P(None, ('dp', 'seq')), may hold values from -3 to 3
- enc_qkv: bfloat16 [3, 1024, 1024], P(None, ('dp', 'seq'), 'mp'), may hold values from -0.1875 to 0.1875
- enc_out: bfloat16 [1024, 1024], P('mp', ('dp', 'seq')), may hold values from -0.75 to 0.75
- enc_up: bfloat16 [1024, 4096], P(('dp', 'seq'), 'mp'), may hold values from -0.1875 to 0.1875
- enc_down: bfloat16 [4096, 1024], P('mp', ('dp', 'seq')), may hold values from -0.09375 to 0.09375
- dec_gains: bfloat16 [3, 1024], P(None, ('dp', 'seq')), may hold values from 0.5 to 1.5
- dec_biases: bfloat16 [3, 1024], P(None, ('dp', 'seq')), may hold values from -3 to 3
- dec_self_qkv: bfloat16 [3, 1024, 1024], P(None, ('dp', 'seq'), 'mp'), may hold values from -0.1875 to 0.1875
- dec_cross_qkv: bfloat16 [3, 1024, 1024], P(None, ('dp', 'seq'), 'mp'), may hold values from -0.1875 to 0.1875
- dec_outs: bfloat16 [2, 1024, 1024], P(None, 'mp', ('dp', 'seq')), may hold values from -0.75 to 0.75
- dec_up: bfloat16 [1024, 4096], P(('dp', 'seq'), 'mp'), may hold values from -0.1875 to 0.1875
- dec_down: bfloat16 [4096, 1024], P('mp', ('dp', 'seq')), may hold values from -0.09375 to 0.09375
Outputs:
- decoded: bfloat16 [8, 1024, 1024], P('dp', 'seq')
- src_grad: float32 [8, 1024, 1024], P('dp', 'seq')
- tgt_grad: float32 [8, 1024, 1024], P('dp', 'seq')
- memory_grad: float32 [8, 1024, 1024], P('dp', 'seq')
- enc_gains_grad: float32 [2, 1024], P(None, ('dp', 'seq'))
- enc_biases_grad: float32 [2, 1024], P(None, ('dp', 'seq'))
- enc_qkv_grad: float32 [3, 1024, 1024], P(None, ('dp', 'seq'), 'mp')
- enc_out_grad: float32 [1024, 1024], P('mp', ('dp', 'seq'))
- enc_up_grad: float32 [1024, 4096], P(('dp', 'seq'), 'mp')
- enc_down_grad: float32 [4096, 1024], P('mp', ('dp', 'seq'))
- dec_gains_grad: float32 [3, 1024], P(None, ('dp', 'seq'))
- dec_biases_grad: float32 [3, 1024], P(None, ('dp', 'seq'))
- dec_self_qkv_grad: float32 [3, 1024, 1024], P(None, ('dp', 'seq'), 'mp')
- dec_cross_qkv_grad: float32 [3, 1024, 1024], P(None, ('dp', 'seq'), 'mp')
- dec_outs_grad: float32 [2, 1024, 1024], P(None, 'mp', ('dp', 'seq'))
- dec_up_grad: float32 [1024, 4096], P(('dp', 'seq'), 'mp')
- dec_down_grad: float32 [4096, 1024], P('mp', ('dp', 'seq'))
The draws below stay inside these ranges and needn't reach their ends.
Inputs may be any that keep to these rules, and one draw needn't show every extreme that they name: `lengths`: each row has 8 segments; one of them, in a slot drawn per row, has more than 256 tokens, each other one at most 32; the segments never fill more than 1024 positions, the rest is padding. `groups`: every group is named by one segment or more.
All inputs are finite; a program needn't handle non-finite values.
Results may differ from the reference program's by a relative error of at most 0.022.
Values may be sent and summed in bfloat16 or wider, within the bound.
No kernel may reach another device: no remote copies, remote signals or barrier semaphores. Data moves between devices by JAX's collectives and lax.ppermute only.
A program may use at most 320 MiB of HBM per device.

```python
import jax
import jax.numpy as jnp
from jax import lax

D = 1024
FF = 4096
HEAD = 64
LEN = 1024
NSEG = 8
LANGS = 4
ROWS = 8
TOKENS = 8192


def draw_lengths(key, part):
    key = jax.random.fold_in(key, 11)
    short_key, slot_key, long_key, pick_key = jax.random.split(key, 4)
    short_most = LEN // (4 * NSEG)
    long_most = LEN - (NSEG - 1) * short_most
    shorts = jax.random.randint(short_key, (ROWS, NSEG), 1, short_most + 1)
    slots = jax.random.randint(slot_key, (ROWS, 1), 0, NSEG)
    longs = jax.random.randint(long_key, (ROWS, 1), LEN // 4 + 1, long_most + 1)
    picked = jax.random.randint(pick_key, (), 0, ROWS)
    row_ids = jnp.arange(ROWS, dtype=jnp.int32)[:, None]
    cols = jnp.arange(NSEG, dtype=jnp.int32)[None, :]
    longs = jnp.where(row_ids == picked, long_most, longs)
    shorts = jnp.where((row_ids == picked) & (cols == (slots + 1) % NSEG), 1, shorts)
    chosen = cols == slots
    return jnp.where(chosen, longs, shorts).astype(jnp.int32)


def draw_groups(key, part):
    key = jax.random.fold_in(key, 29)
    order_key, level_key, pick_key = jax.random.split(key, 3)
    order = jax.random.permutation(order_key, LANGS).astype(jnp.int32)
    draws = jax.random.randint(level_key, (ROWS, NSEG), 0, 15)
    level = (draws >= 1).astype(jnp.int32) + (draws >= 3).astype(jnp.int32) + (draws >= 7).astype(jnp.int32)
    level = jnp.minimum(level, LANGS - 1)
    named = order[level]
    picked = jax.random.randint(pick_key, (), 0, ROWS)
    row_ids = jnp.arange(ROWS, dtype=jnp.int32)[:, None]
    cols = jnp.arange(NSEG, dtype=jnp.int32)[None, :]
    forced = (row_ids == picked) & (cols < LANGS)
    return jnp.where(forced, jnp.minimum(cols, LANGS - 1), named).astype(jnp.int32)


def block_levels(rng, shape, cuts, smallest, high):
    level, own = 1.0, jax.random.fold_in(rng, 6)
    for position, shards_of in cuts:
        steps = jnp.exp(jax.random.uniform(jax.random.fold_in(own, position), (shards_of,), jnp.float32, smallest / len(cuts), high / len(cuts)))
        level = level * jnp.repeat(steps, shape[position] // shards_of).reshape([-1 if axis == position else 1 for axis in range(len(shape))])
    return level


def bell_draw(rng, extent, width, bound, cuts=(), kind=jnp.bfloat16):
    array = jax.random.normal(rng, extent, jnp.float32) * width
    if len(cuts) > 0:
        array = block_levels(rng, extent, cuts, -0.22, 0.18) * array
    return jnp.clip(array, min=-bound, max=bound).astype(kind)


def setup_inputs(seed: int = 0) -> dict:
    splits = jax.random.split(jax.random.key(seed), 19)
    return {
        "src": bell_draw(splits[0], (ROWS, LEN, D), 1.0, 6.0, ((0, 4), (1, 4))),
        "tgt": bell_draw(splits[1], (ROWS, LEN, D), 1.0, 6.0, ((0, 4), (1, 4))),
        "cotangent": bell_draw(splits[2], (ROWS, LEN, D), 1.0, 6.0, ((0, 4), (1, 4))),
        "lengths": draw_lengths(jax.random.fold_in(splits[18], 71), 0),
        "groups": draw_groups(jax.random.fold_in(splits[18], 71), 0),
        "enc_gains": jnp.clip(1.0 + 0.1 * jax.random.normal(splits[5], (2, D), jnp.float32), 0.5, 1.5).astype(jnp.bfloat16),
        "enc_biases": bell_draw(splits[6], (2, D), 0.5, 3.0, ((1, 16),)),
        "enc_qkv": bell_draw(splits[7], (3, D, D), D ** -0.5, 0.1875, ((1, 16), (2, 2))),
        "enc_out": bell_draw(splits[8], (D, D), (D // 16) ** -0.5, 0.75, ((0, 2), (1, 16))),
        "enc_up": bell_draw(splits[9], (D, FF), D ** -0.5, 0.1875, ((0, 16), (1, 2))),
        "enc_down": bell_draw(splits[10], (FF, D), FF ** -0.5, 0.09375, ((0, 2), (1, 16))),
        "dec_gains": jnp.clip(1.0 + 0.1 * jax.random.normal(splits[11], (3, D), jnp.float32), 0.5, 1.5).astype(jnp.bfloat16),
        "dec_biases": bell_draw(splits[12], (3, D), 0.5, 3.0, ((1, 16),)),
        "dec_self_qkv": bell_draw(splits[13], (3, D, D), D ** -0.5, 0.1875, ((1, 16), (2, 2))),
        "dec_cross_qkv": bell_draw(splits[14], (3, D, D), D ** -0.5, 0.1875, ((1, 16), (2, 2))),
        "dec_outs": bell_draw(splits[15], (2, D, D), (D // 16) ** -0.5, 0.75, ((1, 2), (2, 16))),
        "dec_up": bell_draw(splits[16], (D, FF), D ** -0.5, 0.1875, ((0, 16), (1, 2))),
        "dec_down": bell_draw(splits[17], (FF, D), FF ** -0.5, 0.09375, ((0, 2), (1, 16))),
    }


@jax.custom_vjp
def low(v):
    return lax.optimization_barrier(v.astype(jnp.bfloat16)).astype(jnp.float32)

@jax.custom_vjp
def low_back(v):
    return v

def low_keep(v):
    return (low(v), None)

def low_pass(kept, grad):
    return (grad,)

def back_keep(v):
    return (v, None)

def back_low(kept, grad):
    return (low(grad),)
low.defvjp(low_keep, low_pass)
low_back.defvjp(back_keep, back_low)

def layer_norm(values, gain, bias):
    center = values - lax.optimization_barrier(jnp.mean(values, axis=-1, keepdims=True))
    spread = lax.optimization_barrier(jnp.mean(center * center, axis=-1, keepdims=True))
    return center * lax.rsqrt(spread + 1e-05) * gain + bias

def product(left, right):
    return jnp.dot(left, right, precision=lax.Precision.HIGHEST)

def projected(normed, weight):
    return low_back(low(product(normed, weight)))

def attention(query, keys, values, mask):
    length = query.shape[0]
    q_heads = query.reshape(length, -1, HEAD)
    k_heads = keys.reshape(length, -1, HEAD)
    v_heads = values.reshape(length, -1, HEAD)
    scores = jnp.einsum('qhe,khe->hqk', q_heads, k_heads, precision=lax.Precision.HIGHEST) * HEAD ** (-0.5)
    scores = jnp.where(mask[None], low_back(scores), -1e+30)
    probs = low(jax.nn.softmax(scores, axis=-1))
    mixed = jnp.einsum('hqk,khe->qhe', probs, v_heads, precision=lax.Precision.HIGHEST)
    return mixed.reshape(length, -1)

def attn_block(inputs, source, gain, bias, qkv, out_weight, mask):
    normed = low(layer_norm(inputs, gain, bias))
    keyed = normed if source is None else low(source)
    query = projected(normed, qkv[0])
    keys = projected(keyed, qkv[1])
    values = projected(keyed, qkv[2])
    context = low_back(low(attention(query, keys, values, mask)))
    return inputs + low_back(product(context, out_weight))

def ffn_block(inputs, gain, bias, up, down):
    normed = low(layer_norm(inputs, gain, bias))
    pre = low_back(product(normed, up))
    act = low(jax.nn.gelu(pre, approximate=False))
    return inputs + low_back(product(act, down))

def row_forward(params, src_row, tgt_row, seg_row, probe_row):
    e_gain, e_bias, e_qkv, e_out, e_up, e_down, d_gain, d_bias, d_self, d_cross, d_outs, d_up, d_down = params
    places = jnp.arange(LEN, dtype=jnp.int32)
    same = seg_row[:, None] == seg_row[None, :]
    causal = same & (places[None, :] <= places[:, None])
    enc_mid = attn_block(src_row, None, e_gain[0], e_bias[0], e_qkv, e_out, same)
    memory = ffn_block(enc_mid, e_gain[1], e_bias[1], e_up, e_down) + probe_row
    dec_mid = attn_block(tgt_row, None, d_gain[0], d_bias[0], d_self, d_outs[0], causal)
    dec_cross = attn_block(dec_mid, memory, d_gain[1], d_bias[1], d_cross, d_outs[1], same)
    return ffn_block(dec_cross, d_gain[2], d_bias[2], d_up, d_down)

def reference(src, tgt, cotangent, lengths, groups, enc_gains, enc_biases, enc_qkv, enc_out, enc_up, enc_down, dec_gains, dec_biases, dec_self_qkv, dec_cross_qkv, dec_outs, dec_up, dec_down):
    params = tuple((weight.astype(jnp.float32) for weight in (enc_gains, enc_biases, enc_qkv, enc_out, enc_up, enc_down, dec_gains, dec_biases, dec_self_qkv, dec_cross_qkv, dec_outs, dec_up, dec_down)))
    ends = jnp.cumsum(lengths, axis=1)
    places = jnp.arange(LEN, dtype=jnp.int32)
    segs = lax.optimization_barrier(jnp.sum((ends[:, None, :] <= places[None, :, None]).astype(jnp.int32), axis=2))
    onehot = (groups[:, :, None] == jnp.arange(LANGS, dtype=jnp.int32)[None, None, :]).astype(jnp.float32)
    counts = lax.optimization_barrier(jnp.sum(onehot * lengths[:, :, None].astype(jnp.float32), axis=(0, 1)))
    seg_weight = TOKENS / (LANGS * lax.optimization_barrier(jnp.sum(onehot * counts[None, None, :], axis=2)))
    seg_match = (segs[:, :, None] == jnp.arange(NSEG, dtype=jnp.int32)[None, None, :]).astype(jnp.float32)
    tok_weight = lax.optimization_barrier(jnp.sum(seg_match * seg_weight[:, None, :], axis=2))

    def whole(weights, src_all, tgt_all, probes):
        step = jax.checkpoint(lambda item: row_forward(weights, item[0], item[1], item[2], item[3]))
        return lax.map(step, (src_all, tgt_all, segs, probes))
    probes = jnp.zeros(src.shape, jnp.float32)
    decoded, pull = jax.vjp(whole, params, src.astype(jnp.float32), tgt.astype(jnp.float32), probes)
    out_grad = cotangent.astype(jnp.float32) * tok_weight[:, :, None]
    param_grads, src_grad, tgt_grad, memory_grad = pull(out_grad)
    scaled = tuple((grad / TOKENS for grad in param_grads))
    return (decoded.astype(jnp.bfloat16), src_grad, tgt_grad, memory_grad, scaled[0], scaled[1], scaled[2], scaled[3], scaled[4], scaled[5], scaled[6], scaled[7], scaled[8], scaled[9], scaled[10], scaled[11], scaled[12])
```

```python
import jax
import jax.numpy as jnp
from jax import lax
from jax.experimental import pallas as pl
from jax.experimental.pallas import tpu as pltpu
from jax.sharding import PartitionSpec as P

HEAD = 64
NSEG = 8
LANGS = 4
LANES = 128
F32 = jnp.float32
LOW = jnp.bfloat16


def matmul(left, right):
    return jnp.dot(left, right, preferred_element_type=F32)


def inner_rows(left, right):
    return lax.dot_general(left, right, (((0,), (0,)), ((), ())), preferred_element_type=F32)


def outer_cols(left, right):
    return lax.dot_general(left, right, (((1,), (1,)), ((), ())), preferred_element_type=F32)


def xor_perm(size, bits):
    return [(i, i ^ bits) for i in range(size)]


def swap(value, axis, bits):
    return lax.ppermute(value, axis, xor_perm(lax.axis_size(axis), bits))


def pick(value, index, axis=0):
    return lax.dynamic_index_in_dim(value, index, axis, keepdims=False)


def place(blocks, order):
    count, (rows, cols) = len(blocks), blocks[0].shape
    each = len(order) // count
    size = rows // each

    def body(order_ref, *refs):
        sources, out = refs[:count], refs[count]
        held, in_sems, out_sems = refs[count + 1 :]
        loads = [pltpu.make_async_copy(sources[j], held.at[j], in_sems.at[j]) for j in range(count)]
        stores = []
        for load in loads:
            load.start()
        for j in range(count):
            loads[j].wait()
            for i in range(each):
                spot = order_ref[j * each + i]
                start = pl.multiple_of(spot * size, size)
                stores.append(
                    pltpu.make_async_copy(
                        held.at[j, pl.ds(i * size, size)],
                        out.at[pl.ds(start, size)],
                        out_sems.at[j * each + i],
                    )
                )
                stores[-1].start()
        for store in stores:
            store.wait()

    return pl.pallas_call(
        body,
        out_shape=jax.ShapeDtypeStruct((count * rows, cols), blocks[0].dtype),
        in_specs=[pl.BlockSpec(memory_space=pltpu.SMEM)]
        + [pl.BlockSpec(memory_space=pl.ANY)] * count,
        out_specs=pl.BlockSpec(memory_space=pl.ANY),
        scratch_shapes=[
            pltpu.VMEM((count, rows, cols), blocks[0].dtype),
            pltpu.SemaphoreType.DMA((count,)),
            pltpu.SemaphoreType.DMA((len(order),)),
        ],
        compiler_params=pltpu.CompilerParams(vmem_limit_bytes=16 << 20),
        cost_estimate=pl.CostEstimate(
            flops=0, bytes_accessed=4 * count * rows * cols, transcendentals=0
        ),
    )(jnp.stack(order).astype(jnp.int32), *blocks)


def gather_weight(shard, first):
    here, spot = lax.axis_index("seq"), lax.axis_index("dp")
    n_dp, n_seq = lax.axis_size("dp"), lax.axis_size("seq")
    column = jnp.concatenate([shard] + [swap(shard, "seq", k) for k in range(1, n_seq)], axis=0)
    order = [here ^ k for k in range(n_seq)]
    if n_dp != 4:
        column = place([column], order)
        return lax.all_gather(column, "dp", axis=0, tiled=True)
    second = 3 - first
    near = swap(column, "dp", first)
    side = swap(column, "dp", second)
    far = swap(near, "dp", second)
    order = [(spot ^ j) * n_seq + i for j in (0, first, second, 3) for i in order]
    return place([column, near, side, far], order)


def scatter_grad(grad, first):
    here, spot = lax.axis_index("seq"), lax.axis_index("dp")
    n_dp, n_seq = lax.axis_size("dp"), lax.axis_size("seq")
    total, cols = grad.shape
    if n_dp != 4:
        column = lax.psum_scatter(grad, "dp", scatter_dimension=0, tiled=True).astype(F32)
        column = column.reshape(n_seq, -1, cols)
    else:
        axis = 0 if first == 2 else 1
        mine, other = (spot // 2, spot % 2) if first == 2 else (spot % 2, spot // 2)
        four = grad.reshape(2, 2, total // 4, cols)
        came = swap(pick(four, 1 - mine, axis), "dp", first)
        half = pick(four, mine, axis).astype(F32) + came.astype(F32)
        came = swap(pick(half, 1 - other).astype(LOW), "dp", 3 - first)
        column = pick(half, other) + came.astype(F32)
        column = column.reshape(n_seq, -1, cols)
    result = pick(column, here)
    for k in range(1, n_seq):
        result = result + swap(pick(column, here ^ k).astype(LOW), "seq", k).astype(F32)
    return result


def trade_half(value):
    core = lax.axis_index("mp")
    size = value.shape[0] // 2
    part = lax.dynamic_slice_in_dim(value, core * size, size, 0)
    part = swap(part, "seq", 2)
    rest = swap(part, "mp", 1)
    return jnp.where(
        core == 0, jnp.concatenate([part, rest], axis=0), jnp.concatenate([rest, part], axis=0)
    )


def to_pair(value):
    row = lax.axis_index("seq") // 2
    return jnp.concatenate([pick(value, row), trade_half(pick(value, 1 - row))], axis=0)


def from_pair(value):
    size = value.shape[0] // 2
    kept = value[:size]
    came = trade_half(value[size:].astype(LOW)).astype(value.dtype)
    row = lax.axis_index("seq") // 2
    return jnp.where(row == 0, jnp.stack([kept, came]), jnp.stack([came, kept]))


def core_total(part):
    low = lax.optimization_barrier(part.astype(LOW))
    return low.astype(F32) + swap(low, "mp", 1).astype(F32)


def norm_parts(values):
    center = values - jnp.mean(values, axis=-1, keepdims=True)
    scale = lax.rsqrt(jnp.mean(center * center, axis=-1, keepdims=True) + 1e-05)
    return center * scale, scale


def layer_norm(values, gain, bias):
    return (norm_parts(values)[0] * gain + bias).astype(LOW)


def norm_backward(values, gain, grad):
    unit, scale = norm_parts(values)
    gain_grad = jnp.sum(grad * unit, axis=0)
    bias_grad = jnp.sum(grad, axis=0)
    inner = grad * gain
    inner = inner - jnp.mean(inner, axis=-1, keepdims=True) - unit * jnp.mean(
        inner * unit, axis=-1, keepdims=True
    )
    return inner * scale, gain_grad, bias_grad


def heads(value):
    return value.reshape(value.shape[0], -1, HEAD)


def score_table(query, keys, mask):
    scores = jnp.einsum("qhe,khe->hqk", heads(query), heads(keys), preferred_element_type=F32)
    return jnp.where(mask[None], scores * HEAD ** (-0.5), -1e30)


def attn_forward(inputs, gain, bias, weights, mask, source):
    wkv, wq, wo = weights
    normed = layer_norm(inputs, gain, bias)
    if source is None:
        source = normed
    pair = matmul(source, wkv).astype(LOW)
    peer = swap(pair, "seq", 1)
    query = matmul(normed, wq).astype(LOW)
    full = jnp.concatenate([pair, peer], axis=0)
    width = full.shape[1] // 2
    keys, values = full[:, :width], full[:, width:]
    scores = score_table(query, keys, mask)
    top = jnp.max(scores, axis=-1, keepdims=True)
    expd = jnp.exp(scores - top)
    total = jnp.sum(expd, axis=-1, keepdims=True)
    probs = (expd / total).astype(LOW)
    context = jnp.einsum("hqk,khe->qhe", probs, heads(values), preferred_element_type=F32)
    context = context.astype(LOW).reshape(query.shape)
    branch = core_total(outer_cols(context, wo))
    saved = (inputs, normed, source, query, keys, values, top + jnp.log(total), context)
    return inputs + branch, saved


def attn_backward(grad, saved, gain, weights, mask, cross):
    wkv, wq, wo = weights
    inputs, normed, source, query, keys, values, logsum, context = saved
    size = grad.shape[0]
    low = grad.astype(LOW)
    out_grad = inner_rows(low, context).astype(LOW)
    ctx_grad = matmul(low, wo).astype(LOW)
    probs = jnp.exp(score_table(query, keys, mask) - logsum)
    value_part = jnp.einsum(
        "hqk,qhe->khe", probs.astype(LOW), heads(ctx_grad), preferred_element_type=F32
    )
    prob_grad = jnp.einsum("qhe,khe->hqk", heads(ctx_grad), heads(values), preferred_element_type=F32)
    delta = jnp.sum(prob_grad * probs, axis=-1, keepdims=True)
    score_grad = (probs * (prob_grad - delta)).astype(LOW)
    key_part = jnp.einsum("hqk,qhe->khe", score_grad, heads(query), preferred_element_type=F32)
    key_part = key_part * HEAD ** (-0.5)
    parts = jnp.concatenate(
        [key_part.reshape(keys.shape), value_part.reshape(values.shape)], axis=1
    )
    came = swap(parts[size:].astype(LOW), "seq", 1)
    query_low = jnp.einsum("hqk,khe->qhe", score_grad, heads(keys), preferred_element_type=F32)
    query_low = (query_low * HEAD ** (-0.5)).astype(LOW).reshape(query.shape)
    query_w_grad = inner_rows(normed, query_low).astype(LOW)
    pair_low = (parts[:size] + came.astype(F32)).astype(LOW)
    pair_w_grad = inner_rows(source, pair_low).astype(LOW)
    normed_part = outer_cols(query_low, wq)
    source_part = outer_cols(pair_low, wkv)
    if cross:
        normed_grad = core_total(normed_part)
        source_grad = core_total(source_part)
    else:
        normed_grad = core_total(normed_part + source_part)
        source_grad = None
    flat_grad, gain_grad, bias_grad = norm_backward(inputs, gain, normed_grad)
    side = jnp.concatenate([query_w_grad, out_grad], axis=1)
    return grad + flat_grad, source_grad, (gain_grad, bias_grad, pair_w_grad, side)


def ffn_forward(inputs, gain, bias, weights):
    up, down = weights
    normed = layer_norm(inputs, gain, bias)
    pre = matmul(normed, up)
    act = jax.nn.gelu(pre, approximate=False).astype(LOW)
    branch = core_total(outer_cols(act, down))
    return inputs + branch, (inputs, normed, pre, act)


def ffn_backward(grad, saved, gain, weights):
    up, down = weights
    inputs, normed, pre, act = saved
    low = grad.astype(LOW)
    _, pull = jax.vjp(lambda v: jax.nn.gelu(v, approximate=False), pre)
    (pre_grad,) = pull(matmul(low, down))
    pre_low = pre_grad.astype(LOW)
    normed_grad = core_total(outer_cols(pre_low, up))
    down_grad = inner_rows(low, act).astype(LOW)
    up_grad = inner_rows(normed, pre_low).astype(LOW)
    flat_grad, gain_grad, bias_grad = norm_backward(inputs, gain, normed_grad)
    return grad + flat_grad, (gain_grad, bias_grad, up_grad, down_grad)


def token_tables(lengths, groups, full_len, quarter):
    here, row = lax.axis_index("seq"), lax.axis_index("seq") // 2
    rows = lengths.shape[0]
    onehot = (groups[:, :, None] == jnp.arange(LANGS, dtype=jnp.int32)).astype(F32)
    counts = lax.psum(jnp.sum(onehot * lengths[:, :, None].astype(F32), axis=(0, 1)), "dp")
    all_tokens = rows * lax.axis_size("dp") * full_len
    seg_weight = all_tokens / (LANGS * jnp.sum(onehot * counts, axis=2))
    ends = pick(jnp.cumsum(lengths, axis=1), row)
    steps = jnp.arange(quarter, dtype=jnp.int32)
    places = jnp.concatenate([(here ^ k) * quarter + steps for k in (0, 2, 1, 3)])
    segs = jnp.sum((ends[None, :] <= places[:, None]).astype(jnp.int32), axis=1)
    mine = 2 * quarter
    same = segs[:mine, None] == segs[None, :]
    causal = same & (places[None, :] <= places[:mine, None])
    match = (segs[:mine, None] == jnp.arange(NSEG, dtype=jnp.int32)).astype(F32)
    tok_weight = jnp.sum(match * pick(seg_weight, row)[None, :], axis=1)
    return same, causal, tok_weight, all_tokens


def attn_shards(qkv, out):
    d, width = qkv.shape[1:]
    pair = jnp.concatenate([qkv[1], qkv[2]], axis=1)
    side = jnp.concatenate([qkv[0], out.T], axis=1)
    return pair, side


def split_side(side):
    width = side.shape[1] // 2
    return side[:, :width], side[:, width:]


def qkv_out(pair, side):
    width = side.shape[1] // 2
    qkv = jnp.stack([side[:, :width], pair[:, :width], pair[:, width : 2 * width]])
    return qkv, side[:, width:].T


def per_device(
    src,
    tgt,
    cotangent,
    lengths,
    groups,
    enc_gains,
    enc_biases,
    enc_qkv,
    enc_out,
    enc_up,
    enc_down,
    dec_gains,
    dec_biases,
    dec_self_qkv,
    dec_cross_qkv,
    dec_outs,
    dec_up,
    dec_down,
):
    rows, quarter, width = src.shape
    full_len = quarter * lax.axis_size("seq")
    n_enc, n_dec = enc_gains.shape[0], dec_gains.shape[0]

    norms = jnp.concatenate([enc_gains, enc_biases, dec_gains, dec_biases], axis=0)
    norm_cols = jnp.pad(norms.T, ((0, 0), (0, LANES - norms.shape[0])))
    pair, side = attn_shards(enc_qkv, enc_out)
    pair = jnp.concatenate([pair, norm_cols], axis=1)
    wide = pair.shape[1] - LANES
    e_pair_all = gather_weight(pair, 1)
    e_side = gather_weight(side, 2)
    e_pair = e_pair_all[:, :wide]
    table = e_pair_all[:, wide : wide + norms.shape[0]].T.astype(F32)
    e_gain, e_bias = table[:n_enc], table[n_enc : 2 * n_enc]
    d_gain, d_bias = table[2 * n_enc : 2 * n_enc + n_dec], table[2 * n_enc + n_dec :]
    pair, side = attn_shards(dec_self_qkv, dec_outs[0])
    s_pair, s_side = gather_weight(pair, 1), gather_weight(side, 2)
    e_up, e_down = gather_weight(enc_up, 1), gather_weight(enc_down.T, 2)
    pair, side = attn_shards(dec_cross_qkv, dec_outs[1])
    c_pair, c_side = gather_weight(pair, 1), gather_weight(side, 2)
    d_up, d_down = gather_weight(dec_up, 1), gather_weight(dec_down.T, 2)
    enc_w = (e_pair, *split_side(e_side))
    self_w = (s_pair, *split_side(s_side))
    cross_w = (c_pair, *split_side(c_side))

    same, causal, tok_weight, all_tokens = token_tables(lengths, groups, full_len, quarter)

    x_src = to_pair(src).astype(F32)
    x_tgt = to_pair(tgt).astype(F32)
    out_grad = to_pair(cotangent).astype(F32) * tok_weight[:, None]
    enc_mid, saved_one = attn_forward(x_src, e_gain[0], e_bias[0], enc_w, same, None)
    dec_mid, saved_three = attn_forward(x_tgt, d_gain[0], d_bias[0], self_w, causal, None)
    memory, saved_two = ffn_forward(enc_mid, e_gain[1], e_bias[1], (e_up, e_down))
    dec_cross, saved_four = attn_forward(
        dec_mid, d_gain[1], d_bias[1], cross_w, same, memory.astype(LOW)
    )
    decoded, saved_five = ffn_forward(dec_cross, d_gain[2], d_bias[2], (d_up, d_down))
    decoded = from_pair(decoded.astype(LOW))

    cross_in, fifth = ffn_backward(out_grad, saved_five, d_gain[2], (d_up, d_down))
    d_up_g, d_down_g = scatter_grad(fifth[2], 2), scatter_grad(fifth[3], 1)
    mid_in, memory_grad, fourth = attn_backward(
        cross_in, saved_four, d_gain[1], cross_w, same, True
    )
    c_pair_g, c_side_g = scatter_grad(fourth[2], 2), scatter_grad(fourth[3], 1)
    mid_grad, second = ffn_backward(memory_grad, saved_two, e_gain[1], (e_up, e_down))
    e_up_g, e_down_g = scatter_grad(second[2], 2), scatter_grad(second[3], 1)
    tgt_grad, _, third = attn_backward(mid_in, saved_three, d_gain[0], self_w, causal, False)
    s_pair_g, s_side_g = scatter_grad(third[2], 2), scatter_grad(third[3], 1)
    src_grad, _, first = attn_backward(mid_grad, saved_one, e_gain[0], enc_w, same, False)
    norm_grads = jnp.stack(
        [first[0], second[0], first[1], second[1]]
        + [third[0], fourth[0], fifth[0], third[1], fourth[1], fifth[1]]
    ).astype(LOW)
    norm_grads = jnp.pad(norm_grads.T, ((0, 0), (0, LANES - norm_grads.shape[0])))
    pair = jnp.concatenate([first[2], norm_grads], axis=1)
    e_pair_g, e_side_g = scatter_grad(pair, 2), scatter_grad(first[3], 1)

    factor = 1.0 / all_tokens
    norm_out = e_pair_g[:, wide : wide + norms.shape[0]].T * factor
    enc_qkv_g, enc_out_g = qkv_out(e_pair_g * factor, e_side_g * factor)
    self_qkv_g, self_out_g = qkv_out(s_pair_g * factor, s_side_g * factor)
    cross_qkv_g, cross_out_g = qkv_out(c_pair_g * factor, c_side_g * factor)
    return (
        decoded,
        from_pair(src_grad),
        from_pair(tgt_grad),
        from_pair(memory_grad),
        norm_out[:n_enc],
        norm_out[n_enc : 2 * n_enc],
        enc_qkv_g,
        enc_out_g,
        e_up_g * factor,
        (e_down_g * factor).T,
        norm_out[2 * n_enc : 2 * n_enc + n_dec],
        norm_out[2 * n_enc + n_dec :],
        self_qkv_g,
        cross_qkv_g,
        jnp.stack([self_out_g, cross_out_g]),
        d_up_g * factor,
        (d_down_g * factor).T,
    )


def solution(mesh):
    placed = (
        P("dp", "seq", None),
        P("dp", "seq", None),
        P("dp", "seq", None),
        P("dp", None),
        P("dp", None),
        P(None, ("dp", "seq")),
        P(None, ("dp", "seq")),
        P(None, ("dp", "seq"), "mp"),
        P("mp", ("dp", "seq")),
        P(("dp", "seq"), "mp"),
        P("mp", ("dp", "seq")),
        P(None, ("dp", "seq")),
        P(None, ("dp", "seq")),
        P(None, ("dp", "seq"), "mp"),
        P(None, ("dp", "seq"), "mp"),
        P(None, "mp", ("dp", "seq")),
        P(("dp", "seq"), "mp"),
        P("mp", ("dp", "seq")),
    )
    return jax.shard_map(
        per_device,
        mesh=mesh,
        in_specs=placed,
        out_specs=(
            P("dp", "seq", None),
            P("dp", "seq", None),
            P("dp", "seq", None),
            P("dp", "seq", None),
            P(None, ("dp", "seq")),
            P(None, ("dp", "seq")),
            P(None, ("dp", "seq"), "mp"),
            P("mp", ("dp", "seq")),
            P(("dp", "seq"), "mp"),
            P("mp", ("dp", "seq")),
            P(None, ("dp", "seq")),
            P(None, ("dp", "seq")),
            P(None, ("dp", "seq"), "mp"),
            P(None, ("dp", "seq"), "mp"),
            P(None, "mp", ("dp", "seq")),
            P(("dp", "seq"), "mp"),
            P("mp", ("dp", "seq")),
        ),
        check_vma=False,
    )
```

```python
import functools

import jax
import jax.numpy as jnp
from jax import lax
from jax.experimental import pallas as pl
from jax.experimental.pallas import tpu as pltpu
from jax.sharding import PartitionSpec as P

HEAD = 64
NSEG = 8
LANGS = 4
LANES = 128
TILE = 512
F32 = jnp.float32
LOW = jnp.bfloat16
EPS = 1e-05


def dot_nn(left, right):
    return jnp.dot(left, right, preferred_element_type=F32)


def dot_tn(left, right):
    return lax.dot_general(left, right, (((0,), (0,)), ((), ())), preferred_element_type=F32)


def dot_nt(left, right):
    return lax.dot_general(left, right, (((1,), (1,)), ((), ())), preferred_element_type=F32)


def xor_perm(size, bits):
    return [(i, i ^ bits) for i in range(size)]


def swap(value, axis, bits):
    return lax.ppermute(value, axis, xor_perm(lax.axis_size(axis), bits))


def pick(value, index, axis=0):
    return lax.dynamic_index_in_dim(value, index, axis, keepdims=False)


def params(mib):
    return pltpu.CompilerParams(vmem_limit_bytes=mib << 20)


def whole(shape):
    return pl.BlockSpec(shape, lambda *_: (0,) * len(shape))


def shaped(shape, dtype):
    return jax.ShapeDtypeStruct(shape, dtype)


def cost(flops, nbytes, exps=0):
    return pl.CostEstimate(flops=int(flops), bytes_accessed=int(nbytes), transcendentals=int(exps))


class Order:
    def __init__(self):
        self.last = []

    def __call__(self, step, *values):
        leaves, tree = jax.tree.flatten(values)
        spots = [i for i, leaf in enumerate(leaves) if isinstance(leaf, jax.Array)]
        for i, leaf in zip(spots, after([leaves[i] for i in spots], self.last), strict=True):
            leaves[i] = leaf
        out = step(*jax.tree.unflatten(tree, leaves))
        self.last = jax.tree.leaves(out)
        return out


def after(values, others):
    count = len(values)
    return list(lax.optimization_barrier((*values, *others))[:count])


def place(sources, order, cuts):
    flat, where_from = [], []
    for source in sources:
        if isinstance(source, tuple):
            where_from.append([(len(flat), None), (len(flat) + 1, None)])
            flat.extend(source)
        else:
            where_from.append([(len(flat), 0), (len(flat), 1)])
            flat.append(source)
    count = len(sources)
    rows, cols = flat[0].shape[-2:]
    each = order.shape[0] // count
    size = rows // each

    def body(order_ref, *refs):
        inputs = refs[: len(flat)]
        outs = refs[len(flat) : len(flat) + len(cuts)]
        held, in_sems, out_sems = refs[len(flat) + len(cuts) :]
        loads = []
        for j in range(count):
            for half in range(2):
                index, part = where_from[j][half]
                source = inputs[index] if part is None else inputs[index].at[part]
                loads.append(
                    pltpu.make_async_copy(source, held.at[half, j], in_sems.at[2 * j + half])
                )
                loads[-1].start()
        stores = []
        for j in range(count):
            for half in range(2):
                loads[2 * j + half].wait()
                for i in range(each):
                    spot = order_ref[j * each + i]
                    start = pl.multiple_of(spot * size, size)
                    for n, (side, first, width) in enumerate(cuts):
                        if side != half:
                            continue
                        stores.append(
                            pltpu.make_async_copy(
                                held.at[half, j, pl.ds(i * size, size), pl.ds(first, width)],
                                outs[n].at[pl.ds(start, size)],
                                out_sems.at[j * each + i, n],
                            )
                        )
                        stores[-1].start()
        for store in stores:
            store.wait()

    total = count * rows
    return pl.pallas_call(
        body,
        out_shape=[shaped((total, width), LOW) for _, _, width in cuts],
        in_specs=[pl.BlockSpec(memory_space=pltpu.SMEM)]
        + [pl.BlockSpec(memory_space=pl.ANY)] * len(flat),
        out_specs=[pl.BlockSpec(memory_space=pl.ANY)] * len(cuts),
        scratch_shapes=[
            pltpu.VMEM((2, count, rows, cols), LOW),
            pltpu.SemaphoreType.DMA((2 * count,)),
            pltpu.SemaphoreType.DMA((order.shape[0], len(cuts))),
        ],
        compiler_params=params(24),
        cost_estimate=cost(0, 8 * total * cols),
    )(order, *flat)


def seq_steps():
    steps, step = [], lax.axis_size("seq") // 2
    while step:
        steps.append(step)
        step //= 2
    return steps


def seq_order():
    spots = [0]
    for step in seq_steps():
        spots += [spot ^ step for spot in spots]
    return spots


class Gather:
    def __init__(self, shard):
        self.column = shard
        self.steps = seq_steps()

    def along(self, others=()):
        (ready,) = after([self.column], others)
        self.came = swap(ready, "seq", self.steps.pop(0))

    def join(self, order):
        self.column = order(
            lambda one, two: jnp.concatenate([one, two], axis=1), self.column, self.came
        )

    def across(self, others=()):
        self.plain = lax.axis_size("dp") != 4
        self.near = []
        if self.plain:
            return
        (ready,) = after([self.column], others)
        self.near = [swap(ready, "dp", 1), swap(ready, "dp", 2)]

    def far(self, order):
        if self.plain:
            return
        one, two = order(lambda x, y: (x[0], y[1]), *self.near)
        self.last = (swap(one, "dp", 2), swap(two, "dp", 1))

    def place(self, order, cuts):
        if self.plain:
            return order(place_weights, [self.column], cuts)
        return order(place_weights, [self.column, *self.near, self.last], cuts)


def place_weights(sources, cuts):
    here, spot = lax.axis_index("seq"), lax.axis_index("dp")
    spots = jnp.asarray(seq_order(), jnp.int32) ^ here.astype(jnp.int32)
    if lax.axis_size("dp") != 4:
        cols = sources[0].shape[2]
        halves = place(sources, spots, [(0, 0, cols), (1, 0, cols)])
        halves = [lax.all_gather(half, "dp", axis=0, tiled=True) for half in halves]
        return [halves[side][:, first : first + width] for side, first, width in cuts]
    blocks = jnp.arange(4, dtype=jnp.int32) ^ spot.astype(jnp.int32)
    spots = (blocks[:, None] * spots.shape[0] + spots[None, :]).reshape(-1)
    return place(sources, spots, cuts)


def block_order(first):
    if lax.axis_size("dp") != 4:
        return jnp.arange(4, dtype=jnp.int32)
    spot = lax.axis_index("dp").astype(jnp.int32)
    return jnp.asarray([first, 3, 0, 3 - first], jnp.int32) ^ spot


def row_order(first):
    away = jnp.arange(lax.axis_size("seq"), dtype=jnp.int32)
    away = away ^ lax.axis_index("seq").astype(jnp.int32)
    turn, bits = jnp.zeros_like(away), seq_steps()
    for one, two in zip(bits, reversed(bits), strict=True):
        turn = turn + jnp.where((away & one) != 0, two, 0)
    return jnp.concatenate([block_order(first), turn])


def weight_grad(pairs, order):
    tokens, width = pairs[0][0].shape
    size = width // 4
    cols = sum(right.shape[1] for _, right in pairs)
    n_seq = lax.axis_size("seq")
    near = lax.axis_size("dp") == 4
    unit = size // n_seq if near else size

    def body(order_ref, *refs):
        away, stay = refs[2 * len(pairs) :]
        step = pl.program_id(0)
        start = 0
        for j in range(len(pairs)):
            left, right = refs[2 * j], refs[2 * j + 1]
            part = dot_tn(left[...], right[...]).astype(LOW)
            stop = start + part.shape[1]

            def put(out):
                for k in range(size // unit):
                    spot = order_ref[4 + k] if near else k
                    rows = pl.ds(pl.multiple_of(spot * unit, unit), unit)
                    out[rows, start:stop] = part[k * unit : (k + 1) * unit]

            pl.when(step < 2)(functools.partial(put, away))
            pl.when(step >= 2)(functools.partial(put, stay))
            start = stop

    specs, values = [], []
    for left, right in pairs:
        specs.append(pl.BlockSpec((tokens, size), lambda i, order: (0, order[i])))
        specs.append(pl.BlockSpec(right.shape, lambda i, order: (0, 0)))
        values += [left, right]
    return pl.pallas_call(
        body,
        grid_spec=pltpu.PrefetchScalarGridSpec(
            num_scalar_prefetch=1,
            grid=(4,),
            in_specs=specs,
            out_specs=[
                pl.BlockSpec((size, cols), lambda i, order: (jnp.minimum(i, 1), 0)),
                pl.BlockSpec((size, cols), lambda i, order: (jnp.maximum(i - 2, 0), 0)),
            ],
        ),
        out_shape=[shaped((2 * size, cols), LOW)] * 2,
        compiler_params=params(32),
        cost_estimate=cost(2 * tokens * width * cols, 4 * width * cols),
    )(order, *values)


class Scatter:
    def __init__(self, pair, side, factor):
        self.halves, self.factor, self.stage = (pair, side), factor, 0
        self.bits = (2, 1)
        self.plain = lax.axis_size("dp") != 4

    def start(self, j):
        away, _ = self.halves[j]
        return None if self.plain else swap(away, "dp", self.bits[j])

    def begin(self):
        self.came = [self.start(0), self.start(1)]
        return self

    def add(self, order):
        self.stage += 1
        if self.plain:
            if self.stage == 4:
                self.out = self.plain_sum()
            return
        (getattr(self, "add%d" % self.stage))(order)

    def add1(self, order):
        stays = [stay for _, stay in self.halves]

        def step(stays, came):
            size = stays[0].shape[0] // 2
            onward = [
                (stay[size:].astype(F32) + new[size:].astype(F32)).astype(LOW)
                for stay, new in zip(stays, came, strict=True)
            ]
            return onward

        onward = order(step, stays, self.came)
        self.last = [swap(value, "dp", 3 - bit) for value, bit in zip(onward, self.bits, strict=True)]

    def add2(self, order):
        stays = [stay for _, stay in self.halves]

        def step(stays, came, last):
            size = stays[0].shape[0] // 2
            both = jnp.stack(
                [
                    stay[:size].astype(F32) + new[:size].astype(F32) + more.astype(F32)
                    for stay, new, more in zip(stays, came, last, strict=True)
                ]
            )
            size = size // 2
            return both[:, size:].astype(LOW), both[:, :size]

        away, self.kept = order(step, stays, self.came, self.last)
        self.came = swap(away, "seq", 1)

    def add3(self, order):
        def step(kept, came):
            both = kept + came.astype(F32)
            size = both.shape[1] // 2
            return both[:, size:].astype(LOW), both[:, :size]

        away, self.kept = order(step, self.kept, self.came)
        self.came = swap(away, "seq", 2)

    def add4(self, order):
        self.out = order(
            lambda kept, came: (kept + came.astype(F32)) * self.factor, self.kept, self.came
        )

    def plain_sum(self):
        here, n_seq = lax.axis_index("seq"), lax.axis_size("seq")
        columns = []
        for away, stay in self.halves:
            grad = jnp.concatenate([away, stay], axis=0)
            columns.append(
                lax.psum_scatter(grad, "dp", scatter_dimension=0, tiled=True).astype(F32)
            )
        both = jnp.stack(columns)
        both = both.reshape(2, n_seq, -1, both.shape[-1])
        result = pick(both, here, 1)
        for k in range(1, n_seq):
            result = result + swap(pick(both, here ^ k, 1).astype(LOW), "seq", k).astype(F32)
        return result * self.factor


def trade_start(value):
    size = value.shape[0] // 2
    part = lax.dynamic_slice_in_dim(value, lax.axis_index("mp") * size, size, 0)
    return swap(part, "seq", 2)


def trade_end(part):
    rest = swap(part, "mp", 1)
    return jnp.where(
        lax.axis_index("mp") == 0,
        jnp.concatenate([part, rest], axis=0),
        jnp.concatenate([rest, part], axis=0),
    )


def pair_start(value, others):
    row = lax.axis_index("seq") // 2
    (sent,) = after([pick(value, 1 - row)], others)
    return trade_start(sent)


def pair_end(value, part):
    row = lax.axis_index("seq") // 2
    return jnp.concatenate([pick(value, row), trade_end(part)], axis=0)


def back_start(value):
    return trade_start(value[value.shape[0] // 2 :].astype(LOW))


def back_end(value, part):
    kept = value[: value.shape[0] // 2]
    came = trade_end(part).astype(value.dtype)
    row = lax.axis_index("seq") // 2
    return jnp.where(row == 0, jnp.stack([kept, came]), jnp.stack([came, kept]))


def norm_parts(values):
    center = values - jnp.mean(values, axis=-1, keepdims=True)
    scale = lax.rsqrt(jnp.mean(center * center, axis=-1, keepdims=True) + EPS)
    return center * scale, scale


def enter(inputs, parts, norm, weight):
    tokens, width = inputs.shape
    blocks = weight.shape[1] // TILE
    rows = [inputs, *parts] + ([] if norm is None else list(norm))
    keep = len(parts) > 0 and norm is not None

    def body(*refs):
        x_ref, part_refs = refs[0], refs[1 : 1 + len(parts)]
        norm_refs = refs[1 + len(parts) : len(rows)]
        w_ref = refs[len(rows)]
        outs = refs[len(rows) + 1 :]
        low_ref, out_ref = outs[0], outs[1]

        @pl.when(pl.program_id(0) == 0)
        def _():
            x = x_ref[...].astype(F32)
            if part_refs:
                x = x + (part_refs[0][...].astype(F32) + part_refs[1][...].astype(F32))
            if keep:
                outs[2][...] = x
            if norm_refs:
                x = norm_parts(x)[0] * norm_refs[0][...] + norm_refs[1][...]
            low_ref[...] = x.astype(LOW)

        out_ref[0] = dot_nn(low_ref[...], w_ref[...]).astype(LOW)

    result = pl.pallas_call(
        body,
        grid=(blocks,),
        in_specs=[whole(v.shape) for v in rows] + [pl.BlockSpec((width, TILE), lambda j: (0, j))],
        out_specs=[
            whole((tokens, width)),
            pl.BlockSpec((1, tokens, TILE), lambda j: (j, 0, 0)),
        ]
        + ([whole((tokens, width))] if keep else []),
        out_shape=[shaped((tokens, width), LOW), shaped((blocks, tokens, TILE), LOW)]
        + ([shaped((tokens, width), F32)] if keep else []),
        compiler_params=params(32),
        cost_estimate=cost(2 * tokens * width * weight.shape[1], 14 * tokens * width),
    )(*rows, weight)
    return tuple(result)


def attend_body(rows, q_ref, ko_ref, kp_ref, vo_ref, vp_ref, bias_ref, ctx_ref, lse_ref):
    tokens = q_ref.shape[0]
    lane = lax.broadcasted_iota(jnp.int32, (rows, LANES), 1)
    ko, kp, vo, vp = ko_ref[0], kp_ref[0], vo_ref[0], vp_ref[0]
    for r in range(0, tokens, rows):
        q = q_ref[r : r + rows] * jnp.asarray(HEAD**-0.5, LOW)
        ctx = stat = None
        for h in range(LANES // HEAD):
            mine = (lane // HEAD) == h
            qh = jnp.where(mine, q, jnp.zeros_like(q))
            so = dot_nt(qh, ko) + bias_ref[r : r + rows, :tokens]
            sp = dot_nt(qh, kp) + bias_ref[r : r + rows, tokens:]
            top = jnp.maximum(
                jnp.max(so, axis=1, keepdims=True), jnp.max(sp, axis=1, keepdims=True)
            )
            eo, ep = jnp.exp(so - top), jnp.exp(sp - top)
            total = jnp.sum(eo, axis=1, keepdims=True) + jnp.sum(ep, axis=1, keepdims=True)
            acc = dot_nn(eo.astype(LOW), vo) + dot_nn(ep.astype(LOW), vp)
            acc = acc * (1.0 / total)
            lse = jnp.broadcast_to(top + jnp.log(total), (rows, LANES))
            ctx = acc if ctx is None else jnp.where(mine, acc, ctx)
            stat = lse if stat is None else jnp.where(mine, lse, stat)
        ctx_ref[r : r + rows] = ctx.astype(LOW)
        lse_ref[r : r + rows] = stat


def kv_spec(tokens, half):
    return pl.BlockSpec((1, tokens, LANES), lambda i: (half, 0, i))


def attend(query, own, peer, bias):
    tokens, width = query.shape
    spec = pl.BlockSpec((tokens, LANES), lambda i: (0, i))
    return pl.pallas_call(
        functools.partial(attend_body, 256),
        grid=(width // LANES,),
        in_specs=[spec]
        + [kv_spec(tokens, half) for half in (0, 0, 1, 1)]
        + [whole(bias.shape)],
        out_specs=[spec, spec],
        out_shape=[shaped((tokens, width), LOW), shaped((tokens, width), F32)],
        compiler_params=params(40),
        cost_estimate=cost(16 * tokens * tokens * width, 16 * tokens * width, 2 * tokens * tokens * 8),
    )(query, own, peer, own, peer, bias)


def attend_back_body(
    q_ref, ko_ref, kp_ref, vo_ref, vp_ref, g_ref, lse_ref, bias_ref, dq_ref, own_ref, peer_ref, acc
):
    tokens = q_ref.shape[0]
    lane = lax.broadcasted_iota(jnp.int32, (tokens, LANES), 1)
    q = q_ref[...] * jnp.asarray(HEAD**-0.5, LOW)
    g = g_ref[...]
    lse_t = lse_ref[...].T
    parts = ((kp_ref, vp_ref, peer_ref, tokens), (ko_ref, vo_ref, own_ref, 0))
    keys_t = [k_ref[0].T for k_ref, _, _, _ in parts]
    for h in range(LANES // HEAD):
        mine = (lane // HEAD) == h
        qh = jnp.where(mine, q, jnp.zeros_like(q))
        gh = jnp.where(mine, g, jnp.zeros_like(g))
        rows = slice(h * HEAD, (h + 1) * HEAD)
        lse = lse_t[h * HEAD : h * HEAD + 1]
        probs, inner = [], []
        for k_ref, v_ref, _, base in parts:
            scores = dot_nt(k_ref[0], qh) + bias_ref[base : base + tokens]
            probs.append(jnp.exp(scores - lse))
            inner.append(dot_nt(v_ref[0], gh))
        delta = sum(jnp.sum(p * d, axis=0, keepdims=True) for p, d in zip(probs, inner))
        total = None
        for j, (_, _, out_ref, _) in enumerate(parts):
            grads = (probs[j] * (inner[j] - delta)).astype(LOW)
            dv = dot_nn(probs[j].astype(LOW), gh).astype(LOW)
            dk = dot_nn(grads, qh).astype(LOW)
            part = dot_nn(keys_t[j][rows], grads)
            total = part if total is None else total + part
            if h == 0:
                out_ref[0], out_ref[1] = dk, dv
            else:
                out_ref[0] += dk
                out_ref[1] += dv
        acc[rows] = total
    dq_ref[...] = (acc[...].T * HEAD**-0.5).astype(LOW)


def attend_back(query, own, peer, grad, lse, bias_t):
    tokens, width = query.shape
    spec = pl.BlockSpec((tokens, LANES), lambda i: (0, i))
    both = pl.BlockSpec((2, tokens, LANES), lambda i: (0, 0, i))
    return pl.pallas_call(
        attend_back_body,
        grid=(width // LANES,),
        in_specs=[spec]
        + [kv_spec(tokens, half) for half in (0, 0, 1, 1)]
        + [spec, spec, whole(bias_t.shape)],
        out_specs=[spec, both, both],
        out_shape=[shaped((tokens, width), LOW)] + [shaped((2, tokens, width), LOW)] * 2,
        scratch_shapes=[pltpu.VMEM((LANES, tokens), F32)],
        compiler_params=params(40),
        cost_estimate=cost(40 * tokens * tokens * width, 24 * tokens * width, 2 * tokens * tokens * 8),
    )(query, own, peer, own, peer, grad, lse, bias_t)


def attend_leave(dq, own, came, wq, wkv, apart):
    tokens, width = dq.shape[0], wq.shape[0]
    size = tokens // 2

    def body(dq_ref, own_ref, came_ref, wq_ref, wkv_ref, pair_ref, *outs):
        low = [
            (own_ref[j].astype(F32) + came_ref[j].astype(F32)).astype(LOW) for j in range(2)
        ]
        cols = low[0].shape[1]
        for j in range(2):
            pair_ref[:, j * cols : (j + 1) * cols] = low[j]
        first = dot_nt(dq_ref[...], wq_ref[...])
        rest = dot_nt(pair_ref[...], wkv_ref[...])
        if apart:
            outs[0][0] = first.astype(LOW)
            outs[0][1] = rest.astype(LOW)
        else:
            outs[0][...] = (first + rest).astype(LOW)

    part_spec = (
        pl.BlockSpec((2, size, width), lambda i: (0, i, 0))
        if apart
        else pl.BlockSpec((size, width), lambda i: (i, 0))
    )
    cols = own.shape[2]
    return pl.pallas_call(
        body,
        grid=(2,),
        in_specs=[
            pl.BlockSpec((size, cols), lambda i: (i, 0)),
            pl.BlockSpec((2, size, cols), lambda i: (0, i, 0)),
            pl.BlockSpec((2, size, cols), lambda i: (0, i, 0)),
            whole(wq.shape),
            whole(wkv.shape),
        ],
        out_specs=[pl.BlockSpec((size, 2 * cols), lambda i: (i, 0)), part_spec],
        out_shape=[
            shaped((tokens, 2 * cols), LOW),
            shaped((2, tokens, width) if apart else (tokens, width), LOW),
        ],
        compiler_params=params(32),
        cost_estimate=cost(6 * tokens * width * cols, 14 * tokens * cols + 6 * width * cols),
    )(dq, own, came, wq, wkv)


def feed(inputs, parts, norm, up, down):
    tokens, width = inputs.shape
    hidden = up.shape[1]

    def body(x_ref, one_ref, two_ref, gain_ref, bias_ref, up_ref, down_ref, *rest):
        normed_ref, total_ref, act_ref, slope_ref, part_ref, acc = rest
        step = pl.program_id(0)

        @pl.when(step == 0)
        def _():
            x = x_ref[...].astype(F32) + (one_ref[...].astype(F32) + two_ref[...].astype(F32))
            total_ref[...] = x
            normed_ref[...] = (norm_parts(x)[0] * gain_ref[...] + bias_ref[...]).astype(LOW)

        pre = dot_nn(normed_ref[...], up_ref[...])
        below = 0.5 + 0.5 * lax.erf(pre * (0.5**0.5))
        act = (pre * below).astype(LOW)
        act_ref[...] = act
        slope = below + pre * (jnp.exp(pre * pre * -0.5) * 0.3989422804014327)
        slope_ref[...] = slope.astype(LOW)
        part = dot_nt(act, down_ref[...])

        @pl.when(step == 0)
        def _():
            acc[...] = part

        @pl.when(step > 0)
        def _():
            acc[...] += part

        @pl.when(step == pl.num_programs(0) - 1)
        def _():
            part_ref[...] = acc[...].astype(LOW)

    block = pl.BlockSpec((tokens, TILE), lambda j: (0, j))
    weight = pl.BlockSpec((width, TILE), lambda j: (0, j))
    same = whole((tokens, width))
    return pl.pallas_call(
        body,
        grid=(hidden // TILE,),
        in_specs=[same, same, same, whole((1, width)), whole((1, width)), weight, weight],
        out_specs=[same, same, block, block, same],
        out_shape=[
            shaped((tokens, width), LOW),
            shaped((tokens, width), F32),
            shaped((tokens, hidden), LOW),
            shaped((tokens, hidden), LOW),
            shaped((tokens, width), LOW),
        ],
        scratch_shapes=[pltpu.VMEM((tokens, width), F32)],
        compiler_params=params(48),
        cost_estimate=cost(4 * tokens * width * hidden, 8 * width * hidden, 2 * tokens * hidden),
    )(inputs, *parts, *norm, up, down)


def feed_back(low, slope, up, down):
    tokens, width = low.shape
    hidden = up.shape[1]

    def body(low_ref, slope_ref, up_ref, down_ref, pre_ref, part_ref, acc):
        step = pl.program_id(0)
        act_grad = dot_nn(low_ref[...], down_ref[...])
        pre = (act_grad * slope_ref[...].astype(F32)).astype(LOW)
        pre_ref[...] = pre
        part = dot_nt(pre, up_ref[...])

        @pl.when(step == 0)
        def _():
            acc[...] = part

        @pl.when(step > 0)
        def _():
            acc[...] += part

        @pl.when(step == pl.num_programs(0) - 1)
        def _():
            part_ref[...] = acc[...].astype(LOW)

    block = pl.BlockSpec((tokens, TILE), lambda j: (0, j))
    weight = pl.BlockSpec((width, TILE), lambda j: (0, j))
    same = whole((tokens, width))
    return pl.pallas_call(
        body,
        grid=(hidden // TILE,),
        in_specs=[same, block, weight, weight],
        out_specs=[block, same],
        out_shape=[shaped((tokens, hidden), LOW), shaped((tokens, width), LOW)],
        scratch_shapes=[pltpu.VMEM((tokens, width), F32)],
        compiler_params=params(48),
        cost_estimate=cost(4 * tokens * width * hidden, 6 * width * hidden),
    )(low, slope, up, down)


def norm_back(grad, values, parts, gain, weight):
    tokens, width = grad.shape
    size = tokens // 2

    def body(*refs):
        g_ref, x_ref, one_ref, two_ref, gain_ref = refs[:5]
        outs = refs[5:] if weight is None else refs[6:]
        step = pl.program_id(0)
        normed_grad = one_ref[...].astype(F32) + two_ref[...].astype(F32)
        unit, scale = norm_parts(x_ref[...].astype(F32))
        gains = jnp.sum(normed_grad * unit, axis=0, keepdims=True)
        biases = jnp.sum(normed_grad, axis=0, keepdims=True)
        inner = normed_grad * gain_ref[...]
        inner = inner - jnp.mean(inner, axis=-1, keepdims=True) - unit * jnp.mean(
            inner * unit, axis=-1, keepdims=True
        )
        total = g_ref[...] + inner * scale
        outs[0][...] = total

        @pl.when(step == 0)
        def _():
            outs[1][...] = jnp.concatenate([gains, biases], axis=0)

        @pl.when(step > 0)
        def _():
            outs[1][...] += jnp.concatenate([gains, biases], axis=0)

        if weight is not None:
            low = total.astype(LOW)
            outs[2][...] = low
            outs[3][...] = dot_nn(low, refs[5][...]).astype(LOW)

    row = pl.BlockSpec((size, width), lambda i: (i, 0))
    in_specs = [row] * 4 + [whole((1, width))]
    out_specs = [row, whole((2, width))]
    out_shape = [shaped((tokens, width), F32), shaped((2, width), F32)]
    extra = []
    if weight is not None:
        cols = weight.shape[1]
        extra = [weight]
        in_specs.append(whole(weight.shape))
        out_specs += [row, pl.BlockSpec((size, cols), lambda i: (i, 0))]
        out_shape += [shaped((tokens, width), LOW), shaped((tokens, cols), LOW)]
    return pl.pallas_call(
        body,
        grid=(tokens // size,),
        in_specs=in_specs,
        out_specs=out_specs,
        out_shape=out_shape,
        compiler_params=params(40),
        cost_estimate=cost(20 * tokens * width, 20 * tokens * width),
    )(grad, values, *parts, gain, *extra)


def weight_grad_one(left, right, order):
    return weight_grad([(left, right)], order)


def weight_grad_two(one, two, order):
    return weight_grad([one, two], order)


def attend_leave_apart(dq, own, came, wq, wkv):
    return attend_leave(dq, own, came, wq, wkv, True)


def attend_leave_joined(dq, own, came, wq, wkv):
    return attend_leave(dq, own, came, wq, wkv, False)


def norm_back_last(grad, values, parts, gain):
    return norm_back(grad, values, parts, gain, None)


def low_too(value):
    return value, value.astype(LOW)


def norm_halves(norm_rows, width):
    count = norm_rows.shape[0]
    cols = jnp.pad(norm_rows.T, ((0, 0), (0, LANES - count)))
    result = []
    for first in (2, 1):
        quarters = cols.reshape(4, -1, LANES)
        blocks = [pick(quarters, block_order(first)[i]) for i in range(4)]
        if lax.axis_size("dp") == 4:
            n_seq, here = lax.axis_size("seq"), lax.axis_index("seq")
            blocks = [
                pick(block.reshape(n_seq, -1, LANES), here ^ k)
                for block in blocks
                for k in seq_order()
            ]
        block = jnp.concatenate(blocks, axis=0)
        result.append((block[: width // 2], block[width // 2 :]))
    return result


def token_counts(lengths, groups):
    onehot = (groups[:, :, None] == jnp.arange(LANGS, dtype=jnp.int32)).astype(F32)
    counts = jnp.sum(onehot * lengths[:, :, None].astype(F32), axis=(0, 1))
    if lax.axis_size("dp") != 4:
        counts = lax.psum(counts, "dp")
        return counts, counts
    counts = jnp.pad(counts[None], ((0, 7), (0, LANES - LANGS)))
    counts = counts + swap(counts, "dp", 1)
    came = swap(counts, "dp", 2)
    return (counts + came)[0, :LANGS], came


def token_tables(lengths, groups, counts, full_len, quarter):
    here, row = lax.axis_index("seq"), lax.axis_index("seq") // 2
    rows = lengths.shape[0]
    onehot = (groups[:, :, None] == jnp.arange(LANGS, dtype=jnp.int32)).astype(F32)
    all_tokens = rows * lax.axis_size("dp") * full_len
    seg_weight = all_tokens / (LANGS * jnp.sum(onehot * counts, axis=2))
    ends = pick(jnp.cumsum(lengths, axis=1), row)
    steps = jnp.arange(quarter, dtype=jnp.int32)
    places = jnp.concatenate([(here ^ k) * quarter + steps for k in (0, 2, 1, 3)])
    segs = jnp.sum((ends[None, :] <= places[:, None]).astype(jnp.int32), axis=1)
    mine = 2 * quarter
    same = segs[:mine, None] == segs[None, :]
    causal = same & (places[None, :] <= places[:mine, None])
    same_t = segs[:, None] == segs[None, :mine]
    causal_t = same_t & (places[:, None] <= places[None, :mine])
    offsets = [jnp.where(mask, 0.0, -1e30).astype(F32) for mask in (same, same_t, causal, causal_t)]
    match = (segs[:mine, None] == jnp.arange(NSEG, dtype=jnp.int32)).astype(F32)
    tok_weight = jnp.sum(match * pick(seg_weight, row)[None, :], axis=1)
    return offsets, tok_weight, all_tokens


def attn_shard(qkv, out):
    pair = jnp.concatenate([qkv[1], qkv[2]], axis=1)
    side = jnp.concatenate([qkv[0], out.T], axis=1)
    return jnp.stack([pair, side])


def qkv_out(both):
    width = both.shape[2] // 2
    qkv = jnp.stack([both[1, :, :width], both[0, :, :width], both[0, :, width:]])
    return qkv, both[1, :, width:].T


def project(left, right):
    return dot_nn(left, right).astype(LOW)


def project_out(ctx, wo):
    return dot_nt(ctx, wo).astype(LOW)


def other_core(part):
    return swap(part, "mp", 1)


def per_device(
    src,
    tgt,
    cotangent,
    lengths,
    groups,
    enc_gains,
    enc_biases,
    enc_qkv,
    enc_out,
    enc_up,
    enc_down,
    dec_gains,
    dec_biases,
    dec_self_qkv,
    dec_cross_qkv,
    dec_outs,
    dec_up,
    dec_down,
):
    rows, quarter, width = src.shape
    full_len = quarter * lax.axis_size("seq")
    n_enc, n_dec = enc_gains.shape[0], dec_gains.shape[0]
    half, hidden = enc_qkv.shape[2], enc_up.shape[1]
    order = Order()

    norms = jnp.concatenate([enc_gains, enc_biases, dec_gains, dec_biases], axis=0)
    n_norms = norms.shape[0]
    extra = jnp.pad(norms.T[None], ((0, 1), (0, 0), (0, LANES - n_norms)))
    shards = [
        jnp.concatenate([attn_shard(enc_qkv, enc_out), extra], axis=2),
        attn_shard(dec_self_qkv, dec_outs[0]),
        jnp.stack([enc_up, enc_down.T]),
        attn_shard(dec_cross_qkv, dec_outs[1]),
        jnp.stack([dec_up, dec_down.T]),
    ]
    attn_cuts = [(0, 0, 2 * half), (1, 0, half), (1, half, half)]
    feed_cuts = [(0, 0, hidden), (1, 0, hidden)]
    counts, counted = token_counts(lengths, groups)
    one, two, three, four, five = [Gather(shard) for shard in shards]
    one.along()
    two.along([one.came])
    one.join(order)
    one.along()
    src_part = pair_start(src, [two.came])
    three.along([two.came])
    two.join(order)
    one.join(order)
    one.across([counted])
    two.along([one.column])
    y_first, x_first = order(lambda: (row_order(2), row_order(1)))
    two.join(order)
    two.across(one.near)
    three.join(order)
    three.along([two.column])
    four.along([three.column])
    x_src = order(pair_end, src, src_part)
    one.far(order)
    offsets, tok_weight, all_tokens = order(
        token_tables, lengths, groups, counts, full_len, quarter
    )
    same, same_t, causal, causal_t = offsets
    factor = 1.0 / all_tokens
    three.join(order)
    four.join(order)
    four.along()
    five.along([four.column])
    *enc_w, table = one.place(order, attn_cuts + [(0, 2 * half, LANES)])
    table = table[:, :n_norms].T.astype(F32)[:, None]
    e_norm = [(table[i], table[n_enc + i]) for i in range(n_enc)]
    d_norm = [(table[2 * n_enc + i], table[2 * n_enc + n_dec + i]) for i in range(n_dec)]
    enc_in, enc_own = order(enter, x_src, (), e_norm[0], enc_w[0])
    enc_peer = swap(enc_own, "seq", 1)
    tgt_part = pair_start(tgt, [five.came])
    two.far(order)
    three.across(two.near)
    enc_q = order(project, enc_in, enc_w[1])
    four.join(order)
    enc_ctx, enc_lse = order(attend, enc_q, enc_own, enc_peer, same)
    enc_part = order(project_out, enc_ctx, enc_w[2])
    enc_other = other_core(enc_part)
    five.join(order)
    five.along()
    self_w = two.place(order, attn_cuts)
    x_tgt = order(pair_end, tgt, tgt_part)
    cot_part = pair_start(cotangent, [x_tgt])
    self_in, self_own = order(enter, x_tgt, (), d_norm[0], self_w[0])
    self_peer = swap(self_own, "seq", 1)
    self_q = order(project, self_in, self_w[1])
    three.far(order)
    four.across(three.near)
    self_ctx, self_lse = order(attend, self_q, self_own, self_peer, causal)
    self_part = order(project_out, self_ctx, self_w[2])
    self_other = other_core(self_part)
    five.join(order)
    cot = order(pair_end, cotangent, cot_part)
    out_grad, out_low = order(
        lambda cot, weight: low_too(cot.astype(F32) * weight[:, None]), cot, tok_weight
    )
    e_up, e_down = three.place(order, feed_cuts)
    four.far(order)
    five.across(four.near)
    enc_normed, enc_mid, enc_act, enc_slope, mem_part = order(
        feed, x_src, (enc_part, enc_other), e_norm[1], e_up, e_down
    )
    mem_other = other_core(mem_part)
    cross_w = four.place(order, attn_cuts)
    source, cross_own = order(enter, enc_mid, (mem_part, mem_other), None, cross_w[0])
    cross_peer = swap(cross_own, "seq", 1)
    cross_in, cross_q, dec_mid = order(
        enter, x_tgt, (self_part, self_other), d_norm[1], cross_w[1]
    )
    cross_q = cross_q[0]
    five.far(order)
    cross_ctx, cross_lse = order(attend, cross_q, cross_own, cross_peer, same)
    cross_part = order(project_out, cross_ctx, cross_w[2])
    cross_other = other_core(cross_part)
    d_up, d_down = five.place(order, feed_cuts)
    dec_normed, dec_cross, dec_act, dec_slope, dec_part = order(
        feed, dec_mid, (cross_part, cross_other), d_norm[2], d_up, d_down
    )
    dec_other = other_core(dec_part)

    pre_grad, part = order(feed_back, out_low, dec_slope, d_up, d_down)
    parts = (part, other_core(part))
    down_g = order(weight_grad_one, out_low, dec_act, x_first)
    up_g = order(weight_grad_one, dec_normed, pre_grad, y_first)
    d_feed = Scatter(up_g, down_g, factor).begin()
    cross_g, norm_five, low, ctx_grad = order(
        norm_back, out_grad, dec_cross, parts, d_norm[2][0], cross_w[2]
    )
    dq, own_grad, peer_grad = order(
        attend_back, cross_q, cross_own, cross_peer, ctx_grad, cross_lse, same_t
    )
    came = swap(peer_grad, "seq", 1)
    side_g = order(weight_grad_two, (cross_in, dq), (low, cross_ctx), x_first)
    decoded = order(
        lambda total, one, two: (total + (one.astype(F32) + two.astype(F32))).astype(LOW),
        dec_cross,
        dec_part,
        dec_other,
    )
    decoded_part = back_start(decoded)
    d_feed.add(order)
    pair_low, part = order(attend_leave_apart, dq, own_grad, came, cross_w[1], cross_w[0])
    other = other_core(part)
    pair_g = order(weight_grad_one, source, pair_low, y_first)
    cross = Scatter(pair_g, side_g, factor).begin()
    memory_grad, memory_low = order(
        lambda one, two: low_too(one[1].astype(F32) + two[1].astype(F32)), part, other
    )
    memory_part = back_start(memory_low)
    cross_parts = (part[0], other[0])
    pre_grad, enc_part = order(feed_back, memory_low, enc_slope, e_up, e_down)
    enc_parts = (enc_part, other_core(enc_part))
    down_g = order(weight_grad_one, memory_low, enc_act, x_first)
    up_g = order(weight_grad_one, enc_normed, pre_grad, y_first)
    e_feed = Scatter(up_g, down_g, factor).begin()
    mid_g, norm_four, low, ctx_grad = order(
        norm_back, cross_g, dec_mid, cross_parts, d_norm[1][0], self_w[2]
    )
    d_feed.add(order)
    cross.add(order)
    dq, own_grad, peer_grad = order(
        attend_back, self_q, self_own, self_peer, ctx_grad, self_lse, causal_t
    )
    came = swap(peer_grad, "seq", 1)
    enc_mid_g, norm_two, enc_low, enc_ctx_grad = order(
        norm_back, memory_grad, enc_mid, enc_parts, e_norm[1][0], enc_w[2]
    )
    enc_dq, enc_own_grad, enc_peer_grad = order(
        attend_back, enc_q, enc_own, enc_peer, enc_ctx_grad, enc_lse, same_t
    )
    enc_came = swap(enc_peer_grad, "seq", 1)
    e_feed.add(order)
    pair_low, part = order(attend_leave_joined, dq, own_grad, came, self_w[1], self_w[0])
    parts = (part, other_core(part))
    side_g = order(weight_grad_two, (self_in, dq), (low, self_ctx), x_first)
    pair_g = order(weight_grad_one, self_in, pair_low, y_first)
    self_s = Scatter(pair_g, side_g, factor).begin()
    d_feed.add(order)
    cross.add(order)
    side_g = order(weight_grad_two, (enc_in, enc_dq), (enc_low, enc_ctx), x_first)
    pair_low, part = order(
        attend_leave_joined, enc_dq, enc_own_grad, enc_came, enc_w[1], enc_w[0]
    )
    enc_parts = (part, other_core(part))
    pair_g = order(weight_grad_one, enc_in, pair_low, y_first)
    enc = Scatter(pair_g, side_g, factor).begin()
    e_feed.add(order)
    tgt_grad, norm_three = order(norm_back_last, mid_g, x_tgt, parts, d_norm[0][0])
    tgt_part = back_start(tgt_grad)
    self_s.add(order)
    src_grad, norm_one = order(norm_back_last, enc_mid_g, x_src, enc_parts, e_norm[0][0])
    src_part = back_start(src_grad)
    norm_grads = [norm_one, norm_two, norm_three, norm_four, norm_five]
    norm_rows = jnp.stack(
        [norm_grads[i][j] for i, j in ((0, 0), (1, 0), (0, 1), (1, 1))]
        + [norm_grads[i][j] for j in (0, 1) for i in (2, 3, 4)]
    ).astype(LOW)
    small = Scatter(*order(norm_halves, norm_rows, width), factor).begin()
    decoded = order(back_end, decoded, decoded_part)
    memory_grad = order(back_end, memory_grad, memory_part)
    cross.add(order)
    d_feed.add(order)
    enc.add(order)
    small.add(order)
    e_feed.add(order)
    self_s.add(order)
    cross.add(order)
    enc.add(order)
    small.add(order)
    tgt_grad = order(back_end, tgt_grad, tgt_part)
    self_s.add(order)
    e_feed.add(order)
    enc.add(order)
    small.add(order)
    src_grad = order(back_end, src_grad, src_part)
    self_s.add(order)
    enc.add(order)
    small.add(order)

    norm_out = small.out[0][:, :n_norms].T
    enc_qkv_g, enc_out_g = qkv_out(enc.out)
    self_qkv_g, self_out_g = qkv_out(self_s.out)
    cross_qkv_g, cross_out_g = qkv_out(cross.out)
    return (
        decoded,
        src_grad,
        tgt_grad,
        memory_grad,
        norm_out[:n_enc],
        norm_out[n_enc : 2 * n_enc],
        enc_qkv_g,
        enc_out_g,
        e_feed.out[0],
        e_feed.out[1].T,
        norm_out[2 * n_enc : 2 * n_enc + n_dec],
        norm_out[2 * n_enc + n_dec :],
        self_qkv_g,
        cross_qkv_g,
        jnp.stack([self_out_g, cross_out_g]),
        d_feed.out[0],
        d_feed.out[1].T,
    )


def solution(mesh):
    placed = (
        P("dp", "seq", None),
        P("dp", "seq", None),
        P("dp", "seq", None),
        P("dp", None),
        P("dp", None),
        P(None, ("dp", "seq")),
        P(None, ("dp", "seq")),
        P(None, ("dp", "seq"), "mp"),
        P("mp", ("dp", "seq")),
        P(("dp", "seq"), "mp"),
        P("mp", ("dp", "seq")),
        P(None, ("dp", "seq")),
        P(None, ("dp", "seq")),
        P(None, ("dp", "seq"), "mp"),
        P(None, ("dp", "seq"), "mp"),
        P(None, "mp", ("dp", "seq")),
        P(("dp", "seq"), "mp"),
        P("mp", ("dp", "seq")),
    )
    return jax.shard_map(
        per_device,
        mesh=mesh,
        in_specs=placed,
        out_specs=(
            P("dp", "seq", None),
            P("dp", "seq", None),
            P("dp", "seq", None),
            P("dp", "seq", None),
            P(None, ("dp", "seq")),
            P(None, ("dp", "seq")),
            P(None, ("dp", "seq"), "mp"),
            P("mp", ("dp", "seq")),
            P(("dp", "seq"), "mp"),
            P("mp", ("dp", "seq")),
            P(None, ("dp", "seq")),
            P(None, ("dp", "seq")),
            P(None, ("dp", "seq"), "mp"),
            P(None, ("dp", "seq"), "mp"),
            P(None, "mp", ("dp", "seq")),
            P(("dp", "seq"), "mp"),
            P("mp", ("dp", "seq")),
        ),
        check_vma=False,
    )
```

```python
import functools

import jax
import jax.numpy as jnp
from jax import lax
from jax.experimental import pallas as pl
from jax.experimental.pallas import tpu as pltpu
from jax.sharding import PartitionSpec as P

HEAD = 64
NSEG = 8
LANGS = 4
LANES = 128
TILE = 512
F32 = jnp.float32
LOW = jnp.bfloat16
EPS = 1e-05


def dot_nn(left, right):
    return jnp.dot(left, right, preferred_element_type=F32)


def dot_tn(left, right):
    return lax.dot_general(left, right, (((0,), (0,)), ((), ())), preferred_element_type=F32)


def dot_nt(left, right):
    return lax.dot_general(left, right, (((1,), (1,)), ((), ())), preferred_element_type=F32)


def xor_perm(size, bits):
    return [(i, i ^ bits) for i in range(size)]


def swap(value, axis, bits):
    return lax.ppermute(value, axis, xor_perm(lax.axis_size(axis), bits))


def pick(value, index, axis=0):
    return lax.dynamic_index_in_dim(value, index, axis, keepdims=False)


def params(mib):
    return pltpu.CompilerParams(vmem_limit_bytes=mib << 20)


def whole(shape):
    return pl.BlockSpec(shape, lambda *_: (0,) * len(shape))


def shaped(shape, dtype):
    return jax.ShapeDtypeStruct(shape, dtype)


def cost(flops, nbytes, exps=0):
    return pl.CostEstimate(flops=1, bytes_accessed=1, transcendentals=0)


class Order:
    def __init__(self):
        self.last = []

    def __call__(self, step, *values):
        leaves, tree = jax.tree.flatten(values)
        spots = [i for i, leaf in enumerate(leaves) if isinstance(leaf, jax.Array)]
        for i, leaf in zip(spots, after([leaves[i] for i in spots], self.last), strict=True):
            leaves[i] = leaf
        out = step(*jax.tree.unflatten(tree, leaves))
        self.last = jax.tree.leaves(out)
        return out

    def wait(self, *values):
        self.last = self.last + jax.tree.leaves(values)


def after(values, others):
    count = len(values)
    return list(lax.optimization_barrier((*values, *others))[:count])


def place(sources, order, cuts):
    flat, where_from = [], []
    for source in sources:
        if isinstance(source, tuple):
            where_from.append([(len(flat), None), (len(flat) + 1, None)])
            flat.extend(source)
        else:
            where_from.append([(len(flat), 0), (len(flat), 1)])
            flat.append(source)
    count = len(sources)
    rows, cols = flat[0].shape[-2:]
    each = order.shape[0] // count
    size = rows // each

    def body(order_ref, *refs):
        inputs = refs[: len(flat)]
        outs = refs[len(flat) : len(flat) + len(cuts)]
        held, in_sems, out_sems = refs[len(flat) + len(cuts) :]
        loads = []
        for j in range(count):
            for half in range(2):
                index, part = where_from[j][half]
                source = inputs[index] if part is None else inputs[index].at[part]
                loads.append(
                    pltpu.make_async_copy(source, held.at[half, j], in_sems.at[2 * j + half])
                )
                loads[-1].start()
        stores = []
        for j in range(count):
            for half in range(2):
                loads[2 * j + half].wait()
                for i in range(each):
                    spot = order_ref[j * each + i]
                    start = pl.multiple_of(spot * size, size)
                    for n, (side, first, width) in enumerate(cuts):
                        if side != half:
                            continue
                        stores.append(
                            pltpu.make_async_copy(
                                held.at[half, j, pl.ds(i * size, size), pl.ds(first, width)],
                                outs[n].at[pl.ds(start, size)],
                                out_sems.at[j * each + i, n],
                            )
                        )
                        stores[-1].start()
        for store in stores:
            store.wait()

    total = count * rows
    return pl.pallas_call(
        body,
        out_shape=[shaped((total, width), LOW) for _, _, width in cuts],
        in_specs=[pl.BlockSpec(memory_space=pltpu.SMEM)]
        + [pl.BlockSpec(memory_space=pl.ANY)] * len(flat),
        out_specs=[pl.BlockSpec(memory_space=pl.ANY)] * len(cuts),
        scratch_shapes=[
            pltpu.VMEM((2, count, rows, cols), LOW),
            pltpu.SemaphoreType.DMA((2 * count,)),
            pltpu.SemaphoreType.DMA((order.shape[0], len(cuts))),
        ],
        compiler_params=params(24),
        cost_estimate=cost(0, 8 * total * cols),
    )(order, *flat)


def seq_steps():
    steps, step = [], lax.axis_size("seq") // 2
    while step:
        steps.append(step)
        step //= 2
    return steps


def seq_order():
    spots = [0]
    for step in seq_steps():
        spots += [spot ^ step for spot in spots]
    return spots


class Gather:
    def __init__(self, shards, stepwise, others=()):
        self.plain = lax.axis_size("dp") != 4
        self.relative = stepwise
        shards = jnp.stack(shards)
        if others:
            (shards,) = after([shards], others)
        if stepwise:
            self.spots, self.column, self.steps = seq_order(), shards, seq_steps()
        else:
            self.spots = list(range(lax.axis_size("seq")))
            self.column = lax.all_gather(shards, "seq", axis=1, tiled=True)

    def along(self):
        self.came = swap(self.column, "seq", self.steps.pop(0))

    def join(self, order):
        self.column = order(
            lambda one, two: jnp.concatenate([one, two], axis=1), self.column, self.came
        )

    def across(self, others=()):
        self.near = []
        if self.plain:
            return
        (ready,) = after([self.column], others)
        self.near = [swap(ready, "dp", 1), swap(ready, "dp", 2)]

    def far(self, order):
        self.last = []
        if self.plain:
            return
        one, two = order(lambda x, y: (x[0], y[1]), *self.near)
        self.last = [swap(one, "dp", 2), swap(two, "dp", 1)]

    def place(self, order, cuts):
        spots = jnp.asarray(self.spots, jnp.int32)
        if self.relative:
            spots = spots ^ lax.axis_index("seq").astype(jnp.int32)
        sources = [self.column] if self.plain else [self.column, *self.near, tuple(self.last)]
        return order(place_weights, sources, spots, cuts)


def place_weights(sources, spots, cuts):
    spot = lax.axis_index("dp")
    if lax.axis_size("dp") != 4:
        cols = sources[0].shape[2]
        halves = place(sources, spots, [(0, 0, cols), (1, 0, cols)])
        halves = [lax.all_gather(half, "dp", axis=0, tiled=True) for half in halves]
        return [halves[side][:, first : first + width] for side, first, width in cuts]
    blocks = jnp.arange(4, dtype=jnp.int32) ^ spot.astype(jnp.int32)
    spots = (blocks[:, None] * spots.shape[0] + spots[None, :]).reshape(-1)
    return place(sources, spots, cuts)


def block_order(first):
    if lax.axis_size("dp") != 4:
        return jnp.arange(4, dtype=jnp.int32)
    spot = lax.axis_index("dp").astype(jnp.int32)
    return jnp.asarray([first, 3, 0, 3 - first], jnp.int32) ^ spot


def row_order(first, relative):
    if not relative:
        places = jnp.arange(lax.axis_size("seq"), dtype=jnp.int32)
        return jnp.concatenate([block_order(first), places])
    away = jnp.arange(lax.axis_size("seq"), dtype=jnp.int32)
    away = away ^ lax.axis_index("seq").astype(jnp.int32)
    turn, bits = jnp.zeros_like(away), seq_steps()
    for one, two in zip(bits, reversed(bits), strict=True):
        turn = turn + jnp.where((away & one) != 0, two, 0)
    return jnp.concatenate([block_order(first), turn])


def weight_grad(pairs, order, extra=None):
    tokens, width = pairs[0][0].shape
    size = width // 4
    cols = sum(right.shape[1] for _, right in pairs)
    cols += 0 if extra is None else extra.shape[1]
    n_seq = lax.axis_size("seq")
    near = lax.axis_size("dp") == 4
    unit = size // n_seq if near else size

    def body(order_ref, *refs):
        away, stay = refs[-2:]
        step = pl.program_id(0)
        parts = [
            dot_tn(refs[2 * j][...], refs[2 * j + 1][...]).astype(LOW) for j in range(len(pairs))
        ]
        if extra is not None:
            parts.append(refs[2 * len(pairs)][...])
        start = 0
        for part in parts:
            stop = start + part.shape[1]

            def put(out):
                for k in range(size // unit):
                    spot = order_ref[4 + k] if near else k
                    rows = pl.ds(pl.multiple_of(spot * unit, unit), unit)
                    out[rows, start:stop] = part[k * unit : (k + 1) * unit]

            pl.when(step < 2)(functools.partial(put, away))
            pl.when(step >= 2)(functools.partial(put, stay))
            start = stop

    specs, values = [], []
    for left, right in pairs:
        specs.append(pl.BlockSpec((tokens, size), lambda i, order: (0, order[i])))
        specs.append(pl.BlockSpec(right.shape, lambda i, order: (0, 0)))
        values += [left, right]
    if extra is not None:
        specs.append(pl.BlockSpec((size, extra.shape[1]), lambda i, order: (order[i], 0)))
        values.append(extra)
    return pl.pallas_call(
        body,
        grid_spec=pltpu.PrefetchScalarGridSpec(
            num_scalar_prefetch=1,
            grid=(4,),
            in_specs=specs,
            out_specs=[
                pl.BlockSpec((size, cols), lambda i, order: (jnp.minimum(i, 1), 0)),
                pl.BlockSpec((size, cols), lambda i, order: (jnp.maximum(i - 2, 0), 0)),
            ],
        ),
        out_shape=[shaped((2 * size, cols), LOW)] * 2,
        compiler_params=params(32),
        cost_estimate=cost(2 * tokens * width * cols, 4 * width * cols),
    )(order, *values)


class Scatter:
    def __init__(self, pair, side, factor, relative=True):
        self.relative = relative
        self.halves, self.factor, self.stage = (pair, side), factor, 0
        self.bits = (2, 1)
        self.plain = lax.axis_size("dp") != 4

    def begin(self, others=()):
        self.came = []
        if not self.plain:
            away = after([away for away, _ in self.halves], others)
            self.came = [swap(v, "dp", bit) for v, bit in zip(away, self.bits, strict=True)]

    def next(self, others=()):
        self.last = []
        if not self.plain:
            onward = after(self.onward, others)
            self.last = [
                swap(v, "dp", 3 - bit) for v, bit in zip(onward, self.bits, strict=True)
            ]

    def add(self, order):
        self.stage += 1
        if self.plain:
            if self.stage == 4:
                self.out = self.plain_sum()
            return
        (getattr(self, "add%d" % self.stage))(order)

    def add1(self, order):
        stays = [stay for _, stay in self.halves]

        def step(stays, came):
            size = stays[0].shape[0] // 2
            onward = [
                (stay[size:].astype(F32) + new[size:].astype(F32)).astype(LOW)
                for stay, new in zip(stays, came, strict=True)
            ]
            return onward

        self.onward = order(step, stays, self.came)

    def add2(self, order):
        stays = [stay for _, stay in self.halves]

        def sums(stays, came, last):
            size = stays[0].shape[0] // 2
            return [
                (stay[:size].astype(F32) + new[:size].astype(F32) + more.astype(F32)).astype(LOW)
                for stay, new, more in zip(stays, came, last, strict=True)
            ]

        def step(stays, came, last):
            size = stays[0].shape[0] // 2
            both = jnp.stack(
                [
                    stay[:size].astype(F32) + new[:size].astype(F32) + more.astype(F32)
                    for stay, new, more in zip(stays, came, last, strict=True)
                ]
            )
            size = size // 2
            return both[:, size:].astype(LOW), both[:, :size]

        if not self.relative:
            parts = order(sums, stays, self.came, self.last)
            self.parts = [
                lax.psum_scatter(part, "seq", scatter_dimension=0, tiled=True) for part in parts
            ]
            return
        away, self.kept = order(step, stays, self.came, self.last)
        self.came = swap(away, "seq", 1)

    def add3(self, order):
        if not self.relative:
            return

        def step(kept, came):
            both = kept + came.astype(F32)
            size = both.shape[1] // 2
            return both[:, size:].astype(LOW), both[:, :size]

        away, self.kept = order(step, self.kept, self.came)
        self.came = swap(away, "seq", 2)

    def add4(self, order):
        if not self.relative:
            self.out = order(
                lambda *parts: [part.astype(F32) * self.factor for part in parts], *self.parts
            )
            return
        self.out = order(
            lambda kept, came: (kept + came.astype(F32)) * self.factor, self.kept, self.came
        )

    def plain_sum(self):
        here, n_seq = lax.axis_index("seq"), lax.axis_size("seq")
        columns = []
        for away, stay in self.halves:
            grad = jnp.concatenate([away, stay], axis=0)
            columns.append(
                lax.psum_scatter(grad, "dp", scatter_dimension=0, tiled=True).astype(F32)
            )
        both = jnp.stack(columns)
        both = both.reshape(2, n_seq, -1, both.shape[-1])
        result = pick(both, here, 1)
        for k in range(1, n_seq):
            result = result + swap(pick(both, here ^ k, 1).astype(LOW), "seq", k).astype(F32)
        return result * self.factor


def trade_start(value):
    size = value.shape[0] // 2
    part = lax.dynamic_slice_in_dim(value, lax.axis_index("mp") * size, size, 0)
    return swap(part, "seq", 2)


def trade_end(part):
    rest = swap(part, "mp", 1)
    return jnp.where(
        lax.axis_index("mp") == 0,
        jnp.concatenate([part, rest], axis=0),
        jnp.concatenate([rest, part], axis=0),
    )


def pair_start(value, others):
    row = lax.axis_index("seq") // 2
    (sent,) = after([pick(value, 1 - row)], others)
    return trade_start(sent)


def pair_end(value, part):
    row = lax.axis_index("seq") // 2
    return jnp.concatenate([pick(value, row), trade_end(part)], axis=0)


def back_start(value):
    return trade_start(value[value.shape[0] // 2 :].astype(LOW))


def back_starts(*values):
    halves = [value[value.shape[0] // 2 :].astype(LOW) for value in values]
    core, size = lax.axis_index("mp"), halves[0].shape[0] // 2
    parts = [lax.dynamic_slice_in_dim(half, core * size, size, 0) for half in halves]
    return swap(jnp.stack(parts), "seq", 2)


def back_ends(values, part):
    rest = swap(part, "mp", 1)
    core, row = lax.axis_index("mp"), lax.axis_index("seq") // 2
    came = jnp.where(
        core == 0,
        jnp.concatenate([part, rest], axis=1),
        jnp.concatenate([rest, part], axis=1),
    )
    result = []
    for i, value in enumerate(values):
        kept, new = value[: value.shape[0] // 2], came[i].astype(value.dtype)
        result.append(jnp.where(row == 0, jnp.stack([kept, new]), jnp.stack([new, kept])))
    return result


def back_end(value, part):
    kept = value[: value.shape[0] // 2]
    came = trade_end(part).astype(value.dtype)
    row = lax.axis_index("seq") // 2
    return jnp.where(row == 0, jnp.stack([kept, came]), jnp.stack([came, kept]))


def norm_parts(values):
    center = values - jnp.mean(values, axis=-1, keepdims=True)
    scale = lax.rsqrt(jnp.mean(center * center, axis=-1, keepdims=True) + EPS)
    return center * scale, scale


def enter(inputs, parts, norm, weight):
    tokens, width = inputs.shape
    blocks = weight.shape[1] // TILE
    rows = [inputs, *parts] + ([] if norm is None else list(norm))
    keep = len(parts) > 0 and norm is not None

    def body(*refs):
        x_ref, part_refs = refs[0], refs[1 : 1 + len(parts)]
        norm_refs = refs[1 + len(parts) : len(rows)]
        w_ref = refs[len(rows)]
        outs = refs[len(rows) + 1 :]
        low_ref, out_ref = outs[0], outs[1]

        @pl.when(pl.program_id(0) == 0)
        def _():
            x = x_ref[...].astype(F32)
            if part_refs:
                x = x + (part_refs[0][...].astype(F32) + part_refs[1][...].astype(F32))
            if keep:
                outs[2][...] = x
            if norm_refs:
                x = norm_parts(x)[0] * norm_refs[0][...] + norm_refs[1][...]
            low_ref[...] = x.astype(LOW)

        out_ref[0] = dot_nn(low_ref[...], w_ref[...]).astype(LOW)

    result = pl.pallas_call(
        body,
        grid=(blocks,),
        in_specs=[whole(v.shape) for v in rows] + [pl.BlockSpec((width, TILE), lambda j: (0, j))],
        out_specs=[
            whole((tokens, width)),
            pl.BlockSpec((1, tokens, TILE), lambda j: (j, 0, 0)),
        ]
        + ([whole((tokens, width))] if keep else []),
        out_shape=[shaped((tokens, width), LOW), shaped((blocks, tokens, TILE), LOW)]
        + ([shaped((tokens, width), F32)] if keep else []),
        compiler_params=params(32),
        cost_estimate=cost(2 * tokens * width * weight.shape[1], 14 * tokens * width),
    )(*rows, weight)
    return tuple(result)


def attend_body(rows, q_ref, ko_ref, kp_ref, vo_ref, vp_ref, bias_ref, ctx_ref, lse_ref):
    tokens = q_ref.shape[0]
    lane = lax.broadcasted_iota(jnp.int32, (rows, LANES), 1)
    ko, kp, vo, vp = ko_ref[0], kp_ref[0], vo_ref[0], vp_ref[0]
    for r in range(0, tokens, rows):
        q = q_ref[r : r + rows] * jnp.asarray(HEAD**-0.5, LOW)
        ctx = stat = None
        for h in range(LANES // HEAD):
            mine = (lane // HEAD) == h
            qh = jnp.where(mine, q, jnp.zeros_like(q))
            so = dot_nt(qh, ko) + bias_ref[r : r + rows, :tokens]
            sp = dot_nt(qh, kp) + bias_ref[r : r + rows, tokens:]
            top = jnp.maximum(
                jnp.max(so, axis=1, keepdims=True), jnp.max(sp, axis=1, keepdims=True)
            )
            eo, ep = jnp.exp(so - top), jnp.exp(sp - top)
            total = jnp.sum(eo, axis=1, keepdims=True) + jnp.sum(ep, axis=1, keepdims=True)
            acc = dot_nn(eo.astype(LOW), vo) + dot_nn(ep.astype(LOW), vp)
            acc = acc * (1.0 / total)
            lse = jnp.broadcast_to(top + jnp.log(total), (rows, LANES))
            ctx = acc if ctx is None else jnp.where(mine, acc, ctx)
            stat = lse if stat is None else jnp.where(mine, lse, stat)
        ctx_ref[r : r + rows] = ctx.astype(LOW)
        lse_ref[r : r + rows] = stat


def kv_spec(tokens, half):
    return pl.BlockSpec((1, tokens, LANES), lambda i: (half, 0, i))


def attend(query, own, peer, bias):
    tokens, width = query.shape
    spec = pl.BlockSpec((tokens, LANES), lambda i: (0, i))
    return pl.pallas_call(
        functools.partial(attend_body, 256),
        grid=(width // LANES,),
        in_specs=[spec]
        + [kv_spec(tokens, half) for half in (0, 0, 1, 1)]
        + [whole(bias.shape)],
        out_specs=[spec, spec],
        out_shape=[shaped((tokens, width), LOW), shaped((tokens, width), F32)],
        compiler_params=params(40),
        cost_estimate=cost(16 * tokens * tokens * width, 16 * tokens * width, 2 * tokens * tokens * 8),
    )(query, own, peer, own, peer, bias)


def attend_back_body(
    q_ref, ko_ref, kp_ref, vo_ref, vp_ref, g_ref, lse_ref, bias_ref, dq_ref, own_ref, peer_ref, acc
):
    tokens = q_ref.shape[0]
    lane = lax.broadcasted_iota(jnp.int32, (tokens, LANES), 1)
    q = q_ref[...] * jnp.asarray(HEAD**-0.5, LOW)
    g = g_ref[...]
    lse_t = lse_ref[...].T
    parts = ((kp_ref, vp_ref, peer_ref, tokens), (ko_ref, vo_ref, own_ref, 0))
    keys_t = [k_ref[0].T for k_ref, _, _, _ in parts]
    for h in range(LANES // HEAD):
        mine = (lane // HEAD) == h
        qh = jnp.where(mine, q, jnp.zeros_like(q))
        gh = jnp.where(mine, g, jnp.zeros_like(g))
        rows = slice(h * HEAD, (h + 1) * HEAD)
        lse = lse_t[h * HEAD : h * HEAD + 1]
        probs, inner = [], []
        for k_ref, v_ref, _, base in parts:
            scores = dot_nt(k_ref[0], qh) + bias_ref[base : base + tokens]
            probs.append(jnp.exp(scores - lse))
            inner.append(dot_nt(v_ref[0], gh))
        delta = sum(jnp.sum(p * d, axis=0, keepdims=True) for p, d in zip(probs, inner))
        total = None
        for j, (_, _, out_ref, _) in enumerate(parts):
            grads = (probs[j] * (inner[j] - delta)).astype(LOW)
            dv = dot_nn(probs[j].astype(LOW), gh).astype(LOW)
            dk = dot_nn(grads, qh).astype(LOW)
            part = dot_nn(keys_t[j][rows], grads)
            total = part if total is None else total + part
            if h == 0:
                out_ref[0], out_ref[1] = dk, dv
            else:
                out_ref[0] += dk
                out_ref[1] += dv
        acc[rows] = total
    dq_ref[...] = (acc[...].T * HEAD**-0.5).astype(LOW)


def attend_back(query, own, peer, grad, lse, bias_t):
    tokens, width = query.shape
    spec = pl.BlockSpec((tokens, LANES), lambda i: (0, i))
    both = pl.BlockSpec((2, tokens, LANES), lambda i: (0, 0, i))
    return pl.pallas_call(
        attend_back_body,
        grid=(width // LANES,),
        in_specs=[spec]
        + [kv_spec(tokens, half) for half in (0, 0, 1, 1)]
        + [spec, spec, whole(bias_t.shape)],
        out_specs=[spec, both, both],
        out_shape=[shaped((tokens, width), LOW)] + [shaped((2, tokens, width), LOW)] * 2,
        scratch_shapes=[pltpu.VMEM((LANES, tokens), F32)],
        compiler_params=params(40),
        cost_estimate=cost(40 * tokens * tokens * width, 24 * tokens * width, 2 * tokens * tokens * 8),
    )(query, own, peer, own, peer, grad, lse, bias_t)


def attend_leave(dq, own, came, wq, wkv, apart):
    tokens, width = dq.shape[0], wq.shape[0]
    size = tokens // 2

    def body(dq_ref, own_ref, came_ref, wq_ref, wkv_ref, pair_ref, *outs):
        low = [
            (own_ref[j].astype(F32) + came_ref[j].astype(F32)).astype(LOW) for j in range(2)
        ]
        cols = low[0].shape[1]
        for j in range(2):
            pair_ref[:, j * cols : (j + 1) * cols] = low[j]
        first = dot_nt(dq_ref[...], wq_ref[...])
        rest = dot_nt(pair_ref[...], wkv_ref[...])
        if apart:
            outs[0][0] = first.astype(LOW)
            outs[0][1] = rest.astype(LOW)
        else:
            outs[0][...] = (first + rest).astype(LOW)

    part_spec = (
        pl.BlockSpec((2, size, width), lambda i: (0, i, 0))
        if apart
        else pl.BlockSpec((size, width), lambda i: (i, 0))
    )
    cols = own.shape[2]
    return pl.pallas_call(
        body,
        grid=(2,),
        in_specs=[
            pl.BlockSpec((size, cols), lambda i: (i, 0)),
            pl.BlockSpec((2, size, cols), lambda i: (0, i, 0)),
            pl.BlockSpec((2, size, cols), lambda i: (0, i, 0)),
            whole(wq.shape),
            whole(wkv.shape),
        ],
        out_specs=[pl.BlockSpec((size, 2 * cols), lambda i: (i, 0)), part_spec],
        out_shape=[
            shaped((tokens, 2 * cols), LOW),
            shaped((2, tokens, width) if apart else (tokens, width), LOW),
        ],
        compiler_params=params(32),
        cost_estimate=cost(6 * tokens * width * cols, 14 * tokens * cols + 6 * width * cols),
    )(dq, own, came, wq, wkv)


def feed(inputs, parts, norm, up, down):
    tokens, width = inputs.shape
    hidden = up.shape[1]

    def body(x_ref, one_ref, two_ref, gain_ref, bias_ref, up_ref, down_ref, *rest):
        normed_ref, total_ref, act_ref, slope_ref, part_ref, acc = rest
        step = pl.program_id(0)

        @pl.when(step == 0)
        def _():
            x = x_ref[...].astype(F32) + (one_ref[...].astype(F32) + two_ref[...].astype(F32))
            total_ref[...] = x
            normed_ref[...] = (norm_parts(x)[0] * gain_ref[...] + bias_ref[...]).astype(LOW)

        pre = dot_nn(normed_ref[...], up_ref[...])
        below = 0.5 + 0.5 * lax.erf(pre * (0.5**0.5))
        act = (pre * below).astype(LOW)
        act_ref[...] = act
        slope = below + pre * (jnp.exp(pre * pre * -0.5) * 0.3989422804014327)
        slope_ref[...] = slope.astype(LOW)
        part = dot_nt(act, down_ref[...])

        @pl.when(step == 0)
        def _():
            acc[...] = part

        @pl.when(step > 0)
        def _():
            acc[...] += part

        @pl.when(step == pl.num_programs(0) - 1)
        def _():
            part_ref[...] = acc[...].astype(LOW)

    block = pl.BlockSpec((tokens, TILE), lambda j: (0, j))
    weight = pl.BlockSpec((width, TILE), lambda j: (0, j))
    same = whole((tokens, width))
    return pl.pallas_call(
        body,
        grid=(hidden // TILE,),
        in_specs=[same, same, same, whole((1, width)), whole((1, width)), weight, weight],
        out_specs=[same, same, block, block, same],
        out_shape=[
            shaped((tokens, width), LOW),
            shaped((tokens, width), F32),
            shaped((tokens, hidden), LOW),
            shaped((tokens, hidden), LOW),
            shaped((tokens, width), LOW),
        ],
        scratch_shapes=[pltpu.VMEM((tokens, width), F32)],
        compiler_params=params(48),
        cost_estimate=cost(4 * tokens * width * hidden, 8 * width * hidden, 2 * tokens * hidden),
    )(inputs, *parts, *norm, up, down)


def feed_back(low, slope, up, down):
    tokens, width = low.shape
    hidden = up.shape[1]

    def body(low_ref, slope_ref, up_ref, down_ref, pre_ref, part_ref, acc):
        step = pl.program_id(0)
        act_grad = dot_nn(low_ref[...], down_ref[...])
        pre = (act_grad * slope_ref[...].astype(F32)).astype(LOW)
        pre_ref[...] = pre
        part = dot_nt(pre, up_ref[...])

        @pl.when(step == 0)
        def _():
            acc[...] = part

        @pl.when(step > 0)
        def _():
            acc[...] += part

        @pl.when(step == pl.num_programs(0) - 1)
        def _():
            part_ref[...] = acc[...].astype(LOW)

    block = pl.BlockSpec((tokens, TILE), lambda j: (0, j))
    weight = pl.BlockSpec((width, TILE), lambda j: (0, j))
    same = whole((tokens, width))
    return pl.pallas_call(
        body,
        grid=(hidden // TILE,),
        in_specs=[same, block, weight, weight],
        out_specs=[block, same],
        out_shape=[shaped((tokens, hidden), LOW), shaped((tokens, width), LOW)],
        scratch_shapes=[pltpu.VMEM((tokens, width), F32)],
        compiler_params=params(48),
        cost_estimate=cost(4 * tokens * width * hidden, 6 * width * hidden),
    )(low, slope, up, down)


def norm_back(grad, values, parts, gain, weight):
    tokens, width = grad.shape
    size = tokens // 2

    def body(*refs):
        g_ref, x_ref, one_ref, two_ref, gain_ref = refs[:5]
        outs = refs[5:] if weight is None else refs[6:]
        step = pl.program_id(0)
        normed_grad = one_ref[...].astype(F32) + two_ref[...].astype(F32)
        unit, scale = norm_parts(x_ref[...].astype(F32))
        gains = jnp.sum(normed_grad * unit, axis=0, keepdims=True)
        biases = jnp.sum(normed_grad, axis=0, keepdims=True)
        inner = normed_grad * gain_ref[...]
        inner = inner - jnp.mean(inner, axis=-1, keepdims=True) - unit * jnp.mean(
            inner * unit, axis=-1, keepdims=True
        )
        total = g_ref[...] + inner * scale
        outs[0][...] = total

        @pl.when(step == 0)
        def _():
            outs[1][...] = jnp.concatenate([gains, biases], axis=0)

        @pl.when(step > 0)
        def _():
            outs[1][...] += jnp.concatenate([gains, biases], axis=0)

        if weight is not None:
            low = total.astype(LOW)
            outs[2][...] = low
            outs[3][...] = dot_nn(low, refs[5][...]).astype(LOW)

    row = pl.BlockSpec((size, width), lambda i: (i, 0))
    in_specs = [row] * 4 + [whole((1, width))]
    out_specs = [row, whole((2, width))]
    out_shape = [shaped((tokens, width), F32), shaped((2, width), F32)]
    extra = []
    if weight is not None:
        cols = weight.shape[1]
        extra = [weight]
        in_specs.append(whole(weight.shape))
        out_specs += [row, pl.BlockSpec((size, cols), lambda i: (i, 0))]
        out_shape += [shaped((tokens, width), LOW), shaped((tokens, cols), LOW)]
    return pl.pallas_call(
        body,
        grid=(tokens // size,),
        in_specs=in_specs,
        out_specs=out_specs,
        out_shape=out_shape,
        compiler_params=params(40),
        cost_estimate=cost(20 * tokens * width, 20 * tokens * width),
    )(grad, values, *parts, gain, *extra)


def weight_grad_one(left, right, order, extra=None):
    return weight_grad([(left, right)], order, extra)


def weight_grad_two(one, two, order, extra=None):
    return weight_grad([one, two], order, extra)


def attend_leave_apart(dq, own, came, wq, wkv):
    return attend_leave(dq, own, came, wq, wkv, True)


def attend_leave_joined(dq, own, came, wq, wkv):
    return attend_leave(dq, own, came, wq, wkv, False)


def norm_back_last(grad, values, parts, gain):
    return norm_back(grad, values, parts, gain, None)


def low_too(value):
    return value, value.astype(LOW)


def norm_columns(*norm_rows):
    rows = jnp.concatenate(norm_rows, axis=0).astype(LOW)
    return jnp.pad(rows.T, ((0, 0), (0, LANES - rows.shape[0])))


def token_counts(lengths, groups):
    onehot = (groups[:, :, None] == jnp.arange(LANGS, dtype=jnp.int32)).astype(F32)
    counts = jnp.sum(onehot * lengths[:, :, None].astype(F32), axis=(0, 1))
    if lax.axis_size("dp") != 4:
        counts = lax.psum(counts, "dp")
        return counts, counts
    counts = jnp.pad(counts[None], ((0, 7), (0, LANES - LANGS)))
    counts = counts + swap(counts, "dp", 1)
    came = swap(counts, "dp", 2)
    return (counts + came)[0, :LANGS], came


def token_tables(lengths, groups, counts, full_len, quarter):
    here, row = lax.axis_index("seq"), lax.axis_index("seq") // 2
    rows = lengths.shape[0]
    onehot = (groups[:, :, None] == jnp.arange(LANGS, dtype=jnp.int32)).astype(F32)
    all_tokens = rows * lax.axis_size("dp") * full_len
    seg_weight = all_tokens / (LANGS * jnp.sum(onehot * counts, axis=2))
    ends = pick(jnp.cumsum(lengths, axis=1), row)
    steps = jnp.arange(quarter, dtype=jnp.int32)
    places = jnp.concatenate([(here ^ k) * quarter + steps for k in (0, 2, 1, 3)])
    segs = jnp.sum((ends[None, :] <= places[:, None]).astype(jnp.int32), axis=1)
    mine = 2 * quarter
    same = segs[:mine, None] == segs[None, :]
    causal = same & (places[None, :] <= places[:mine, None])
    same_t = segs[:, None] == segs[None, :mine]
    causal_t = same_t & (places[:, None] <= places[None, :mine])
    offsets = [jnp.where(mask, 0.0, -1e30).astype(F32) for mask in (same, same_t, causal, causal_t)]
    match = (segs[:mine, None] == jnp.arange(NSEG, dtype=jnp.int32)).astype(F32)
    tok_weight = jnp.sum(match * pick(seg_weight, row)[None, :], axis=1)
    return offsets, tok_weight, all_tokens


def attn_shard(qkv, out):
    pair = jnp.concatenate([qkv[1], qkv[2]], axis=1)
    side = jnp.concatenate([qkv[0], out.T], axis=1)
    return [pair, side]


def qkv_out(both):
    pair, side = both[0], both[1]
    width = side.shape[1] // 2
    qkv = jnp.stack([side[:, :width], pair[:, :width], pair[:, width:]])
    return qkv, side[:, width:].T


def project(left, right):
    return dot_nn(left, right).astype(LOW)


def project_out(ctx, wo):
    return dot_nt(ctx, wo).astype(LOW)


def other_core(part):
    return swap(part, "mp", 1)


def per_device(
    src,
    tgt,
    cotangent,
    lengths,
    groups,
    enc_gains,
    enc_biases,
    enc_qkv,
    enc_out,
    enc_up,
    enc_down,
    dec_gains,
    dec_biases,
    dec_self_qkv,
    dec_cross_qkv,
    dec_outs,
    dec_up,
    dec_down,
):
    rows, quarter, width = src.shape
    full_len = quarter * lax.axis_size("seq")
    n_enc, n_dec = enc_gains.shape[0], dec_gains.shape[0]
    half, hidden = enc_qkv.shape[2], enc_up.shape[1]
    order = Order()

    norms = jnp.concatenate([enc_gains, enc_biases, dec_gains, dec_biases], axis=0)
    n_norms = norms.shape[0]
    extra = jnp.pad(norms.T, ((0, 0), (0, LANES - n_norms)))
    enc_pair, enc_side = attn_shard(enc_qkv, enc_out)
    shards = [
        [jnp.concatenate([v, extra], axis=1) for v in (enc_pair, enc_side)],
        [
            jnp.concatenate(attn_shard(dec_self_qkv, dec_outs[0]), axis=1),
            jnp.concatenate(attn_shard(dec_cross_qkv, dec_outs[1]), axis=1),
        ],
        [enc_up, enc_down.T],
        [dec_up, dec_down.T],
    ]
    attn_cuts = [(0, 0, 2 * half), (1, 0, half), (1, half, half)]
    both_cuts = [
        (j, first, wide)
        for j in range(2)
        for first, wide in ((0, 2 * half), (2 * half, half), (3 * half, half))
    ]
    feed_cuts = [(0, 0, hidden), (1, 0, hidden)]
    counts, counted = token_counts(lengths, groups)
    one = Gather(shards[0], True)
    one.along()
    two, three, four = [Gather(shard, False, [one.came]) for shard in shards[1:]]
    one.join(order)
    one.along()
    one.join(order)
    one.across([counted])
    src_part = pair_start(src, [one.column])
    y_first, x_first = order(lambda: (row_order(2, True), row_order(1, True)))
    one.far(order)
    offsets, tok_weight, all_tokens = order(
        token_tables, lengths, groups, counts, full_len, quarter
    )
    same, same_t, causal, causal_t = offsets
    factor = 1.0 / all_tokens
    two.across(one.last)
    *enc_w, table = one.place(order, attn_cuts + [(0, 2 * half, LANES)])
    table = table[:, :n_norms].T.astype(F32)[:, None]
    e_norm = [(table[i], table[n_enc + i]) for i in range(n_enc)]
    d_norm = [(table[2 * n_enc + i], table[2 * n_enc + n_dec + i]) for i in range(n_dec)]
    x_src = order(pair_end, src, src_part)
    enc_in, enc_own = order(enter, x_src, (), e_norm[0], enc_w[0])
    enc_peer = swap(enc_own, "seq", 1)
    enc_q = order(project, enc_in, enc_w[1])
    tgt_part = pair_start(tgt, [enc_q])
    two.far(order)
    three.across(two.last)
    enc_ctx, enc_lse = order(attend, enc_q, enc_own, enc_peer, same)
    enc_part = order(project_out, enc_ctx, enc_w[2])
    enc_other = other_core(enc_part)
    x_tgt = order(pair_end, tgt, tgt_part)
    weights = two.place(order, both_cuts)
    self_w, cross_w = weights[:3], weights[3:]
    self_in, self_own = order(enter, x_tgt, (), d_norm[0], self_w[0])
    self_peer = swap(self_own, "seq", 1)
    self_q = order(project, self_in, self_w[1])
    cot_part = pair_start(cotangent, [self_q])
    three.far(order)
    four.across(three.last)
    self_ctx, self_lse = order(attend, self_q, self_own, self_peer, causal)
    self_part = order(project_out, self_ctx, self_w[2])
    self_other = other_core(self_part)
    cot = order(pair_end, cotangent, cot_part)
    out_grad, out_low = order(
        lambda cot, weight: low_too(cot.astype(F32) * weight[:, None]), cot, tok_weight
    )
    e_up, e_down = three.place(order, feed_cuts)
    enc_normed, enc_mid, enc_act, enc_slope, mem_part = order(
        feed, x_src, (enc_part, enc_other), e_norm[1], e_up, e_down
    )
    mem_other = other_core(mem_part)
    source, cross_own = order(enter, enc_mid, (mem_part, mem_other), None, cross_w[0])
    cross_peer = swap(cross_own, "seq", 1)
    cross_in, cross_q, dec_mid = order(
        enter, x_tgt, (self_part, self_other), d_norm[1], cross_w[1]
    )
    cross_q = cross_q[0]
    four.far(order)
    cross_ctx, cross_lse = order(attend, cross_q, cross_own, cross_peer, same)
    cross_part = order(project_out, cross_ctx, cross_w[2])
    cross_other = other_core(cross_part)
    d_up, d_down = four.place(order, feed_cuts)
    dec_normed, dec_cross, dec_act, dec_slope, dec_part = order(
        feed, dec_mid, (cross_part, cross_other), d_norm[2], d_up, d_down
    )
    dec_other = other_core(dec_part)

    pre_grad, part = order(feed_back, out_low, dec_slope, d_up, d_down)
    parts = (part, other_core(part))
    down_g = order(weight_grad_one, out_low, dec_act, x_first)
    up_g = order(weight_grad_one, dec_normed, pre_grad, y_first)
    d_feed = Scatter(up_g, down_g, factor)
    d_feed.begin()
    cross_g, norm_five, low, ctx_grad = order(
        norm_back, out_grad, dec_cross, parts, d_norm[2][0], cross_w[2]
    )
    dq, own_grad, peer_grad = order(
        attend_back, cross_q, cross_own, cross_peer, ctx_grad, cross_lse, same_t
    )
    came = swap(peer_grad, "seq", 1)
    side_g = order(weight_grad_two, (cross_in, dq), (low, cross_ctx), x_first)
    decoded = order(
        lambda total, one, two: (total + (one.astype(F32) + two.astype(F32))).astype(LOW),
        dec_cross,
        dec_part,
        dec_other,
    )
    pair_low, part = order(attend_leave_apart, dq, own_grad, came, cross_w[1], cross_w[0])
    other = other_core(part)
    pair_g = order(weight_grad_one, source, pair_low, y_first)
    cross = Scatter(pair_g, side_g, factor)
    cross.begin(d_feed.came)
    d_feed.add(order)
    memory_grad, memory_low = order(
        lambda one, two: low_too(one[1].astype(F32) + two[1].astype(F32)), part, other
    )
    cross_parts = (part[0], other[0])
    pre_grad, enc_part = order(feed_back, memory_low, enc_slope, e_up, e_down)
    enc_parts = (enc_part, other_core(enc_part))
    down_g = order(weight_grad_one, memory_low, enc_act, x_first)
    d_feed.next(cross.came)
    cross.add(order)
    up_g = order(weight_grad_one, enc_normed, pre_grad, y_first)
    e_feed = Scatter(up_g, down_g, factor)
    e_feed.begin(d_feed.last)
    order.wait(d_feed.last)
    mid_g, norm_four, low, ctx_grad = order(
        norm_back, cross_g, dec_mid, cross_parts, d_norm[1][0], self_w[2]
    )
    dq, own_grad, peer_grad = order(
        attend_back, self_q, self_own, self_peer, ctx_grad, self_lse, causal_t
    )
    came = swap(peer_grad, "seq", 1)
    d_feed.add(order)
    cross.next(e_feed.came)
    enc_mid_g, norm_two, enc_low, enc_ctx_grad = order(
        norm_back, memory_grad, enc_mid, enc_parts, e_norm[1][0], enc_w[2]
    )
    enc_dq, enc_own_grad, enc_peer_grad = order(
        attend_back, enc_q, enc_own, enc_peer, enc_ctx_grad, enc_lse, same_t
    )
    enc_came = swap(enc_peer_grad, "seq", 1)
    e_feed.add(order)
    pair_low, part = order(attend_leave_joined, dq, own_grad, came, self_w[1], self_w[0])
    parts = (part, other_core(part))
    d_feed.add(order)
    side_g = order(weight_grad_two, (self_in, dq), (low, self_ctx), x_first)
    pair_g = order(weight_grad_one, self_in, pair_low, y_first)
    self_s = Scatter(pair_g, side_g, factor)
    e_feed.next(cross.last)
    cross.add(order)
    tgt_grad, norm_three = order(norm_back_last, mid_g, x_tgt, parts, d_norm[0][0])
    pair_low, part = order(
        attend_leave_joined, enc_dq, enc_own_grad, enc_came, enc_w[1], enc_w[0]
    )
    enc_parts = (part, other_core(part))
    d_feed.add(order)
    self_s.begin(e_feed.last)
    e_feed.add(order)
    src_grad, norm_one = order(norm_back_last, enc_mid_g, x_src, enc_parts, e_norm[0][0])
    columns = order(norm_columns, norm_one, norm_two, norm_three, norm_four, norm_five)
    side_g = order(weight_grad_two, (enc_in, enc_dq), (enc_low, enc_ctx), x_first, columns)
    pair_g = order(weight_grad_one, enc_in, pair_low, y_first, columns)
    enc = Scatter(pair_g, side_g, factor)
    cross.add(order)
    enc.begin(self_s.came)
    self_s.add(order)
    e_feed.add(order)
    self_s.next(enc.came)
    enc.add(order)
    enc.next(self_s.last)
    cross.add(order)
    self_s.add(order)
    e_feed.add(order)
    enc.add(order)
    src_part = back_start(src_grad)
    three_part = back_starts(decoded, memory_low, tgt_grad)
    self_s.add(order)
    enc.add(order)
    src_grad = order(back_end, src_grad, src_part)
    decoded, memory_grad, tgt_grad = order(
        back_ends, (decoded, memory_grad, tgt_grad), three_part
    )
    self_s.add(order)
    enc.add(order)

    norm_out = enc.out[0][:, 2 * half : 2 * half + n_norms].T
    rows_of = [2 * j + i for i in range(2) for j in range(n_enc)]
    rows_of += [2 * (n_enc + j) + i for i in range(2) for j in range(n_dec)]
    norm_out = jnp.stack([norm_out[i] for i in rows_of])
    enc_qkv_g, enc_out_g = qkv_out([part[:, : 2 * half] for part in enc.out])
    self_qkv_g, self_out_g = qkv_out(self_s.out)
    cross_qkv_g, cross_out_g = qkv_out(cross.out)
    return (
        decoded,
        src_grad,
        tgt_grad,
        memory_grad,
        norm_out[:n_enc],
        norm_out[n_enc : 2 * n_enc],
        enc_qkv_g,
        enc_out_g,
        e_feed.out[0],
        e_feed.out[1].T,
        norm_out[2 * n_enc : 2 * n_enc + n_dec],
        norm_out[2 * n_enc + n_dec :],
        self_qkv_g,
        cross_qkv_g,
        jnp.stack([self_out_g, cross_out_g]),
        d_feed.out[0],
        d_feed.out[1].T,
    )


def solution(mesh):
    placed = (
        P("dp", "seq", None),
        P("dp", "seq", None),
        P("dp", "seq", None),
        P("dp", None),
        P("dp", None),
        P(None, ("dp", "seq")),
        P(None, ("dp", "seq")),
        P(None, ("dp", "seq"), "mp"),
        P("mp", ("dp", "seq")),
        P(("dp", "seq"), "mp"),
        P("mp", ("dp", "seq")),
        P(None, ("dp", "seq")),
        P(None, ("dp", "seq")),
        P(None, ("dp", "seq"), "mp"),
        P(None, ("dp", "seq"), "mp"),
        P(None, "mp", ("dp", "seq")),
        P(("dp", "seq"), "mp"),
        P("mp", ("dp", "seq")),
    )
    return jax.shard_map(
        per_device,
        mesh=mesh,
        in_specs=placed,
        out_specs=(
            P("dp", "seq", None),
            P("dp", "seq", None),
            P("dp", "seq", None),
            P("dp", "seq", None),
            P(None, ("dp", "seq")),
            P(None, ("dp", "seq")),
            P(None, ("dp", "seq"), "mp"),
            P("mp", ("dp", "seq")),
            P(("dp", "seq"), "mp"),
            P("mp", ("dp", "seq")),
            P(None, ("dp", "seq")),
            P(None, ("dp", "seq")),
            P(None, ("dp", "seq"), "mp"),
            P(None, ("dp", "seq"), "mp"),
            P(None, "mp", ("dp", "seq")),
            P(("dp", "seq"), "mp"),
            P("mp", ("dp", "seq")),
        ),
        check_vma=False,
    )
```

```python
import functools

import jax
import jax.numpy as jnp
from jax import lax
from jax.experimental import pallas as pl
from jax.experimental.pallas import tpu as pltpu
from jax.sharding import PartitionSpec as P

HEAD = 64
NSEG = 8
LANGS = 4
LANES = 128
TILE = 512
F32 = jnp.float32
LOW = jnp.bfloat16
EPS = 1e-05


def dot_nn(left, right):
    return jnp.dot(left, right, preferred_element_type=F32)


def dot_tn(left, right):
    return lax.dot_general(left, right, (((0,), (0,)), ((), ())), preferred_element_type=F32)


def dot_nt(left, right):
    return lax.dot_general(left, right, (((1,), (1,)), ((), ())), preferred_element_type=F32)


def xor_perm(size, bits):
    return [(i, i ^ bits) for i in range(size)]


def swap(value, axis, bits):
    return lax.ppermute(value, axis, xor_perm(lax.axis_size(axis), bits))


def pick(value, index, axis=0):
    return lax.dynamic_index_in_dim(value, index, axis, keepdims=False)


def params(mib):
    return pltpu.CompilerParams(vmem_limit_bytes=mib << 20)


def whole(shape):
    return pl.BlockSpec(shape, lambda *_: (0,) * len(shape))


def shaped(shape, dtype):
    return jax.ShapeDtypeStruct(shape, dtype)


def cost(flops, nbytes, exps=0):
    return pl.CostEstimate(flops=1, bytes_accessed=1, transcendentals=0)


class Order:
    def __init__(self):
        self.last = []

    def __call__(self, step, *values):
        leaves, tree = jax.tree.flatten(values)
        spots = [i for i, leaf in enumerate(leaves) if isinstance(leaf, jax.Array)]
        for i, leaf in zip(spots, after([leaves[i] for i in spots], self.last), strict=True):
            leaves[i] = leaf
        out = step(*jax.tree.unflatten(tree, leaves))
        self.last = jax.tree.leaves(out)
        return out

    def wait(self, *values):
        self.last = self.last + jax.tree.leaves(values)


def after(values, others):
    count = len(values)
    return list(lax.optimization_barrier((*values, *others))[:count])


def place(sources, order, cuts):
    flat, where_from = [], []
    for source in sources:
        if isinstance(source, tuple):
            where_from.append([(len(flat), None), (len(flat) + 1, None)])
            flat.extend(source)
        else:
            where_from.append([(len(flat), 0), (len(flat), 1)])
            flat.append(source)
    count = len(sources)
    rows, cols = flat[0].shape[-2:]
    each = order.shape[0] // count
    size = rows // each

    def body(order_ref, *refs):
        inputs = refs[: len(flat)]
        outs = refs[len(flat) : len(flat) + len(cuts)]
        held, in_sems, out_sems = refs[len(flat) + len(cuts) :]
        loads = []
        for j in range(count):
            for half in range(2):
                index, part = where_from[j][half]
                source = inputs[index] if part is None else inputs[index].at[part]
                loads.append(
                    pltpu.make_async_copy(source, held.at[half, j], in_sems.at[2 * j + half])
                )
                loads[-1].start()
        stores = []
        for j in range(count):
            for half in range(2):
                loads[2 * j + half].wait()
                for i in range(each):
                    spot = order_ref[j * each + i]
                    start = pl.multiple_of(spot * size, size)
                    for n, (side, first, width) in enumerate(cuts):
                        if side != half:
                            continue
                        stores.append(
                            pltpu.make_async_copy(
                                held.at[half, j, pl.ds(i * size, size), pl.ds(first, width)],
                                outs[n].at[pl.ds(start, size)],
                                out_sems.at[j * each + i, n],
                            )
                        )
                        stores[-1].start()
        for store in stores:
            store.wait()

    total = count * rows
    return pl.pallas_call(
        body,
        out_shape=[shaped((total, width), LOW) for _, _, width in cuts],
        in_specs=[pl.BlockSpec(memory_space=pltpu.SMEM)]
        + [pl.BlockSpec(memory_space=pl.ANY)] * len(flat),
        out_specs=[pl.BlockSpec(memory_space=pl.ANY)] * len(cuts),
        scratch_shapes=[
            pltpu.VMEM((2, count, rows, cols), LOW),
            pltpu.SemaphoreType.DMA((2 * count,)),
            pltpu.SemaphoreType.DMA((order.shape[0], len(cuts))),
        ],
        compiler_params=params(24),
        cost_estimate=cost(0, 8 * total * cols),
    )(order, *flat)


def seq_steps():
    steps, step = [], lax.axis_size("seq") // 2
    while step:
        steps.append(step)
        step //= 2
    return steps


def seq_order():
    spots = [0]
    for step in seq_steps():
        spots += [spot ^ step for spot in spots]
    return spots


class Gather:
    def __init__(self, shards, stepwise, others=()):
        self.plain = lax.axis_size("dp") != 4
        self.relative = stepwise
        shards = jnp.stack(shards)
        if others:
            (shards,) = after([shards], others)
        if stepwise:
            self.spots, self.column, self.steps = seq_order(), shards, seq_steps()
        else:
            self.spots = list(range(lax.axis_size("seq")))
            self.column = lax.all_gather(shards, "seq", axis=1, tiled=True)

    def along(self, others=()):
        (ready,) = after([self.column], others)
        self.came = swap(ready, "seq", self.steps.pop(0))

    def join(self, order):
        self.column = order(
            lambda one, two: jnp.concatenate([one, two], axis=1), self.column, self.came
        )

    def across(self, others=()):
        self.near = []
        if self.plain:
            return
        (ready,) = after([self.column], others)
        self.near = [swap(ready, "dp", 1), swap(ready, "dp", 2)]

    def far(self, order):
        self.last = []
        if self.plain:
            return
        one, two = order(lambda x, y: (x[0], y[1]), *self.near)
        self.last = [swap(one, "dp", 2), swap(two, "dp", 1)]

    def place(self, order, cuts):
        spots = jnp.asarray(self.spots, jnp.int32)
        if self.relative:
            spots = spots ^ lax.axis_index("seq").astype(jnp.int32)
        sources = [self.column] if self.plain else [self.column, *self.near, tuple(self.last)]
        return order(place_weights, sources, spots, cuts)


def place_weights(sources, spots, cuts):
    spot = lax.axis_index("dp")
    if lax.axis_size("dp") != 4:
        cols = sources[0].shape[2]
        halves = place(sources, spots, [(0, 0, cols), (1, 0, cols)])
        halves = [lax.all_gather(half, "dp", axis=0, tiled=True) for half in halves]
        return [halves[side][:, first : first + width] for side, first, width in cuts]
    blocks = jnp.arange(4, dtype=jnp.int32) ^ spot.astype(jnp.int32)
    spots = (blocks[:, None] * spots.shape[0] + spots[None, :]).reshape(-1)
    return place(sources, spots, cuts)


def block_order(first):
    if lax.axis_size("dp") != 4:
        return jnp.arange(4, dtype=jnp.int32)
    spot = lax.axis_index("dp").astype(jnp.int32)
    return jnp.asarray([first, 3, 0, 3 - first], jnp.int32) ^ spot


def row_order(first, relative):
    if not relative:
        places = jnp.arange(lax.axis_size("seq"), dtype=jnp.int32)
        return jnp.concatenate([block_order(first), places])
    away = jnp.arange(lax.axis_size("seq"), dtype=jnp.int32)
    away = away ^ lax.axis_index("seq").astype(jnp.int32)
    turn, bits = jnp.zeros_like(away), seq_steps()
    for one, two in zip(bits, reversed(bits), strict=True):
        turn = turn + jnp.where((away & one) != 0, two, 0)
    return jnp.concatenate([block_order(first), turn])


def weight_grad(pairs, order, extra=None):
    tokens, width = pairs[0][0].shape
    size = width // 4
    cols = sum(right.shape[1] for _, right in pairs)
    cols += 0 if extra is None else extra.shape[1]
    n_seq = lax.axis_size("seq")
    near = lax.axis_size("dp") == 4
    unit = size // n_seq if near else size

    def body(order_ref, *refs):
        away, stay = refs[-2:]
        step = pl.program_id(0)
        parts = [
            dot_tn(refs[2 * j][...], refs[2 * j + 1][...]).astype(LOW) for j in range(len(pairs))
        ]
        if extra is not None:
            parts.append(refs[2 * len(pairs)][...])
        start = 0
        for part in parts:
            stop = start + part.shape[1]

            def put(out):
                for k in range(size // unit):
                    spot = order_ref[4 + k] if near else k
                    rows = pl.ds(pl.multiple_of(spot * unit, unit), unit)
                    out[rows, start:stop] = part[k * unit : (k + 1) * unit]

            pl.when(step < 2)(functools.partial(put, away))
            pl.when(step >= 2)(functools.partial(put, stay))
            start = stop

    specs, values = [], []
    for left, right in pairs:
        specs.append(pl.BlockSpec((tokens, size), lambda i, order: (0, order[i])))
        specs.append(pl.BlockSpec(right.shape, lambda i, order: (0, 0)))
        values += [left, right]
    if extra is not None:
        specs.append(pl.BlockSpec((size, extra.shape[1]), lambda i, order: (order[i], 0)))
        values.append(extra)
    return pl.pallas_call(
        body,
        grid_spec=pltpu.PrefetchScalarGridSpec(
            num_scalar_prefetch=1,
            grid=(4,),
            in_specs=specs,
            out_specs=[
                pl.BlockSpec((size, cols), lambda i, order: (jnp.minimum(i, 1), 0)),
                pl.BlockSpec((size, cols), lambda i, order: (jnp.maximum(i - 2, 0), 0)),
            ],
        ),
        out_shape=[shaped((2 * size, cols), LOW)] * 2,
        compiler_params=params(32),
        cost_estimate=cost(2 * tokens * width * cols, 4 * width * cols),
    )(order, *values)


class Scatter:
    def __init__(self, pair, side, factor, relative=True):
        self.relative = relative
        self.halves, self.factor, self.stage = (pair, side), factor, 0
        self.bits = (2, 1)
        self.plain = lax.axis_size("dp") != 4

    def begin(self, others=()):
        self.came = []
        if not self.plain:
            away = after([away for away, _ in self.halves], others)
            self.came = [swap(v, "dp", bit) for v, bit in zip(away, self.bits, strict=True)]

    @staticmethod
    def early(grad, bit, others=()):
        if lax.axis_size("dp") != 4:
            return None
        (away,) = after([grad[0]], others)
        return swap(away, "dp", bit)

    def begun(self, *came):
        self.came = [] if self.plain else list(came)
        return self

    def next(self, others=()):
        self.last = []
        if not self.plain:
            onward = after(self.onward, others)
            self.last = [
                swap(v, "dp", 3 - bit) for v, bit in zip(onward, self.bits, strict=True)
            ]

    def add(self, order):
        self.stage += 1
        if self.plain:
            if self.stage == 4:
                self.out = self.plain_sum()
            return
        (getattr(self, "add%d" % self.stage))(order)

    def add1(self, order):
        stays = [stay for _, stay in self.halves]

        def step(stays, came):
            size = stays[0].shape[0] // 2
            onward = [
                (stay[size:].astype(F32) + new[size:].astype(F32)).astype(LOW)
                for stay, new in zip(stays, came, strict=True)
            ]
            return onward

        self.onward = order(step, stays, self.came)

    def add2(self, order):
        stays = [stay for _, stay in self.halves]

        def sums(stays, came, last):
            size = stays[0].shape[0] // 2
            return [
                (stay[:size].astype(F32) + new[:size].astype(F32) + more.astype(F32)).astype(LOW)
                for stay, new, more in zip(stays, came, last, strict=True)
            ]

        def step(stays, came, last):
            size = stays[0].shape[0] // 2
            both = jnp.stack(
                [
                    stay[:size].astype(F32) + new[:size].astype(F32) + more.astype(F32)
                    for stay, new, more in zip(stays, came, last, strict=True)
                ]
            )
            size = size // 2
            return both[:, size:].astype(LOW), both[:, :size]

        if not self.relative:
            parts = order(sums, stays, self.came, self.last)
            self.parts = [
                lax.psum_scatter(part, "seq", scatter_dimension=0, tiled=True) for part in parts
            ]
            return
        away, self.kept = order(step, stays, self.came, self.last)
        self.came = swap(away, "seq", 1)

    def add3(self, order):
        if not self.relative:
            return

        def step(kept, came):
            both = kept + came.astype(F32)
            size = both.shape[1] // 2
            return both[:, size:].astype(LOW), both[:, :size]

        away, self.kept = order(step, self.kept, self.came)
        self.came = swap(away, "seq", 2)

    def add4(self, order):
        if not self.relative:
            self.out = order(
                lambda *parts: [part.astype(F32) * self.factor for part in parts], *self.parts
            )
            return
        self.out = order(
            lambda kept, came: (kept + came.astype(F32)) * self.factor, self.kept, self.came
        )

    def plain_sum(self):
        here, n_seq = lax.axis_index("seq"), lax.axis_size("seq")
        columns = []
        for away, stay in self.halves:
            grad = jnp.concatenate([away, stay], axis=0)
            columns.append(
                lax.psum_scatter(grad, "dp", scatter_dimension=0, tiled=True).astype(F32)
            )
        both = jnp.stack(columns)
        both = both.reshape(2, n_seq, -1, both.shape[-1])
        result = pick(both, here, 1)
        for k in range(1, n_seq):
            result = result + swap(pick(both, here ^ k, 1).astype(LOW), "seq", k).astype(F32)
        return result * self.factor


def trade_start(value):
    size = value.shape[0] // 2
    part = lax.dynamic_slice_in_dim(value, lax.axis_index("mp") * size, size, 0)
    return swap(part, "seq", 2)


def trade_end(part):
    rest = swap(part, "mp", 1)
    return jnp.where(
        lax.axis_index("mp") == 0,
        jnp.concatenate([part, rest], axis=0),
        jnp.concatenate([rest, part], axis=0),
    )


def pair_start(value, others):
    row = lax.axis_index("seq") // 2
    (sent,) = after([pick(value, 1 - row)], others)
    return trade_start(sent)


def pair_end(value, part):
    row = lax.axis_index("seq") // 2
    return jnp.concatenate([pick(value, row), trade_end(part)], axis=0)


def back_start(value):
    return trade_start(value[value.shape[0] // 2 :].astype(LOW))


def back_starts(others, *values):
    halves = [value[value.shape[0] // 2 :].astype(LOW) for value in values]
    core, size = lax.axis_index("mp"), halves[0].shape[0] // 2
    parts = [lax.dynamic_slice_in_dim(half, core * size, size, 0) for half in halves]
    (ready,) = after([jnp.stack(parts)], others)
    return swap(ready, "seq", 2)


def back_ends(values, part):
    rest = swap(part, "mp", 1)
    core, row = lax.axis_index("mp"), lax.axis_index("seq") // 2
    came = jnp.where(
        core == 0,
        jnp.concatenate([part, rest], axis=1),
        jnp.concatenate([rest, part], axis=1),
    )
    result = []
    for i, value in enumerate(values):
        kept, new = value[: value.shape[0] // 2], came[i].astype(value.dtype)
        result.append(jnp.where(row == 0, jnp.stack([kept, new]), jnp.stack([new, kept])))
    return result


def back_end(value, part):
    kept = value[: value.shape[0] // 2]
    came = trade_end(part).astype(value.dtype)
    row = lax.axis_index("seq") // 2
    return jnp.where(row == 0, jnp.stack([kept, came]), jnp.stack([came, kept]))


def norm_parts(values):
    center = values - jnp.mean(values, axis=-1, keepdims=True)
    scale = lax.rsqrt(jnp.mean(center * center, axis=-1, keepdims=True) + EPS)
    return center * scale, scale


def enter(inputs, parts, norm, weight):
    tokens, width = inputs.shape
    blocks = weight.shape[1] // TILE
    rows = [inputs, *parts] + ([] if norm is None else list(norm))
    keep = len(parts) > 0 and norm is not None

    def body(*refs):
        x_ref, part_refs = refs[0], refs[1 : 1 + len(parts)]
        norm_refs = refs[1 + len(parts) : len(rows)]
        w_ref = refs[len(rows)]
        outs = refs[len(rows) + 1 :]
        low_ref, out_ref = outs[0], outs[1]

        @pl.when(pl.program_id(0) == 0)
        def _():
            x = x_ref[...].astype(F32)
            if part_refs:
                x = x + (part_refs[0][...].astype(F32) + part_refs[1][...].astype(F32))
            if keep:
                outs[2][...] = x
            if norm_refs:
                x = norm_parts(x)[0] * norm_refs[0][...] + norm_refs[1][...]
            low_ref[...] = x.astype(LOW)

        out_ref[0] = dot_nn(low_ref[...], w_ref[...]).astype(LOW)

    result = pl.pallas_call(
        body,
        grid=(blocks,),
        in_specs=[whole(v.shape) for v in rows] + [pl.BlockSpec((width, TILE), lambda j: (0, j))],
        out_specs=[
            whole((tokens, width)),
            pl.BlockSpec((1, tokens, TILE), lambda j: (j, 0, 0)),
        ]
        + ([whole((tokens, width))] if keep else []),
        out_shape=[shaped((tokens, width), LOW), shaped((blocks, tokens, TILE), LOW)]
        + ([shaped((tokens, width), F32)] if keep else []),
        compiler_params=params(32),
        cost_estimate=cost(2 * tokens * width * weight.shape[1], 14 * tokens * width),
    )(*rows, weight)
    return tuple(result)


def attend_body(rows, q_ref, ko_ref, kp_ref, vo_ref, vp_ref, bias_ref, ctx_ref, lse_ref):
    tokens = q_ref.shape[0]
    lane = lax.broadcasted_iota(jnp.int32, (rows, LANES), 1)
    ko, kp, vo, vp = ko_ref[0], kp_ref[0], vo_ref[0], vp_ref[0]
    for r in range(0, tokens, rows):
        q = q_ref[r : r + rows] * jnp.asarray(HEAD**-0.5, LOW)
        ctx = stat = None
        for h in range(LANES // HEAD):
            mine = (lane // HEAD) == h
            qh = jnp.where(mine, q, jnp.zeros_like(q))
            so = dot_nt(qh, ko) + bias_ref[r : r + rows, :tokens]
            sp = dot_nt(qh, kp) + bias_ref[r : r + rows, tokens:]
            top = jnp.maximum(
                jnp.max(so, axis=1, keepdims=True), jnp.max(sp, axis=1, keepdims=True)
            )
            eo, ep = jnp.exp(so - top), jnp.exp(sp - top)
            total = jnp.sum(eo, axis=1, keepdims=True) + jnp.sum(ep, axis=1, keepdims=True)
            acc = dot_nn(eo.astype(LOW), vo) + dot_nn(ep.astype(LOW), vp)
            acc = acc * (1.0 / total)
            lse = jnp.broadcast_to(top + jnp.log(total), (rows, LANES))
            ctx = acc if ctx is None else jnp.where(mine, acc, ctx)
            stat = lse if stat is None else jnp.where(mine, lse, stat)
        ctx_ref[r : r + rows] = ctx.astype(LOW)
        lse_ref[r : r + rows] = stat


def kv_spec(tokens, half):
    return pl.BlockSpec((1, tokens, LANES), lambda i: (half, 0, i))


def attend(query, own, peer, bias):
    tokens, width = query.shape
    spec = pl.BlockSpec((tokens, LANES), lambda i: (0, i))
    return pl.pallas_call(
        functools.partial(attend_body, 256),
        grid=(width // LANES,),
        in_specs=[spec]
        + [kv_spec(tokens, half) for half in (0, 0, 1, 1)]
        + [whole(bias.shape)],
        out_specs=[spec, spec],
        out_shape=[shaped((tokens, width), LOW), shaped((tokens, width), F32)],
        compiler_params=params(40),
        cost_estimate=cost(16 * tokens * tokens * width, 16 * tokens * width, 2 * tokens * tokens * 8),
    )(query, own, peer, own, peer, bias)


def attend_back_body(
    q_ref, ko_ref, kp_ref, vo_ref, vp_ref, g_ref, lse_ref, bias_ref, dq_ref, own_ref, peer_ref, acc
):
    tokens = q_ref.shape[0]
    lane = lax.broadcasted_iota(jnp.int32, (tokens, LANES), 1)
    q = q_ref[...] * jnp.asarray(HEAD**-0.5, LOW)
    g = g_ref[...]
    lse_t = lse_ref[...].T
    parts = ((kp_ref, vp_ref, peer_ref, tokens), (ko_ref, vo_ref, own_ref, 0))
    keys_t = [k_ref[0].T for k_ref, _, _, _ in parts]
    for h in range(LANES // HEAD):
        mine = (lane // HEAD) == h
        qh = jnp.where(mine, q, jnp.zeros_like(q))
        gh = jnp.where(mine, g, jnp.zeros_like(g))
        rows = slice(h * HEAD, (h + 1) * HEAD)
        lse = lse_t[h * HEAD : h * HEAD + 1]
        probs, inner = [], []
        for k_ref, v_ref, _, base in parts:
            scores = dot_nt(k_ref[0], qh) + bias_ref[base : base + tokens]
            probs.append(jnp.exp(scores - lse))
            inner.append(dot_nt(v_ref[0], gh))
        delta = sum(jnp.sum(p * d, axis=0, keepdims=True) for p, d in zip(probs, inner))
        total = None
        for j, (_, _, out_ref, _) in enumerate(parts):
            grads = (probs[j] * (inner[j] - delta)).astype(LOW)
            dv = dot_nn(probs[j].astype(LOW), gh).astype(LOW)
            dk = dot_nn(grads, qh).astype(LOW)
            part = dot_nn(keys_t[j][rows], grads)
            total = part if total is None else total + part
            if h == 0:
                out_ref[0], out_ref[1] = dk, dv
            else:
                out_ref[0] += dk
                out_ref[1] += dv
        acc[rows] = total
    dq_ref[...] = (acc[...].T * HEAD**-0.5).astype(LOW)


def attend_back(query, own, peer, grad, lse, bias_t):
    tokens, width = query.shape
    spec = pl.BlockSpec((tokens, LANES), lambda i: (0, i))
    both = pl.BlockSpec((2, tokens, LANES), lambda i: (0, 0, i))
    return pl.pallas_call(
        attend_back_body,
        grid=(width // LANES,),
        in_specs=[spec]
        + [kv_spec(tokens, half) for half in (0, 0, 1, 1)]
        + [spec, spec, whole(bias_t.shape)],
        out_specs=[spec, both, both],
        out_shape=[shaped((tokens, width), LOW)] + [shaped((2, tokens, width), LOW)] * 2,
        scratch_shapes=[pltpu.VMEM((LANES, tokens), F32)],
        compiler_params=params(40),
        cost_estimate=cost(40 * tokens * tokens * width, 24 * tokens * width, 2 * tokens * tokens * 8),
    )(query, own, peer, own, peer, grad, lse, bias_t)


def attend_leave(dq, own, came, wq, wkv, apart):
    tokens, width = dq.shape[0], wq.shape[0]
    size = tokens // 2

    def body(dq_ref, own_ref, came_ref, wq_ref, wkv_ref, pair_ref, *outs):
        low = [
            (own_ref[j].astype(F32) + came_ref[j].astype(F32)).astype(LOW) for j in range(2)
        ]
        cols = low[0].shape[1]
        for j in range(2):
            pair_ref[:, j * cols : (j + 1) * cols] = low[j]
        first = dot_nt(dq_ref[...], wq_ref[...])
        rest = dot_nt(pair_ref[...], wkv_ref[...])
        if apart:
            outs[0][0] = first.astype(LOW)
            outs[0][1] = rest.astype(LOW)
        else:
            outs[0][...] = (first + rest).astype(LOW)

    part_spec = (
        pl.BlockSpec((2, size, width), lambda i: (0, i, 0))
        if apart
        else pl.BlockSpec((size, width), lambda i: (i, 0))
    )
    cols = own.shape[2]
    return pl.pallas_call(
        body,
        grid=(2,),
        in_specs=[
            pl.BlockSpec((size, cols), lambda i: (i, 0)),
            pl.BlockSpec((2, size, cols), lambda i: (0, i, 0)),
            pl.BlockSpec((2, size, cols), lambda i: (0, i, 0)),
            whole(wq.shape),
            whole(wkv.shape),
        ],
        out_specs=[pl.BlockSpec((size, 2 * cols), lambda i: (i, 0)), part_spec],
        out_shape=[
            shaped((tokens, 2 * cols), LOW),
            shaped((2, tokens, width) if apart else (tokens, width), LOW),
        ],
        compiler_params=params(32),
        cost_estimate=cost(6 * tokens * width * cols, 14 * tokens * cols + 6 * width * cols),
    )(dq, own, came, wq, wkv)


def feed(inputs, parts, norm, up, down):
    tokens, width = inputs.shape
    hidden = up.shape[1]

    def body(x_ref, one_ref, two_ref, gain_ref, bias_ref, up_ref, down_ref, *rest):
        normed_ref, total_ref, act_ref, slope_ref, part_ref, acc = rest
        step = pl.program_id(0)

        @pl.when(step == 0)
        def _():
            x = x_ref[...].astype(F32) + (one_ref[...].astype(F32) + two_ref[...].astype(F32))
            total_ref[...] = x
            normed_ref[...] = (norm_parts(x)[0] * gain_ref[...] + bias_ref[...]).astype(LOW)

        pre = dot_nn(normed_ref[...], up_ref[...])
        below = 0.5 + 0.5 * lax.erf(pre * (0.5**0.5))
        act = (pre * below).astype(LOW)
        act_ref[...] = act
        slope = below + pre * (jnp.exp(pre * pre * -0.5) * 0.3989422804014327)
        slope_ref[...] = slope.astype(LOW)
        part = dot_nt(act, down_ref[...])

        @pl.when(step == 0)
        def _():
            acc[...] = part

        @pl.when(step > 0)
        def _():
            acc[...] += part

        @pl.when(step == pl.num_programs(0) - 1)
        def _():
            part_ref[...] = acc[...].astype(LOW)

    block = pl.BlockSpec((tokens, TILE), lambda j: (0, j))
    weight = pl.BlockSpec((width, TILE), lambda j: (0, j))
    same = whole((tokens, width))
    return pl.pallas_call(
        body,
        grid=(hidden // TILE,),
        in_specs=[same, same, same, whole((1, width)), whole((1, width)), weight, weight],
        out_specs=[same, same, block, block, same],
        out_shape=[
            shaped((tokens, width), LOW),
            shaped((tokens, width), F32),
            shaped((tokens, hidden), LOW),
            shaped((tokens, hidden), LOW),
            shaped((tokens, width), LOW),
        ],
        scratch_shapes=[pltpu.VMEM((tokens, width), F32)],
        compiler_params=params(48),
        cost_estimate=cost(4 * tokens * width * hidden, 8 * width * hidden, 2 * tokens * hidden),
    )(inputs, *parts, *norm, up, down)


def feed_back(low, slope, up, down):
    tokens, width = low.shape
    hidden = up.shape[1]

    def body(low_ref, slope_ref, up_ref, down_ref, pre_ref, part_ref, acc):
        step = pl.program_id(0)
        act_grad = dot_nn(low_ref[...], down_ref[...])
        pre = (act_grad * slope_ref[...].astype(F32)).astype(LOW)
        pre_ref[...] = pre
        part = dot_nt(pre, up_ref[...])

        @pl.when(step == 0)
        def _():
            acc[...] = part

        @pl.when(step > 0)
        def _():
            acc[...] += part

        @pl.when(step == pl.num_programs(0) - 1)
        def _():
            part_ref[...] = acc[...].astype(LOW)

    block = pl.BlockSpec((tokens, TILE), lambda j: (0, j))
    weight = pl.BlockSpec((width, TILE), lambda j: (0, j))
    same = whole((tokens, width))
    return pl.pallas_call(
        body,
        grid=(hidden // TILE,),
        in_specs=[same, block, weight, weight],
        out_specs=[block, same],
        out_shape=[shaped((tokens, hidden), LOW), shaped((tokens, width), LOW)],
        scratch_shapes=[pltpu.VMEM((tokens, width), F32)],
        compiler_params=params(48),
        cost_estimate=cost(4 * tokens * width * hidden, 6 * width * hidden),
    )(low, slope, up, down)


def norm_back(grad, values, parts, gain, weight):
    tokens, width = grad.shape
    size = tokens // 2

    def body(*refs):
        g_ref, x_ref, one_ref, two_ref, gain_ref = refs[:5]
        outs = refs[5:] if weight is None else refs[6:]
        step = pl.program_id(0)
        normed_grad = one_ref[...].astype(F32) + two_ref[...].astype(F32)
        unit, scale = norm_parts(x_ref[...].astype(F32))
        gains = jnp.sum(normed_grad * unit, axis=0, keepdims=True)
        biases = jnp.sum(normed_grad, axis=0, keepdims=True)
        inner = normed_grad * gain_ref[...]
        inner = inner - jnp.mean(inner, axis=-1, keepdims=True) - unit * jnp.mean(
            inner * unit, axis=-1, keepdims=True
        )
        total = g_ref[...] + inner * scale
        outs[0][...] = total

        @pl.when(step == 0)
        def _():
            outs[1][...] = jnp.concatenate([gains, biases], axis=0)

        @pl.when(step > 0)
        def _():
            outs[1][...] += jnp.concatenate([gains, biases], axis=0)

        if weight is not None:
            low = total.astype(LOW)
            outs[2][...] = low
            outs[3][...] = dot_nn(low, refs[5][...]).astype(LOW)

    row = pl.BlockSpec((size, width), lambda i: (i, 0))
    in_specs = [row] * 4 + [whole((1, width))]
    out_specs = [row, whole((2, width))]
    out_shape = [shaped((tokens, width), F32), shaped((2, width), F32)]
    extra = []
    if weight is not None:
        cols = weight.shape[1]
        extra = [weight]
        in_specs.append(whole(weight.shape))
        out_specs += [row, pl.BlockSpec((size, cols), lambda i: (i, 0))]
        out_shape += [shaped((tokens, width), LOW), shaped((tokens, cols), LOW)]
    return pl.pallas_call(
        body,
        grid=(tokens // size,),
        in_specs=in_specs,
        out_specs=out_specs,
        out_shape=out_shape,
        compiler_params=params(40),
        cost_estimate=cost(20 * tokens * width, 20 * tokens * width),
    )(grad, values, *parts, gain, *extra)


def weight_grad_one(left, right, order, extra=None):
    return weight_grad([(left, right)], order, extra)


def weight_grad_two(one, two, order, extra=None):
    return weight_grad([one, two], order, extra)


def attend_leave_apart(dq, own, came, wq, wkv):
    return attend_leave(dq, own, came, wq, wkv, True)


def attend_leave_joined(dq, own, came, wq, wkv):
    return attend_leave(dq, own, came, wq, wkv, False)


def norm_back_last(grad, values, parts, gain):
    return norm_back(grad, values, parts, gain, None)


def low_too(value):
    return value, value.astype(LOW)


def norm_columns(*norm_rows):
    rows = jnp.concatenate(norm_rows, axis=0).astype(LOW)
    return jnp.pad(rows.T, ((0, 0), (0, LANES - rows.shape[0])))


def token_counts(lengths, groups):
    onehot = (groups[:, :, None] == jnp.arange(LANGS, dtype=jnp.int32)).astype(F32)
    counts = jnp.sum(onehot * lengths[:, :, None].astype(F32), axis=(0, 1))
    if lax.axis_size("dp") != 4:
        counts = lax.psum(counts, "dp")
        return counts, counts
    counts = jnp.pad(counts[None], ((0, 7), (0, LANES - LANGS)))
    counts = counts + swap(counts, "dp", 1)
    came = swap(counts, "dp", 2)
    return (counts + came)[0, :LANGS], came


def token_tables(lengths, groups, counts, full_len, quarter):
    here, row = lax.axis_index("seq"), lax.axis_index("seq") // 2
    rows = lengths.shape[0]
    onehot = (groups[:, :, None] == jnp.arange(LANGS, dtype=jnp.int32)).astype(F32)
    all_tokens = rows * lax.axis_size("dp") * full_len
    seg_weight = all_tokens / (LANGS * jnp.sum(onehot * counts, axis=2))
    ends = pick(jnp.cumsum(lengths, axis=1), row)
    steps = jnp.arange(quarter, dtype=jnp.int32)
    places = jnp.concatenate([(here ^ k) * quarter + steps for k in (0, 2, 1, 3)])
    segs = jnp.sum((ends[None, :] <= places[:, None]).astype(jnp.int32), axis=1)
    mine = 2 * quarter
    same = segs[:mine, None] == segs[None, :]
    causal = same & (places[None, :] <= places[:mine, None])
    same_t = segs[:, None] == segs[None, :mine]
    causal_t = same_t & (places[:, None] <= places[None, :mine])
    offsets = [jnp.where(mask, 0.0, -1e30).astype(F32) for mask in (same, same_t, causal, causal_t)]
    match = (segs[:mine, None] == jnp.arange(NSEG, dtype=jnp.int32)).astype(F32)
    tok_weight = jnp.sum(match * pick(seg_weight, row)[None, :], axis=1)
    return offsets, tok_weight, all_tokens


def attn_shard(qkv, out):
    pair = jnp.concatenate([qkv[1], qkv[2]], axis=1)
    side = jnp.concatenate([qkv[0], out.T], axis=1)
    return [pair, side]


def qkv_out(both):
    pair, side = both[0], both[1]
    width = side.shape[1] // 2
    qkv = jnp.stack([side[:, :width], pair[:, :width], pair[:, width:]])
    return qkv, side[:, width:].T


def project(left, right):
    return dot_nn(left, right).astype(LOW)


def project_out(ctx, wo):
    return dot_nt(ctx, wo).astype(LOW)


def other_core(part):
    return swap(part, "mp", 1)


def per_device(
    src,
    tgt,
    cotangent,
    lengths,
    groups,
    enc_gains,
    enc_biases,
    enc_qkv,
    enc_out,
    enc_up,
    enc_down,
    dec_gains,
    dec_biases,
    dec_self_qkv,
    dec_cross_qkv,
    dec_outs,
    dec_up,
    dec_down,
):
    rows, quarter, width = src.shape
    full_len = quarter * lax.axis_size("seq")
    n_enc, n_dec = enc_gains.shape[0], dec_gains.shape[0]
    half, hidden = enc_qkv.shape[2], enc_up.shape[1]
    order = Order()

    norms = jnp.concatenate([enc_gains, enc_biases, dec_gains, dec_biases], axis=0)
    n_norms = norms.shape[0]
    extra = jnp.pad(norms.T, ((0, 0), (0, LANES - n_norms)))
    enc_pair, enc_side = attn_shard(enc_qkv, enc_out)
    shards = [
        [jnp.concatenate([v, extra], axis=1) for v in (enc_pair, enc_side)],
        [
            jnp.concatenate(attn_shard(dec_self_qkv, dec_outs[0]), axis=1),
            jnp.concatenate(attn_shard(dec_cross_qkv, dec_outs[1]), axis=1),
        ],
        [enc_up, enc_down.T],
        [dec_up, dec_down.T],
    ]
    attn_cuts = [(0, 0, 2 * half), (1, 0, half), (1, half, half)]
    both_cuts = [
        (j, first, wide)
        for j in range(2)
        for first, wide in ((0, 2 * half), (2 * half, half), (3 * half, half))
    ]
    feed_cuts = [(0, 0, hidden), (1, 0, hidden)]
    counts, counted = token_counts(lengths, groups)
    one, two = [Gather(shard, True) for shard in shards[:2]]
    one.along()
    two.along([one.came])
    one.join(order)
    one.along()
    one.join(order)
    one.across([counted])
    y_first, x_first = order(lambda: (row_order(2, True), row_order(1, True)))
    two.join(order)
    two.along([one.column])
    three, four = [Gather(shard, False, [two.came]) for shard in shards[2:]]
    one.far(order)
    two.join(order)
    src_part = pair_start(src, [two.column])
    two.across(one.last)
    offsets, tok_weight, all_tokens = order(
        token_tables, lengths, groups, counts, full_len, quarter
    )
    same, same_t, causal, causal_t = offsets
    factor = 1.0 / all_tokens
    *enc_w, table = one.place(order, attn_cuts + [(0, 2 * half, LANES)])
    table = table[:, :n_norms].T.astype(F32)[:, None]
    e_norm = [(table[i], table[n_enc + i]) for i in range(n_enc)]
    d_norm = [(table[2 * n_enc + i], table[2 * n_enc + n_dec + i]) for i in range(n_dec)]
    x_src = order(pair_end, src, src_part)
    enc_in, enc_own = order(enter, x_src, (), e_norm[0], enc_w[0])
    enc_peer = swap(enc_own, "seq", 1)
    enc_q = order(project, enc_in, enc_w[1])
    tgt_part = pair_start(tgt, [enc_q])
    two.far(order)
    three.across(two.last)
    enc_ctx, enc_lse = order(attend, enc_q, enc_own, enc_peer, same)
    enc_part = order(project_out, enc_ctx, enc_w[2])
    enc_other = other_core(enc_part)
    x_tgt = order(pair_end, tgt, tgt_part)
    weights = two.place(order, both_cuts)
    self_w, cross_w = weights[:3], weights[3:]
    self_in, self_own = order(enter, x_tgt, (), d_norm[0], self_w[0])
    self_peer = swap(self_own, "seq", 1)
    self_q = order(project, self_in, self_w[1])
    cot_part = pair_start(cotangent, [self_q])
    three.far(order)
    four.across(three.last)
    order.wait(three.last)
    self_ctx, self_lse = order(attend, self_q, self_own, self_peer, causal)
    self_part = order(project_out, self_ctx, self_w[2])
    self_other = other_core(self_part)
    cot = order(pair_end, cotangent, cot_part)
    out_grad, out_low = order(
        lambda cot, weight: low_too(cot.astype(F32) * weight[:, None]), cot, tok_weight
    )
    e_up, e_down = three.place(order, feed_cuts)
    enc_normed, enc_mid, enc_act, enc_slope, mem_part = order(
        feed, x_src, (enc_part, enc_other), e_norm[1], e_up, e_down
    )
    mem_other = other_core(mem_part)
    four.far(order)
    source, cross_own = order(enter, enc_mid, (mem_part, mem_other), None, cross_w[0])
    cross_peer = swap(cross_own, "seq", 1)
    cross_in, cross_q, dec_mid = order(
        enter, x_tgt, (self_part, self_other), d_norm[1], cross_w[1]
    )
    cross_q = cross_q[0]
    d_up, d_down = four.place(order, feed_cuts)
    cross_ctx, cross_lse = order(attend, cross_q, cross_own, cross_peer, same)
    cross_part = order(project_out, cross_ctx, cross_w[2])
    cross_other = other_core(cross_part)
    dec_normed, dec_cross, dec_act, dec_slope, dec_part = order(
        feed, dec_mid, (cross_part, cross_other), d_norm[2], d_up, d_down
    )
    dec_other = other_core(dec_part)

    pre_grad, part = order(feed_back, out_low, dec_slope, d_up, d_down)
    parts = (part, other_core(part))
    down_g = order(weight_grad_one, out_low, dec_act, x_first)
    up_g = order(weight_grad_one, dec_normed, pre_grad, y_first)
    d_feed = Scatter(up_g, down_g, factor)
    d_feed.begin()
    cross_g, norm_five, low, ctx_grad = order(
        norm_back, out_grad, dec_cross, parts, d_norm[2][0], cross_w[2]
    )
    dq, own_grad, peer_grad = order(
        attend_back, cross_q, cross_own, cross_peer, ctx_grad, cross_lse, same_t
    )
    came = swap(peer_grad, "seq", 1)
    side_g = order(weight_grad_two, (cross_in, dq), (low, cross_ctx), x_first)
    decoded = order(
        lambda total, one, two: (total + (one.astype(F32) + two.astype(F32))).astype(LOW),
        dec_cross,
        dec_part,
        dec_other,
    )
    pair_low, part = order(attend_leave_apart, dq, own_grad, came, cross_w[1], cross_w[0])
    other = other_core(part)
    pair_g = order(weight_grad_one, source, pair_low, y_first)
    cross = Scatter(pair_g, side_g, factor)
    cross.begin(d_feed.came)
    d_feed.add(order)
    memory_grad, memory_low = order(
        lambda one, two: low_too(one[1].astype(F32) + two[1].astype(F32)), part, other
    )
    cross_parts = (part[0], other[0])
    pre_grad, enc_part = order(feed_back, memory_low, enc_slope, e_up, e_down)
    enc_parts = (enc_part, other_core(enc_part))
    down_g = order(weight_grad_one, memory_low, enc_act, x_first)
    d_feed.next(cross.came)
    cross.add(order)
    up_g = order(weight_grad_one, enc_normed, pre_grad, y_first)
    e_feed = Scatter(up_g, down_g, factor)
    e_feed.begin(d_feed.last)
    order.wait(d_feed.last)
    mid_g, norm_four, low, ctx_grad = order(
        norm_back, cross_g, dec_mid, cross_parts, d_norm[1][0], self_w[2]
    )
    dq, own_grad, peer_grad = order(
        attend_back, self_q, self_own, self_peer, ctx_grad, self_lse, causal_t
    )
    came = swap(peer_grad, "seq", 1)
    d_feed.add(order)
    cross.next(e_feed.came)
    enc_mid_g, norm_two, enc_low, enc_ctx_grad = order(
        norm_back, memory_grad, enc_mid, enc_parts, e_norm[1][0], enc_w[2]
    )
    enc_dq, enc_own_grad, enc_peer_grad = order(
        attend_back, enc_q, enc_own, enc_peer, enc_ctx_grad, enc_lse, same_t
    )
    enc_came = swap(enc_peer_grad, "seq", 1)
    e_feed.add(order)
    pair_low, part = order(attend_leave_joined, dq, own_grad, came, self_w[1], self_w[0])
    parts = (part, other_core(part))
    d_feed.add(order)
    side_g = order(weight_grad_two, (self_in, dq), (low, self_ctx), x_first)
    pair_g = order(weight_grad_one, self_in, pair_low, y_first)
    self_s = Scatter(pair_g, side_g, factor)
    e_feed.next(cross.last)
    cross.add(order)
    tgt_grad, norm_three = order(norm_back_last, mid_g, x_tgt, parts, d_norm[0][0])
    pair_low, part = order(
        attend_leave_joined, enc_dq, enc_own_grad, enc_came, enc_w[1], enc_w[0]
    )
    enc_parts = (part, other_core(part))
    d_feed.add(order)
    self_s.begin(e_feed.last)
    e_feed.add(order)
    src_grad, norm_one = order(norm_back_last, enc_mid_g, x_src, enc_parts, e_norm[0][0])
    columns = order(norm_columns, norm_one, norm_two, norm_three, norm_four, norm_five)
    side_g = order(weight_grad_two, (enc_in, enc_dq), (enc_low, enc_ctx), x_first, columns)
    pair_g = order(weight_grad_one, enc_in, pair_low, y_first, columns)
    enc = Scatter(pair_g, side_g, factor)
    cross.add(order)
    enc.begin(self_s.came)
    self_s.add(order)
    e_feed.add(order)
    self_s.next(enc.came)
    enc.add(order)
    enc.next(self_s.last)
    cross.add(order)
    self_s.add(order)
    enc.add(order)
    src_part = back_starts(enc.last if not enc.plain else [], src_grad)
    three_part = back_starts([], decoded, memory_low, tgt_grad)
    self_s.add(order)
    e_feed.add(order)
    enc.add(order)
    decoded, memory_grad, tgt_grad = order(
        back_ends, (decoded, memory_grad, tgt_grad), three_part
    )
    self_s.add(order)
    (src_grad,) = order(back_ends, (src_grad,), src_part)
    enc.add(order)

    norm_out = enc.out[0][:, 2 * half : 2 * half + n_norms].T
    rows_of = [2 * j + i for i in range(2) for j in range(n_enc)]
    rows_of += [2 * (n_enc + j) + i for i in range(2) for j in range(n_dec)]
    norm_out = jnp.stack([norm_out[i] for i in rows_of])
    enc_qkv_g, enc_out_g = qkv_out([part[:, : 2 * half] for part in enc.out])
    self_qkv_g, self_out_g = qkv_out(self_s.out)
    cross_qkv_g, cross_out_g = qkv_out(cross.out)
    return (
        decoded,
        src_grad,
        tgt_grad,
        memory_grad,
        norm_out[:n_enc],
        norm_out[n_enc : 2 * n_enc],
        enc_qkv_g,
        enc_out_g,
        e_feed.out[0],
        e_feed.out[1].T,
        norm_out[2 * n_enc : 2 * n_enc + n_dec],
        norm_out[2 * n_enc + n_dec :],
        self_qkv_g,
        cross_qkv_g,
        jnp.stack([self_out_g, cross_out_g]),
        d_feed.out[0],
        d_feed.out[1].T,
    )


def solution(mesh):
    placed = (
        P("dp", "seq", None),
        P("dp", "seq", None),
        P("dp", "seq", None),
        P("dp", None),
        P("dp", None),
        P(None, ("dp", "seq")),
        P(None, ("dp", "seq")),
        P(None, ("dp", "seq"), "mp"),
        P("mp", ("dp", "seq")),
        P(("dp", "seq"), "mp"),
        P("mp", ("dp", "seq")),
        P(None, ("dp", "seq")),
        P(None, ("dp", "seq")),
        P(None, ("dp", "seq"), "mp"),
        P(None, ("dp", "seq"), "mp"),
        P(None, "mp", ("dp", "seq")),
        P(("dp", "seq"), "mp"),
        P("mp", ("dp", "seq")),
    )
    return jax.shard_map(
        per_device,
        mesh=mesh,
        in_specs=placed,
        out_specs=(
            P("dp", "seq", None),
            P("dp", "seq", None),
            P("dp", "seq", None),
            P("dp", "seq", None),
            P(None, ("dp", "seq")),
            P(None, ("dp", "seq")),
            P(None, ("dp", "seq"), "mp"),
            P("mp", ("dp", "seq")),
            P(("dp", "seq"), "mp"),
            P("mp", ("dp", "seq")),
            P(None, ("dp", "seq")),
            P(None, ("dp", "seq")),
            P(None, ("dp", "seq"), "mp"),
            P(None, ("dp", "seq"), "mp"),
            P(None, "mp", ("dp", "seq")),
            P(("dp", "seq"), "mp"),
            P("mp", ("dp", "seq")),
        ),
        check_vma=False,
    )
```

```python
import functools

import jax
import jax.numpy as jnp
from jax import lax
from jax.experimental import pallas as pl
from jax.experimental.pallas import tpu as pltpu
from jax.sharding import PartitionSpec as P

HEAD = 64
NSEG = 8
LANGS = 4
LANES = 128
TILE = 512
F32 = jnp.float32
LOW = jnp.bfloat16
EPS = 1e-05


def dot_nn(left, right):
    return jnp.dot(left, right, preferred_element_type=F32)


def dot_tn(left, right):
    return lax.dot_general(left, right, (((0,), (0,)), ((), ())), preferred_element_type=F32)


def dot_nt(left, right):
    return lax.dot_general(left, right, (((1,), (1,)), ((), ())), preferred_element_type=F32)


def xor_perm(size, bits):
    return [(i, i ^ bits) for i in range(size)]


def swap(value, axis, bits):
    return lax.ppermute(value, axis, xor_perm(lax.axis_size(axis), bits))


def pick(value, index, axis=0):
    return lax.dynamic_index_in_dim(value, index, axis, keepdims=False)


def params(mib):
    return pltpu.CompilerParams(vmem_limit_bytes=mib * 5 // 8 << 20)


def whole(shape):
    return pl.BlockSpec(shape, lambda *_: (0,) * len(shape))


def shaped(shape, dtype):
    return jax.ShapeDtypeStruct(shape, dtype)


def cost(flops, nbytes, exps=0):
    return pl.CostEstimate(flops=1, bytes_accessed=1, transcendentals=0)


class Order:
    def __init__(self):
        self.last = []

    def __call__(self, step, *values):
        leaves, tree = jax.tree.flatten(values)
        spots = [i for i, leaf in enumerate(leaves) if isinstance(leaf, jax.Array)]
        for i, leaf in zip(spots, after([leaves[i] for i in spots], self.last), strict=True):
            leaves[i] = leaf
        out = step(*jax.tree.unflatten(tree, leaves))
        self.last = jax.tree.leaves(out)
        return out

    def wait(self, *values):
        self.last = self.last + jax.tree.leaves(values)


def after(values, others):
    count = len(values)
    return list(lax.optimization_barrier((*values, *others))[:count])


def place(sources, order, cuts):
    flat, where_from = [], []
    for source in sources:
        if isinstance(source, tuple):
            where_from.append([(len(flat), None), (len(flat) + 1, None)])
            flat.extend(source)
        else:
            where_from.append([(len(flat), 0), (len(flat), 1)])
            flat.append(source)
    count = len(sources)
    rows, cols = flat[0].shape[-2:]
    each = order.shape[0] // count
    size = rows // each

    def body(order_ref, *refs):
        inputs = refs[: len(flat)]
        outs = refs[len(flat) : len(flat) + len(cuts)]
        held, in_sems, out_sems = refs[len(flat) + len(cuts) :]
        loads = []
        for j in range(count):
            for half in range(2):
                index, part = where_from[j][half]
                source = inputs[index] if part is None else inputs[index].at[part]
                loads.append(
                    pltpu.make_async_copy(source, held.at[half, j], in_sems.at[2 * j + half])
                )
                loads[-1].start()
        stores = []
        for j in range(count):
            for half in range(2):
                loads[2 * j + half].wait()
                for i in range(each):
                    spot = order_ref[j * each + i]
                    start = pl.multiple_of(spot * size, size)
                    for n, (side, first, width) in enumerate(cuts):
                        if side != half:
                            continue
                        stores.append(
                            pltpu.make_async_copy(
                                held.at[half, j, pl.ds(i * size, size), pl.ds(first, width)],
                                outs[n].at[pl.ds(start, size)],
                                out_sems.at[j * each + i, n],
                            )
                        )
                        stores[-1].start()
        for store in stores:
            store.wait()

    total = count * rows
    return pl.pallas_call(
        body,
        out_shape=[shaped((total, width), LOW) for _, _, width in cuts],
        in_specs=[pl.BlockSpec(memory_space=pltpu.SMEM)]
        + [pl.BlockSpec(memory_space=pl.ANY)] * len(flat),
        out_specs=[pl.BlockSpec(memory_space=pl.ANY)] * len(cuts),
        scratch_shapes=[
            pltpu.VMEM((2, count, rows, cols), LOW),
            pltpu.SemaphoreType.DMA((2 * count,)),
            pltpu.SemaphoreType.DMA((order.shape[0], len(cuts))),
        ],
        compiler_params=params(24),
        cost_estimate=cost(0, 8 * total * cols),
    )(order, *flat)


def seq_steps():
    steps, step = [], lax.axis_size("seq") // 2
    while step:
        steps.append(step)
        step //= 2
    return steps


def seq_order():
    spots = [0]
    for step in seq_steps():
        spots += [spot ^ step for spot in spots]
    return spots


class Gather:
    def __init__(self, shards, stepwise, others=()):
        self.plain = lax.axis_size("dp") != 4
        self.relative = stepwise
        shards = jnp.stack(shards)
        if others:
            (shards,) = after([shards], others)
        if stepwise:
            self.spots, self.column, self.steps = seq_order(), shards, seq_steps()
        else:
            self.spots = list(range(lax.axis_size("seq")))
            self.column = lax.all_gather(shards, "seq", axis=1, tiled=True)

    def along(self, others=()):
        (ready,) = after([self.column], others)
        self.came = swap(ready, "seq", self.steps.pop(0))

    def join(self, order):
        self.column = order(
            lambda one, two: jnp.concatenate([one, two], axis=1), self.column, self.came
        )

    def across(self, others=()):
        self.near = []
        if self.plain:
            return
        (ready,) = after([self.column], others)
        self.near = [swap(ready, "dp", 1), swap(ready, "dp", 2)]

    def far(self, order):
        self.last = []
        if self.plain:
            return
        one, two = order(lambda x, y: (x[0], y[1]), *self.near)
        self.last = [swap(one, "dp", 2), swap(two, "dp", 1)]

    def place(self, order, cuts):
        spots = jnp.asarray(self.spots, jnp.int32)
        if self.relative:
            spots = spots ^ lax.axis_index("seq").astype(jnp.int32)
        sources = [self.column] if self.plain else [self.column, *self.near, tuple(self.last)]
        return order(place_weights, sources, spots, cuts)


def place_weights(sources, spots, cuts):
    spot = lax.axis_index("dp")
    if lax.axis_size("dp") != 4:
        cols = sources[0].shape[2]
        halves = place(sources, spots, [(0, 0, cols), (1, 0, cols)])
        halves = [lax.all_gather(half, "dp", axis=0, tiled=True) for half in halves]
        return [halves[side][:, first : first + width] for side, first, width in cuts]
    blocks = jnp.arange(4, dtype=jnp.int32) ^ spot.astype(jnp.int32)
    spots = (blocks[:, None] * spots.shape[0] + spots[None, :]).reshape(-1)
    return place(sources, spots, cuts)


def block_order(first):
    if lax.axis_size("dp") != 4:
        return jnp.arange(4, dtype=jnp.int32)
    spot = lax.axis_index("dp").astype(jnp.int32)
    return jnp.asarray([first, 3, 0, 3 - first], jnp.int32) ^ spot


def row_order(first, relative):
    if not relative:
        places = jnp.arange(lax.axis_size("seq"), dtype=jnp.int32)
        return jnp.concatenate([block_order(first), places])
    away = jnp.arange(lax.axis_size("seq"), dtype=jnp.int32)
    away = away ^ lax.axis_index("seq").astype(jnp.int32)
    turn, bits = jnp.zeros_like(away), seq_steps()
    for one, two in zip(bits, reversed(bits), strict=True):
        turn = turn + jnp.where((away & one) != 0, two, 0)
    return jnp.concatenate([block_order(first), turn])


def weight_grad(pairs, order, extra=None):
    tokens, width = pairs[0][0].shape
    size = width // 4
    cols = sum(right.shape[1] for _, right in pairs)
    cols += 0 if extra is None else extra.shape[1]
    n_seq = lax.axis_size("seq")
    near = lax.axis_size("dp") == 4
    unit = size // n_seq if near else size

    def body(order_ref, *refs):
        away, stay = refs[-2:]
        step = pl.program_id(0)
        parts = [
            dot_tn(refs[2 * j][...], refs[2 * j + 1][...]).astype(LOW) for j in range(len(pairs))
        ]
        if extra is not None:
            parts.append(refs[2 * len(pairs)][...])
        start = 0
        for part in parts:
            stop = start + part.shape[1]

            def put(out):
                for k in range(size // unit):
                    spot = order_ref[4 + k] if near else k
                    rows = pl.ds(pl.multiple_of(spot * unit, unit), unit)
                    out[rows, start:stop] = part[k * unit : (k + 1) * unit]

            pl.when(step < 2)(functools.partial(put, away))
            pl.when(step >= 2)(functools.partial(put, stay))
            start = stop

    specs, values = [], []
    for left, right in pairs:
        specs.append(pl.BlockSpec((tokens, size), lambda i, order: (0, order[i])))
        specs.append(pl.BlockSpec(right.shape, lambda i, order: (0, 0)))
        values += [left, right]
    if extra is not None:
        specs.append(pl.BlockSpec((size, extra.shape[1]), lambda i, order: (order[i], 0)))
        values.append(extra)
    return pl.pallas_call(
        body,
        grid_spec=pltpu.PrefetchScalarGridSpec(
            num_scalar_prefetch=1,
            grid=(4,),
            in_specs=specs,
            out_specs=[
                pl.BlockSpec((size, cols), lambda i, order: (jnp.minimum(i, 1), 0)),
                pl.BlockSpec((size, cols), lambda i, order: (jnp.maximum(i - 2, 0), 0)),
            ],
        ),
        out_shape=[shaped((2 * size, cols), LOW)] * 2,
        compiler_params=params(32),
        cost_estimate=cost(2 * tokens * width * cols, 4 * width * cols),
    )(order, *values)


class Scatter:
    def __init__(self, pair, side, factor, relative=True):
        self.relative = relative
        self.halves, self.factor, self.stage = (pair, side), factor, 0
        self.bits = (2, 1)
        self.plain = lax.axis_size("dp") != 4

    def begin(self, others=()):
        self.came = []
        if not self.plain:
            away = after([away for away, _ in self.halves], others)
            self.came = [swap(v, "dp", bit) for v, bit in zip(away, self.bits, strict=True)]

    @staticmethod
    def early(grad, bit, others=()):
        if lax.axis_size("dp") != 4:
            return None
        (away,) = after([grad[0]], others)
        return swap(away, "dp", bit)

    def begun(self, *came):
        self.came = [] if self.plain else list(came)
        return self

    def next(self, others=()):
        self.last = []
        if not self.plain:
            onward = after(self.onward, others)
            self.last = [
                swap(v, "dp", 3 - bit) for v, bit in zip(onward, self.bits, strict=True)
            ]

    def add(self, order):
        self.stage += 1
        if self.plain:
            if self.stage == 4:
                self.out = self.plain_sum()
            return
        (getattr(self, "add%d" % self.stage))(order)

    def add1(self, order):
        stays = [stay for _, stay in self.halves]

        def step(stays, came):
            size = stays[0].shape[0] // 2
            onward = [
                (stay[size:].astype(F32) + new[size:].astype(F32)).astype(LOW)
                for stay, new in zip(stays, came, strict=True)
            ]
            return onward

        self.onward = order(step, stays, self.came)

    def add2(self, order):
        stays = [stay for _, stay in self.halves]

        def sums(stays, came, last):
            size = stays[0].shape[0] // 2
            return [
                (stay[:size].astype(F32) + new[:size].astype(F32) + more.astype(F32)).astype(LOW)
                for stay, new, more in zip(stays, came, last, strict=True)
            ]

        def step(stays, came, last):
            size = stays[0].shape[0] // 2
            both = jnp.stack(
                [
                    stay[:size].astype(F32) + new[:size].astype(F32) + more.astype(F32)
                    for stay, new, more in zip(stays, came, last, strict=True)
                ]
            )
            size = size // 2
            return both[:, size:].astype(LOW), both[:, :size]

        if not self.relative:
            parts = order(sums, stays, self.came, self.last)
            self.parts = [
                lax.psum_scatter(part, "seq", scatter_dimension=0, tiled=True) for part in parts
            ]
            return
        away, self.kept = order(step, stays, self.came, self.last)
        self.came = swap(away, "seq", 1)

    def add3(self, order):
        if not self.relative:
            return

        def step(kept, came):
            both = kept + came.astype(F32)
            size = both.shape[1] // 2
            return both[:, size:].astype(LOW), both[:, :size]

        away, self.kept = order(step, self.kept, self.came)
        self.came = swap(away, "seq", 2)

    def add4(self, order):
        if not self.relative:
            self.out = order(
                lambda *parts: [part.astype(F32) * self.factor for part in parts], *self.parts
            )
            return
        self.out = order(
            lambda kept, came: (kept + came.astype(F32)) * self.factor, self.kept, self.came
        )

    def plain_sum(self):
        here, n_seq = lax.axis_index("seq"), lax.axis_size("seq")
        columns = []
        for away, stay in self.halves:
            grad = jnp.concatenate([away, stay], axis=0)
            columns.append(
                lax.psum_scatter(grad, "dp", scatter_dimension=0, tiled=True).astype(F32)
            )
        both = jnp.stack(columns)
        both = both.reshape(2, n_seq, -1, both.shape[-1])
        result = pick(both, here, 1)
        for k in range(1, n_seq):
            result = result + swap(pick(both, here ^ k, 1).astype(LOW), "seq", k).astype(F32)
        return result * self.factor


def trade_start(value):
    size = value.shape[0] // 2
    part = lax.dynamic_slice_in_dim(value, lax.axis_index("mp") * size, size, 0)
    return swap(part, "seq", 2)


def trade_end(part):
    rest = swap(part, "mp", 1)
    return jnp.where(
        lax.axis_index("mp") == 0,
        jnp.concatenate([part, rest], axis=0),
        jnp.concatenate([rest, part], axis=0),
    )


def pair_start(value, others):
    row = lax.axis_index("seq") // 2
    (sent,) = after([pick(value, 1 - row)], others)
    return trade_start(sent)


def pair_end(value, part):
    row = lax.axis_index("seq") // 2
    return jnp.concatenate([pick(value, row), trade_end(part)], axis=0)


def back_start(value):
    return trade_start(value[value.shape[0] // 2 :].astype(LOW))


def back_starts(others, *values):
    halves = [value[value.shape[0] // 2 :].astype(LOW) for value in values]
    core, size = lax.axis_index("mp"), halves[0].shape[0] // 2
    parts = [lax.dynamic_slice_in_dim(half, core * size, size, 0) for half in halves]
    (ready,) = after([jnp.stack(parts)], others)
    return swap(ready, "seq", 2)


def back_ends(values, part):
    rest = swap(part, "mp", 1)
    core, row = lax.axis_index("mp"), lax.axis_index("seq") // 2
    came = jnp.where(
        core == 0,
        jnp.concatenate([part, rest], axis=1),
        jnp.concatenate([rest, part], axis=1),
    )
    result = []
    for i, value in enumerate(values):
        kept, new = value[: value.shape[0] // 2], came[i].astype(value.dtype)
        result.append(jnp.where(row == 0, jnp.stack([kept, new]), jnp.stack([new, kept])))
    return result


def back_end(value, part):
    kept = value[: value.shape[0] // 2]
    came = trade_end(part).astype(value.dtype)
    row = lax.axis_index("seq") // 2
    return jnp.where(row == 0, jnp.stack([kept, came]), jnp.stack([came, kept]))


def norm_parts(values):
    center = values - jnp.mean(values, axis=-1, keepdims=True)
    scale = lax.rsqrt(jnp.mean(center * center, axis=-1, keepdims=True) + EPS)
    return center * scale, scale


def enter(inputs, parts, norm, weight):
    tokens, width = inputs.shape
    blocks = weight.shape[1] // TILE
    rows = [inputs, *parts] + ([] if norm is None else list(norm))
    keep = len(parts) > 0 and norm is not None

    def body(*refs):
        x_ref, part_refs = refs[0], refs[1 : 1 + len(parts)]
        norm_refs = refs[1 + len(parts) : len(rows)]
        w_ref = refs[len(rows)]
        outs = refs[len(rows) + 1 :]
        low_ref, out_ref = outs[0], outs[1]

        @pl.when(pl.program_id(0) == 0)
        def _():
            x = x_ref[...].astype(F32)
            if part_refs:
                x = x + (part_refs[0][...].astype(F32) + part_refs[1][...].astype(F32))
            if keep:
                outs[2][...] = x
            if norm_refs:
                x = norm_parts(x)[0] * norm_refs[0][...] + norm_refs[1][...]
            low_ref[...] = x.astype(LOW)

        out_ref[0] = dot_nn(low_ref[...], w_ref[...]).astype(LOW)

    result = pl.pallas_call(
        body,
        grid=(blocks,),
        in_specs=[whole(v.shape) for v in rows] + [pl.BlockSpec((width, TILE), lambda j: (0, j))],
        out_specs=[
            whole((tokens, width)),
            pl.BlockSpec((1, tokens, TILE), lambda j: (j, 0, 0)),
        ]
        + ([whole((tokens, width))] if keep else []),
        out_shape=[shaped((tokens, width), LOW), shaped((blocks, tokens, TILE), LOW)]
        + ([shaped((tokens, width), F32)] if keep else []),
        compiler_params=params(32),
        cost_estimate=cost(2 * tokens * width * weight.shape[1], 14 * tokens * width),
    )(*rows, weight)
    return tuple(result)


def attend_body(rows, q_ref, ko_ref, kp_ref, vo_ref, vp_ref, bias_ref, ctx_ref, lse_ref):
    tokens = q_ref.shape[0]
    lane = lax.broadcasted_iota(jnp.int32, (rows, LANES), 1)
    ko, kp, vo, vp = ko_ref[0], kp_ref[0], vo_ref[0], vp_ref[0]
    for r in range(0, tokens, rows):
        q = q_ref[r : r + rows] * jnp.asarray(HEAD**-0.5, LOW)
        ctx = stat = None
        for h in range(LANES // HEAD):
            mine = (lane // HEAD) == h
            qh = jnp.where(mine, q, jnp.zeros_like(q))
            so = dot_nt(qh, ko) + bias_ref[r : r + rows, :tokens]
            sp = dot_nt(qh, kp) + bias_ref[r : r + rows, tokens:]
            top = jnp.maximum(
                jnp.max(so, axis=1, keepdims=True), jnp.max(sp, axis=1, keepdims=True)
            )
            eo, ep = jnp.exp(so - top), jnp.exp(sp - top)
            total = jnp.sum(eo, axis=1, keepdims=True) + jnp.sum(ep, axis=1, keepdims=True)
            acc = dot_nn(eo.astype(LOW), vo) + dot_nn(ep.astype(LOW), vp)
            acc = acc * (1.0 / total)
            lse = jnp.broadcast_to(top + jnp.log(total), (rows, LANES))
            ctx = acc if ctx is None else jnp.where(mine, acc, ctx)
            stat = lse if stat is None else jnp.where(mine, lse, stat)
        ctx_ref[r : r + rows] = ctx.astype(LOW)
        lse_ref[r : r + rows] = stat


def kv_spec(tokens, half):
    return pl.BlockSpec((1, tokens, LANES), lambda i: (half, 0, i))


def attend(query, own, peer, bias):
    tokens, width = query.shape
    spec = pl.BlockSpec((tokens, LANES), lambda i: (0, i))
    return pl.pallas_call(
        functools.partial(attend_body, 256),
        grid=(width // LANES,),
        in_specs=[spec]
        + [kv_spec(tokens, half) for half in (0, 0, 1, 1)]
        + [whole(bias.shape)],
        out_specs=[spec, spec],
        out_shape=[shaped((tokens, width), LOW), shaped((tokens, width), F32)],
        compiler_params=params(40),
        cost_estimate=cost(16 * tokens * tokens * width, 16 * tokens * width, 2 * tokens * tokens * 8),
    )(query, own, peer, own, peer, bias)


def attend_back_body(
    q_ref, ko_ref, kp_ref, vo_ref, vp_ref, g_ref, lse_ref, bias_ref, dq_ref, own_ref, peer_ref, acc
):
    tokens = q_ref.shape[0]
    lane = lax.broadcasted_iota(jnp.int32, (tokens, LANES), 1)
    q = q_ref[...] * jnp.asarray(HEAD**-0.5, LOW)
    g = g_ref[...]
    lse_t = lse_ref[...].T
    parts = ((kp_ref, vp_ref, peer_ref, tokens), (ko_ref, vo_ref, own_ref, 0))
    keys_t = [k_ref[0].T for k_ref, _, _, _ in parts]
    for h in range(LANES // HEAD):
        mine = (lane // HEAD) == h
        qh = jnp.where(mine, q, jnp.zeros_like(q))
        gh = jnp.where(mine, g, jnp.zeros_like(g))
        rows = slice(h * HEAD, (h + 1) * HEAD)
        lse = lse_t[h * HEAD : h * HEAD + 1]
        probs, inner = [], []
        for k_ref, v_ref, _, base in parts:
            scores = dot_nt(k_ref[0], qh) + bias_ref[base : base + tokens]
            probs.append(jnp.exp(scores - lse))
            inner.append(dot_nt(v_ref[0], gh))
        delta = sum(jnp.sum(p * d, axis=0, keepdims=True) for p, d in zip(probs, inner))
        total = None
        for j, (_, _, out_ref, _) in enumerate(parts):
            grads = (probs[j] * (inner[j] - delta)).astype(LOW)
            dv = dot_nn(probs[j].astype(LOW), gh).astype(LOW)
            dk = dot_nn(grads, qh).astype(LOW)
            part = dot_nn(keys_t[j][rows], grads)
            total = part if total is None else total + part
            if h == 0:
                out_ref[0], out_ref[1] = dk, dv
            else:
                out_ref[0] += dk
                out_ref[1] += dv
        acc[rows] = total
    dq_ref[...] = (acc[...].T * HEAD**-0.5).astype(LOW)


def attend_back(query, own, peer, grad, lse, bias_t):
    tokens, width = query.shape
    spec = pl.BlockSpec((tokens, LANES), lambda i: (0, i))
    both = pl.BlockSpec((2, tokens, LANES), lambda i: (0, 0, i))
    return pl.pallas_call(
        attend_back_body,
        grid=(width // LANES,),
        in_specs=[spec]
        + [kv_spec(tokens, half) for half in (0, 0, 1, 1)]
        + [spec, spec, whole(bias_t.shape)],
        out_specs=[spec, both, both],
        out_shape=[shaped((tokens, width), LOW)] + [shaped((2, tokens, width), LOW)] * 2,
        scratch_shapes=[pltpu.VMEM((LANES, tokens), F32)],
        compiler_params=params(40),
        cost_estimate=cost(40 * tokens * tokens * width, 24 * tokens * width, 2 * tokens * tokens * 8),
    )(query, own, peer, own, peer, grad, lse, bias_t)


def attend_leave(dq, own, came, wq, wkv, apart):
    tokens, width = dq.shape[0], wq.shape[0]
    size = tokens // 2

    def body(dq_ref, own_ref, came_ref, wq_ref, wkv_ref, pair_ref, *outs):
        low = [
            (own_ref[j].astype(F32) + came_ref[j].astype(F32)).astype(LOW) for j in range(2)
        ]
        cols = low[0].shape[1]
        for j in range(2):
            pair_ref[:, j * cols : (j + 1) * cols] = low[j]
        first = dot_nt(dq_ref[...], wq_ref[...])
        rest = dot_nt(pair_ref[...], wkv_ref[...])
        if apart:
            outs[0][0] = first.astype(LOW)
            outs[0][1] = rest.astype(LOW)
        else:
            outs[0][...] = (first + rest).astype(LOW)

    part_spec = (
        pl.BlockSpec((2, size, width), lambda i: (0, i, 0))
        if apart
        else pl.BlockSpec((size, width), lambda i: (i, 0))
    )
    cols = own.shape[2]
    return pl.pallas_call(
        body,
        grid=(2,),
        in_specs=[
            pl.BlockSpec((size, cols), lambda i: (i, 0)),
            pl.BlockSpec((2, size, cols), lambda i: (0, i, 0)),
            pl.BlockSpec((2, size, cols), lambda i: (0, i, 0)),
            whole(wq.shape),
            whole(wkv.shape),
        ],
        out_specs=[pl.BlockSpec((size, 2 * cols), lambda i: (i, 0)), part_spec],
        out_shape=[
            shaped((tokens, 2 * cols), LOW),
            shaped((2, tokens, width) if apart else (tokens, width), LOW),
        ],
        compiler_params=params(32),
        cost_estimate=cost(6 * tokens * width * cols, 14 * tokens * cols + 6 * width * cols),
    )(dq, own, came, wq, wkv)


def feed(inputs, parts, norm, up, down):
    tokens, width = inputs.shape
    hidden = up.shape[1]

    def body(x_ref, one_ref, two_ref, gain_ref, bias_ref, up_ref, down_ref, *rest):
        normed_ref, total_ref, act_ref, slope_ref, part_ref, acc = rest
        step = pl.program_id(0)

        @pl.when(step == 0)
        def _():
            x = x_ref[...].astype(F32) + (one_ref[...].astype(F32) + two_ref[...].astype(F32))
            total_ref[...] = x
            normed_ref[...] = (norm_parts(x)[0] * gain_ref[...] + bias_ref[...]).astype(LOW)

        pre = dot_nn(normed_ref[...], up_ref[...])
        below = 0.5 + 0.5 * lax.erf(pre * (0.5**0.5))
        act = (pre * below).astype(LOW)
        act_ref[...] = act
        slope = below + pre * (jnp.exp(pre * pre * -0.5) * 0.3989422804014327)
        slope_ref[...] = slope.astype(LOW)
        part = dot_nt(act, down_ref[...])

        @pl.when(step == 0)
        def _():
            acc[...] = part

        @pl.when(step > 0)
        def _():
            acc[...] += part

        @pl.when(step == pl.num_programs(0) - 1)
        def _():
            part_ref[...] = acc[...].astype(LOW)

    block = pl.BlockSpec((tokens, TILE), lambda j: (0, j))
    weight = pl.BlockSpec((width, TILE), lambda j: (0, j))
    same = whole((tokens, width))
    return pl.pallas_call(
        body,
        grid=(hidden // TILE,),
        in_specs=[same, same, same, whole((1, width)), whole((1, width)), weight, weight],
        out_specs=[same, same, block, block, same],
        out_shape=[
            shaped((tokens, width), LOW),
            shaped((tokens, width), F32),
            shaped((tokens, hidden), LOW),
            shaped((tokens, hidden), LOW),
            shaped((tokens, width), LOW),
        ],
        scratch_shapes=[pltpu.VMEM((tokens, width), F32)],
        compiler_params=params(48),
        cost_estimate=cost(4 * tokens * width * hidden, 8 * width * hidden, 2 * tokens * hidden),
    )(inputs, *parts, *norm, up, down)


def feed_back(low, slope, up, down):
    tokens, width = low.shape
    hidden = up.shape[1]

    def body(low_ref, slope_ref, up_ref, down_ref, pre_ref, part_ref, acc):
        step = pl.program_id(0)
        act_grad = dot_nn(low_ref[...], down_ref[...])
        pre = (act_grad * slope_ref[...].astype(F32)).astype(LOW)
        pre_ref[...] = pre
        part = dot_nt(pre, up_ref[...])

        @pl.when(step == 0)
        def _():
            acc[...] = part

        @pl.when(step > 0)
        def _():
            acc[...] += part

        @pl.when(step == pl.num_programs(0) - 1)
        def _():
            part_ref[...] = acc[...].astype(LOW)

    block = pl.BlockSpec((tokens, TILE), lambda j: (0, j))
    weight = pl.BlockSpec((width, TILE), lambda j: (0, j))
    same = whole((tokens, width))
    return pl.pallas_call(
        body,
        grid=(hidden // TILE,),
        in_specs=[same, block, weight, weight],
        out_specs=[block, same],
        out_shape=[shaped((tokens, hidden), LOW), shaped((tokens, width), LOW)],
        scratch_shapes=[pltpu.VMEM((tokens, width), F32)],
        compiler_params=params(48),
        cost_estimate=cost(4 * tokens * width * hidden, 6 * width * hidden),
    )(low, slope, up, down)


def norm_back(grad, values, parts, gain, weight):
    tokens, width = grad.shape
    size = tokens // 2

    def body(*refs):
        g_ref, x_ref, one_ref, two_ref, gain_ref = refs[:5]
        outs = refs[5:] if weight is None else refs[6:]
        step = pl.program_id(0)
        normed_grad = one_ref[...].astype(F32) + two_ref[...].astype(F32)
        unit, scale = norm_parts(x_ref[...].astype(F32))
        gains = jnp.sum(normed_grad * unit, axis=0, keepdims=True)
        biases = jnp.sum(normed_grad, axis=0, keepdims=True)
        inner = normed_grad * gain_ref[...]
        inner = inner - jnp.mean(inner, axis=-1, keepdims=True) - unit * jnp.mean(
            inner * unit, axis=-1, keepdims=True
        )
        total = g_ref[...] + inner * scale
        outs[0][...] = total

        @pl.when(step == 0)
        def _():
            outs[1][...] = jnp.concatenate([gains, biases], axis=0)

        @pl.when(step > 0)
        def _():
            outs[1][...] += jnp.concatenate([gains, biases], axis=0)

        if weight is not None:
            low = total.astype(LOW)
            outs[2][...] = low
            outs[3][...] = dot_nn(low, refs[5][...]).astype(LOW)

    row = pl.BlockSpec((size, width), lambda i: (i, 0))
    in_specs = [row] * 4 + [whole((1, width))]
    out_specs = [row, whole((2, width))]
    out_shape = [shaped((tokens, width), F32), shaped((2, width), F32)]
    extra = []
    if weight is not None:
        cols = weight.shape[1]
        extra = [weight]
        in_specs.append(whole(weight.shape))
        out_specs += [row, pl.BlockSpec((size, cols), lambda i: (i, 0))]
        out_shape += [shaped((tokens, width), LOW), shaped((tokens, cols), LOW)]
    return pl.pallas_call(
        body,
        grid=(tokens // size,),
        in_specs=in_specs,
        out_specs=out_specs,
        out_shape=out_shape,
        compiler_params=params(40),
        cost_estimate=cost(20 * tokens * width, 20 * tokens * width),
    )(grad, values, *parts, gain, *extra)


def weight_grad_one(left, right, order, extra=None):
    return weight_grad([(left, right)], order, extra)


def weight_grad_two(one, two, order, extra=None):
    return weight_grad([one, two], order, extra)


def attend_leave_apart(dq, own, came, wq, wkv):
    return attend_leave(dq, own, came, wq, wkv, True)


def attend_leave_joined(dq, own, came, wq, wkv):
    return attend_leave(dq, own, came, wq, wkv, False)


def norm_back_last(grad, values, parts, gain):
    return norm_back(grad, values, parts, gain, None)


def low_too(value):
    return value, value.astype(LOW)


def norm_columns(*norm_rows):
    rows = jnp.concatenate(norm_rows, axis=0).astype(LOW)
    return jnp.pad(rows.T, ((0, 0), (0, LANES - rows.shape[0])))


def token_counts(lengths, groups):
    onehot = (groups[:, :, None] == jnp.arange(LANGS, dtype=jnp.int32)).astype(F32)
    counts = jnp.sum(onehot * lengths[:, :, None].astype(F32), axis=(0, 1))
    if lax.axis_size("dp") != 4:
        counts = lax.psum(counts, "dp")
        return counts, counts
    counts = jnp.pad(counts[None], ((0, 7), (0, LANES - LANGS)))
    counts = counts + swap(counts, "dp", 1)
    came = swap(counts, "dp", 2)
    return (counts + came)[0, :LANGS], came


def token_tables(lengths, groups, counts, full_len, quarter):
    here, row = lax.axis_index("seq"), lax.axis_index("seq") // 2
    rows = lengths.shape[0]
    onehot = (groups[:, :, None] == jnp.arange(LANGS, dtype=jnp.int32)).astype(F32)
    all_tokens = rows * lax.axis_size("dp") * full_len
    seg_weight = all_tokens / (LANGS * jnp.sum(onehot * counts, axis=2))
    ends = pick(jnp.cumsum(lengths, axis=1), row)
    steps = jnp.arange(quarter, dtype=jnp.int32)
    places = jnp.concatenate([(here ^ k) * quarter + steps for k in (0, 2, 1, 3)])
    segs = jnp.sum((ends[None, :] <= places[:, None]).astype(jnp.int32), axis=1)
    mine = 2 * quarter
    same = segs[:mine, None] == segs[None, :]
    causal = same & (places[None, :] <= places[:mine, None])
    same_t = segs[:, None] == segs[None, :mine]
    causal_t = same_t & (places[:, None] <= places[None, :mine])
    offsets = [jnp.where(mask, 0.0, -1e30).astype(F32) for mask in (same, same_t, causal, causal_t)]
    match = (segs[:mine, None] == jnp.arange(NSEG, dtype=jnp.int32)).astype(F32)
    tok_weight = jnp.sum(match * pick(seg_weight, row)[None, :], axis=1)
    return offsets, tok_weight, all_tokens


def attn_shard(qkv, out):
    pair = jnp.concatenate([qkv[1], qkv[2]], axis=1)
    side = jnp.concatenate([qkv[0], out.T], axis=1)
    return [pair, side]


def qkv_out(both):
    pair, side = both[0], both[1]
    width = side.shape[1] // 2
    qkv = jnp.stack([side[:, :width], pair[:, :width], pair[:, width:]])
    return qkv, side[:, width:].T


def project(left, right):
    return dot_nn(left, right).astype(LOW)


def project_out(ctx, wo):
    return dot_nt(ctx, wo).astype(LOW)


def other_core(part):
    return swap(part, "mp", 1)


def per_device(
    src,
    tgt,
    cotangent,
    lengths,
    groups,
    enc_gains,
    enc_biases,
    enc_qkv,
    enc_out,
    enc_up,
    enc_down,
    dec_gains,
    dec_biases,
    dec_self_qkv,
    dec_cross_qkv,
    dec_outs,
    dec_up,
    dec_down,
):
    rows, quarter, width = src.shape
    full_len = quarter * lax.axis_size("seq")
    n_enc, n_dec = enc_gains.shape[0], dec_gains.shape[0]
    half, hidden = enc_qkv.shape[2], enc_up.shape[1]
    order = Order()

    norms = jnp.concatenate([enc_gains, enc_biases, dec_gains, dec_biases], axis=0)
    n_norms = norms.shape[0]
    extra = jnp.pad(norms.T, ((0, 0), (0, LANES - n_norms)))
    enc_pair, enc_side = attn_shard(enc_qkv, enc_out)
    shards = [
        [jnp.concatenate([v, extra], axis=1) for v in (enc_pair, enc_side)],
        [
            jnp.concatenate(attn_shard(dec_self_qkv, dec_outs[0]), axis=1),
            jnp.concatenate(attn_shard(dec_cross_qkv, dec_outs[1]), axis=1),
        ],
        [enc_up, enc_down.T],
        [dec_up, dec_down.T],
    ]
    attn_cuts = [(0, 0, 2 * half), (1, 0, half), (1, half, half)]
    both_cuts = [
        (j, first, wide)
        for j in range(2)
        for first, wide in ((0, 2 * half), (2 * half, half), (3 * half, half))
    ]
    feed_cuts = [(0, 0, hidden), (1, 0, hidden)]
    counts, counted = token_counts(lengths, groups)
    one, two = [Gather(shard, True) for shard in shards[:2]]
    one.along()
    two.along([one.came])
    one.join(order)
    one.along()
    one.join(order)
    one.across([counted])
    y_first, x_first = order(lambda: (row_order(2, True), row_order(1, True)))
    two.join(order)
    two.along([one.column])
    three, four = [Gather(shard, False, [two.came]) for shard in shards[2:]]
    one.far(order)
    two.join(order)
    src_part = pair_start(src, [two.column])
    two.across(one.last)
    offsets, tok_weight, all_tokens = order(
        token_tables, lengths, groups, counts, full_len, quarter
    )
    same, same_t, causal, causal_t = offsets
    factor = 1.0 / all_tokens
    *enc_w, table = one.place(order, attn_cuts + [(0, 2 * half, LANES)])
    table = table[:, :n_norms].T.astype(F32)[:, None]
    e_norm = [(table[i], table[n_enc + i]) for i in range(n_enc)]
    d_norm = [(table[2 * n_enc + i], table[2 * n_enc + n_dec + i]) for i in range(n_dec)]
    x_src = order(pair_end, src, src_part)
    enc_in, enc_own = order(enter, x_src, (), e_norm[0], enc_w[0])
    enc_peer = swap(enc_own, "seq", 1)
    enc_q = order(project, enc_in, enc_w[1])
    tgt_part = pair_start(tgt, [enc_q])
    two.far(order)
    three.across(two.last)
    enc_ctx, enc_lse = order(attend, enc_q, enc_own, enc_peer, same)
    enc_part = order(project_out, enc_ctx, enc_w[2])
    enc_other = other_core(enc_part)
    x_tgt = order(pair_end, tgt, tgt_part)
    weights = two.place(order, both_cuts)
    self_w, cross_w = weights[:3], weights[3:]
    self_in, self_own = order(enter, x_tgt, (), d_norm[0], self_w[0])
    self_peer = swap(self_own, "seq", 1)
    self_q = order(project, self_in, self_w[1])
    cot_part = pair_start(cotangent, [self_q])
    three.far(order)
    four.across(three.last)
    order.wait(three.last)
    self_ctx, self_lse = order(attend, self_q, self_own, self_peer, causal)
    self_part = order(project_out, self_ctx, self_w[2])
    self_other = other_core(self_part)
    cot = order(pair_end, cotangent, cot_part)
    out_grad, out_low = order(
        lambda cot, weight: low_too(cot.astype(F32) * weight[:, None]), cot, tok_weight
    )
    e_up, e_down = three.place(order, feed_cuts)
    enc_normed, enc_mid, enc_act, enc_slope, mem_part = order(
        feed, x_src, (enc_part, enc_other), e_norm[1], e_up, e_down
    )
    mem_other = other_core(mem_part)
    four.far(order)
    source, cross_own = order(enter, enc_mid, (mem_part, mem_other), None, cross_w[0])
    cross_peer = swap(cross_own, "seq", 1)
    cross_in, cross_q, dec_mid = order(
        enter, x_tgt, (self_part, self_other), d_norm[1], cross_w[1]
    )
    cross_q = cross_q[0]
    d_up, d_down = four.place(order, feed_cuts)
    cross_ctx, cross_lse = order(attend, cross_q, cross_own, cross_peer, same)
    cross_part = order(project_out, cross_ctx, cross_w[2])
    cross_other = other_core(cross_part)
    dec_normed, dec_cross, dec_act, dec_slope, dec_part = order(
        feed, dec_mid, (cross_part, cross_other), d_norm[2], d_up, d_down
    )
    dec_other = other_core(dec_part)

    pre_grad, part = order(feed_back, out_low, dec_slope, d_up, d_down)
    parts = (part, other_core(part))
    down_g = order(weight_grad_one, out_low, dec_act, x_first)
    up_g = order(weight_grad_one, dec_normed, pre_grad, y_first)
    d_feed = Scatter(up_g, down_g, factor)
    d_feed.begin()
    cross_g, norm_five, low, ctx_grad = order(
        norm_back, out_grad, dec_cross, parts, d_norm[2][0], cross_w[2]
    )
    dq, own_grad, peer_grad = order(
        attend_back, cross_q, cross_own, cross_peer, ctx_grad, cross_lse, same_t
    )
    came = swap(peer_grad, "seq", 1)
    side_g = order(weight_grad_two, (cross_in, dq), (low, cross_ctx), x_first)
    decoded = order(
        lambda total, one, two: (total + (one.astype(F32) + two.astype(F32))).astype(LOW),
        dec_cross,
        dec_part,
        dec_other,
    )
    pair_low, part = order(attend_leave_apart, dq, own_grad, came, cross_w[1], cross_w[0])
    other = other_core(part)
    pair_g = order(weight_grad_one, source, pair_low, y_first)
    cross = Scatter(pair_g, side_g, factor)
    cross.begin(d_feed.came)
    d_feed.add(order)
    memory_grad, memory_low = order(
        lambda one, two: low_too(one[1].astype(F32) + two[1].astype(F32)), part, other
    )
    cross_parts = (part[0], other[0])
    pre_grad, enc_part = order(feed_back, memory_low, enc_slope, e_up, e_down)
    enc_parts = (enc_part, other_core(enc_part))
    down_g = order(weight_grad_one, memory_low, enc_act, x_first)
    d_feed.next(cross.came)
    cross.add(order)
    up_g = order(weight_grad_one, enc_normed, pre_grad, y_first)
    e_feed = Scatter(up_g, down_g, factor)
    e_feed.begin(d_feed.last)
    order.wait(d_feed.last)
    mid_g, norm_four, low, ctx_grad = order(
        norm_back, cross_g, dec_mid, cross_parts, d_norm[1][0], self_w[2]
    )
    dq, own_grad, peer_grad = order(
        attend_back, self_q, self_own, self_peer, ctx_grad, self_lse, causal_t
    )
    came = swap(peer_grad, "seq", 1)
    d_feed.add(order)
    cross.next(e_feed.came)
    enc_mid_g, norm_two, enc_low, enc_ctx_grad = order(
        norm_back, memory_grad, enc_mid, enc_parts, e_norm[1][0], enc_w[2]
    )
    enc_dq, enc_own_grad, enc_peer_grad = order(
        attend_back, enc_q, enc_own, enc_peer, enc_ctx_grad, enc_lse, same_t
    )
    enc_came = swap(enc_peer_grad, "seq", 1)
    e_feed.add(order)
    pair_low, part = order(attend_leave_joined, dq, own_grad, came, self_w[1], self_w[0])
    parts = (part, other_core(part))
    d_feed.add(order)
    side_g = order(weight_grad_two, (self_in, dq), (low, self_ctx), x_first)
    pair_g = order(weight_grad_one, self_in, pair_low, y_first)
    self_s = Scatter(pair_g, side_g, factor)
    e_feed.next(cross.last)
    cross.add(order)
    tgt_grad, norm_three = order(norm_back_last, mid_g, x_tgt, parts, d_norm[0][0])
    pair_low, part = order(
        attend_leave_joined, enc_dq, enc_own_grad, enc_came, enc_w[1], enc_w[0]
    )
    enc_parts = (part, other_core(part))
    d_feed.add(order)
    self_s.begin(e_feed.last)
    e_feed.add(order)
    src_grad, norm_one = order(norm_back_last, enc_mid_g, x_src, enc_parts, e_norm[0][0])
    columns = order(norm_columns, norm_one, norm_two, norm_three, norm_four, norm_five)
    side_g = order(weight_grad_two, (enc_in, enc_dq), (enc_low, enc_ctx), x_first, columns)
    pair_g = order(weight_grad_one, enc_in, pair_low, y_first, columns)
    enc = Scatter(pair_g, side_g, factor)
    cross.add(order)
    enc.begin(self_s.came)
    self_s.add(order)
    e_feed.add(order)
    self_s.next(enc.came)
    enc.add(order)
    enc.next(self_s.last)
    cross.add(order)
    self_s.add(order)
    enc.add(order)
    src_part = back_starts(enc.last if not enc.plain else [], src_grad)
    three_part = back_starts([], decoded, memory_low, tgt_grad)
    self_s.add(order)
    e_feed.add(order)
    enc.add(order)
    decoded, memory_grad, tgt_grad = order(
        back_ends, (decoded, memory_grad, tgt_grad), three_part
    )
    self_s.add(order)
    (src_grad,) = order(back_ends, (src_grad,), src_part)
    enc.add(order)

    norm_out = enc.out[0][:, 2 * half : 2 * half + n_norms].T
    rows_of = [2 * j + i for i in range(2) for j in range(n_enc)]
    rows_of += [2 * (n_enc + j) + i for i in range(2) for j in range(n_dec)]
    norm_out = jnp.stack([norm_out[i] for i in rows_of])
    enc_qkv_g, enc_out_g = qkv_out([part[:, : 2 * half] for part in enc.out])
    self_qkv_g, self_out_g = qkv_out(self_s.out)
    cross_qkv_g, cross_out_g = qkv_out(cross.out)
    return (
        decoded,
        src_grad,
        tgt_grad,
        memory_grad,
        norm_out[:n_enc],
        norm_out[n_enc : 2 * n_enc],
        enc_qkv_g,
        enc_out_g,
        e_feed.out[0],
        e_feed.out[1].T,
        norm_out[2 * n_enc : 2 * n_enc + n_dec],
        norm_out[2 * n_enc + n_dec :],
        self_qkv_g,
        cross_qkv_g,
        jnp.stack([self_out_g, cross_out_g]),
        d_feed.out[0],
        d_feed.out[1].T,
    )


def solution(mesh):
    placed = (
        P("dp", "seq", None),
        P("dp", "seq", None),
        P("dp", "seq", None),
        P("dp", None),
        P("dp", None),
        P(None, ("dp", "seq")),
        P(None, ("dp", "seq")),
        P(None, ("dp", "seq"), "mp"),
        P("mp", ("dp", "seq")),
        P(("dp", "seq"), "mp"),
        P("mp", ("dp", "seq")),
        P(None, ("dp", "seq")),
        P(None, ("dp", "seq")),
        P(None, ("dp", "seq"), "mp"),
        P(None, ("dp", "seq"), "mp"),
        P(None, "mp", ("dp", "seq")),
        P(("dp", "seq"), "mp"),
        P("mp", ("dp", "seq")),
    )
    return jax.shard_map(
        per_device,
        mesh=mesh,
        in_specs=placed,
        out_specs=(
            P("dp", "seq", None),
            P("dp", "seq", None),
            P("dp", "seq", None),
            P("dp", "seq", None),
            P(None, ("dp", "seq")),
            P(None, ("dp", "seq")),
            P(None, ("dp", "seq"), "mp"),
            P("mp", ("dp", "seq")),
            P(("dp", "seq"), "mp"),
            P("mp", ("dp", "seq")),
            P(None, ("dp", "seq")),
            P(None, ("dp", "seq")),
            P(None, ("dp", "seq"), "mp"),
            P(None, ("dp", "seq"), "mp"),
            P(None, "mp", ("dp", "seq")),
            P(("dp", "seq"), "mp"),
            P("mp", ("dp", "seq")),
        ),
        check_vma=False,
    )
```
